128 devices in a mesh: seq: 32 (over z_lo, y, x), chan: 4 (over z_hi, core).
Axes of the slice: x: 4, y: 4, z: 4 (z_hi: 2, z_lo: 2; z = z_hi * 2 + z_lo), core: 2. Of those that a mesh axis runs over, the one named last changes fastest.
Arguments:
- trunk: bfloat16 [4, 8192, 1536], P(None, 'seq', 'chan'), may hold values from -6 to 6
- merged: bfloat16 [4, 768, 16384], P(None, 'chan', 'seq'), may hold values from -40 to 40
- conv_w: bfloat16 [5, 1536, 768], P(None, 'chan'), may hold values from -0.0625 to 0.0625
- norm_gain: float32 [768], P('chan'), may hold values from 0.25 to 1.75
- head_w: bfloat16 [768, 1024], P('chan'), may hold values from -0.21875 to 0.21875
- head_bias: float32 [1024], replicated, may hold values from -4 to 4
- head_scale: float32 [7], replicated, may hold values from 0.5 to 2
- head_of_track: int32 [1024], replicated, may hold values from 0 to 6
- valid_len: int32 [4], replicated, may hold values from 4096 to 16384
- cot: bfloat16 [4, 1024, 16384], P(None, 'seq'), may hold values from -6 to 6
Outputs:
- d_trunk: bfloat16 [4, 8192, 1536], P(None, 'seq', 'chan')
- d_skip: bfloat16 [4, 768, 16384], P(None, 'chan', 'seq')
- d_conv_w: float32 [5, 768, 1536], P(None, 'seq', 'chan')
The draws below stay inside these ranges and needn't reach their ends.
All inputs are finite; a program needn't handle non-finite values.
Results may differ from the reference program's by a relative error of at most 0.0059.
Values may be sent and summed in bfloat16 or wider, within the bound.
No kernel may reach another device: no remote copies, remote signals or barrier semaphores. Data moves between devices by JAX's collectives and lax.ppermute only.
A program may use at most 128 MiB of HBM per device.

```python
import math
import jax
import jax.numpy as jnp
from jax import lax

BATCH = 4
C_IN = 1536
C_OUT = 768
TRACKS = 1024
HEADS = 7
KERNEL = 5
WINDOW = 16384
TRUNK = 8192


def draw_merged(key, part):
    key = jax.random.fold_in(key, 11)
    base_key, row_key, col_key = jax.random.split(key, 3)
    shape = (BATCH, C_OUT, WINDOW)
    base = jax.random.normal(base_key, shape, jnp.float32)
    row_scale = 0.3 * jnp.exp(jax.random.uniform(row_key, (BATCH, 1, WINDOW), jnp.float32, 0.0, math.log(10.0)))
    column = jnp.arange(C_OUT, dtype=jnp.float32) / C_OUT
    col_scale = 0.5 * jnp.exp(column * math.log(3.0)) * jnp.exp(jax.random.uniform(col_key, (C_OUT,), jnp.float32, 0.0, math.log(3.4)))
    values = jnp.clip(base * row_scale * col_scale[:, None], -40.0, 40.0)
    return values.astype(jnp.bfloat16)


def plant(array, rng, low, top_value):
    dims = array.shape
    index_at = [jax.random.randint(jax.random.fold_in(rng, axis), (), 0, dims[axis]) for axis in range(len(dims))]
    array = array.at[tuple(index_at)].set(low)
    longest = dims.index(max(dims))
    index_at[longest] = (index_at[longest] + 1) % dims[longest]
    return array.at[tuple(index_at)].set(top_value)


def shard_levels(key, extent, cuts, least, largest):
    factor_of, own = 1.0, jax.random.fold_in(key, 6)
    for position, shards_of in cuts:
        heights = jnp.exp(jax.random.uniform(jax.random.fold_in(own, position), (shards_of,), jnp.float32, least / len(cuts), largest / len(cuts)))
        factor_of = factor_of * jnp.repeat(heights, extent[position] // shards_of).reshape([-1 if axis == position else 1 for axis in range(len(extent))])
    return factor_of


def noise(rng, extent, spread, limit, shards=(), kind=jnp.bfloat16):
    entries = spread * jax.random.normal(rng, extent, jnp.float32)
    if shards:
        entries = entries * shard_levels(rng, extent, shards, -0.22, 0.18)
    return jnp.clip(entries, -limit, limit).astype(kind)


def setup_inputs(seed: int = 0) -> dict:
    keys = jax.random.split(jax.random.key(seed), 11)
    trunk = noise(keys[0], (BATCH, TRUNK, C_IN), 1.0, 6.0, ((1, 32), (2, 4)))
    merged = draw_merged(jax.random.fold_in(keys[10], 71), 0)
    conv_w = noise(keys[2], (KERNEL, C_IN, C_OUT), (KERNEL * C_IN) ** -0.5, 0.0625, ((1, 4),))
    norm_gain = jnp.clip(1.0 + 0.15 * jax.random.normal(keys[3], (C_OUT,), jnp.float32), 0.25, 1.75)
    head_w = noise(keys[4], (C_OUT, TRACKS), C_OUT ** -0.5, 0.21875, ((0, 4),))
    head_bias = noise(keys[5], (TRACKS,), 1.0, 4.0, (), jnp.float32)
    head_scale = jnp.clip(jnp.exp(jax.random.uniform(keys[6], (HEADS,), jnp.float32, math.log(0.5), math.log(2.0))), 0.5, 2.0)
    head_of_track = plant(jax.random.randint(keys[7], (TRACKS,), 0, HEADS), jax.random.fold_in(keys[7], 1), 0, HEADS - 1).astype(jnp.int32)
    valid_len = plant(jax.random.randint(keys[8], (BATCH,), WINDOW // 4, WINDOW + 1), jax.random.fold_in(keys[8], 1), WINDOW // 4, WINDOW).astype(jnp.int32)
    cot = noise(keys[9], (BATCH, TRACKS, WINDOW), 1.0, 6.0, ((1, 32),))
    return {"trunk": trunk, "merged": merged, "conv_w": conv_w, "norm_gain": norm_gain, "head_w": head_w, "head_bias": head_bias, "head_scale": head_scale, "head_of_track": head_of_track, "valid_len": valid_len, "cot": cot}


epsilon = 1e-06

def reference(trunk, merged, conv_w, norm_gain, head_w, head_bias, head_scale, head_of_track, valid_len, cot):
    batch_count, trunk_len, in_width = trunk.shape
    length = 2 * trunk_len
    out_width = conv_w.shape[2]
    merged32 = merged.astype(jnp.float32)
    gain32 = norm_gain.astype(jnp.float32)[:, None]
    normed = (merged32 * gain32).astype(jnp.bfloat16)
    inv_rms = lax.rsqrt(lax.optimization_barrier(jnp.mean(merged32 * merged32, axis=1, keepdims=True)) + epsilon)
    head32 = head_w.astype(jnp.float32)
    raw_scores = jnp.einsum('bcl,ct->btl', normed.astype(jnp.float32), head32)
    logits = inv_rms * raw_scores + head_bias.astype(jnp.float32)[:, None]
    positions = jnp.arange(length, dtype=jnp.int32)
    live_mask = (positions[None, :] < valid_len[:, None]).astype(jnp.float32)[:, None, :]
    onehot = (head_of_track[:, None] == jnp.arange(head_scale.shape[0], dtype=jnp.int32)[None, :]).astype(jnp.float32)
    track_scale = lax.optimization_barrier(jnp.sum(onehot * head_scale.astype(jnp.float32)[None, :], axis=1))[:, None]
    d_logits = live_mask * cot.astype(jnp.float32) * track_scale * jax.nn.sigmoid(logits)
    d_rms = lax.optimization_barrier(jnp.sum(d_logits * raw_scores, axis=1, keepdims=True))
    scaled = (inv_rms * d_logits).astype(jnp.bfloat16)
    d_normed = jnp.einsum('btl,ct->bcl', scaled.astype(jnp.float32), head32)
    d_merged = d_normed * gain32 - inv_rms ** 3 * d_rms * merged32 / out_width
    d_skip = d_merged.astype(jnp.bfloat16)
    rimmed = jnp.pad(d_skip, ((0, 0), (0, 0), (2, 2)))
    upsampled = jnp.repeat(trunk, 2, axis=1).astype(jnp.float32)
    d_up = jnp.zeros((batch_count, length, in_width), jnp.float32)
    grad_list = []
    for shift_tap in range(KERNEL):
        window = rimmed[:, :, 4 - shift_tap:4 - shift_tap + length].astype(jnp.float32)
        d_up = d_up + jnp.einsum('bol,io->bli', window, conv_w[shift_tap].astype(jnp.float32))
        grad_list.append(jnp.einsum('bli,bol->oi', upsampled, window))
    d_trunk = d_up.reshape(batch_count, trunk_len, 2, in_width).sum(axis=2).astype(jnp.bfloat16)
    d_conv_w = jnp.stack(grad_list) * (1.0 / math.sqrt(batch_count * length))
    return (d_trunk, d_skip, d_conv_w)
```

```python
import math

import jax
import jax.numpy as jnp
from jax import lax
from jax.experimental import pallas as pl
from jax.experimental.pallas import tpu as pltpu
from jax.sharding import PartitionSpec as P

BATCH = 4
C_OUT = 768
TRACKS = 1024
KERNEL = 5
SEQ = 32
CHAN = 4
LANES = 128
epsilon = 1e-06

BF = jnp.bfloat16
F32 = jnp.float32
VMEM_BYTES = 56 * 1024 * 1024


def params():
    return pltpu.CompilerParams(vmem_limit_bytes=VMEM_BYTES)


def dot(a, b, contract):
    return lax.dot_general(a, b, ((contract[:1], contract[1:]), ((), ())), preferred_element_type=F32)


ANY = pl.BlockSpec(memory_space=pl.ANY)
VM = pl.BlockSpec(memory_space=pltpu.VMEM)
SM = pl.BlockSpec(memory_space=pltpu.SMEM)


def prep_kernel(me_ref, cot_ref, merged_ref, head_ref, gain_ref, send_ref, p0, p1, p2, p3, hg_ref, sems):
    me = me_ref[0]
    copies = []
    for r, piece in enumerate((p0, p1, p2, p3)):
        start = pl.multiple_of((me ^ r) * LANES, LANES)
        copies.append(pltpu.make_async_copy(merged_ref.at[:, :, pl.ds(start, LANES)], piece, sems.at[r]))
    for d in range(SEQ):
        start = pl.multiple_of(d * CHAN * LANES + me * LANES, LANES)
        for b in range(BATCH):
            copies.append(
                pltpu.make_async_copy(
                    cot_ref.at[b, :, pl.ds(start, LANES)],
                    send_ref.at[d, pl.ds(b * 32, 32), :],
                    sems.at[4 + d * BATCH + b],
                )
            )
    for copy in copies:
        copy.start()
    hg_ref[...] = (head_ref[...].astype(F32) * gain_ref[...]).astype(BF)
    for copy in copies:
        copy.wait()


def prep(me, cot, merged, head_w, gain):
    piece = jax.ShapeDtypeStruct((BATCH, 192, LANES), BF)
    return pl.pallas_call(
        prep_kernel,
        out_shape=(jax.ShapeDtypeStruct((SEQ, BATCH * 32, LANES), BF), piece, piece, piece, piece,
                   jax.ShapeDtypeStruct(head_w.shape, BF)),
        in_specs=[SM, ANY, ANY, VM, VM],
        out_specs=(ANY, ANY, ANY, ANY, ANY, VM),
        scratch_shapes=[pltpu.SemaphoreType.DMA((4 + SEQ * BATCH,))],
        compiler_params=params(),
        name="prep",
    )(me, cot, merged, head_w, gain)


def rows_of(pieces):
    return jnp.concatenate(
        [jnp.concatenate([p[b] for b in range(BATCH)], axis=1) for p in pieces], axis=0
    )


def score_kernel(p0, p1, p2, p3, h0, h1, h2, h3, raw_ref, inv_ref):
    m = rows_of((p0, p1, p2, p3))
    m32 = m.astype(F32)
    total = jnp.sum(m32 * m32, axis=0, keepdims=True)
    inv_ref[...] = jnp.broadcast_to(lax.rsqrt(total / C_OUT + epsilon), inv_ref.shape)
    hg = jnp.concatenate([h0[...], h1[...], h2[...], h3[...]], axis=0)
    raw_ref[...] = dot(hg, m, (0, 0))


def scores(pieces, heads):
    return pl.pallas_call(
        score_kernel,
        out_shape=(jax.ShapeDtypeStruct((TRACKS, BATCH * LANES), F32),
                   jax.ShapeDtypeStruct((8, BATCH * LANES), F32)),
        in_specs=[VM] * 8,
        out_specs=(VM, VM),
        compiler_params=params(),
        name="scores",
    )(*pieces, *heads)


def head_kernel(ids_ref, valid_ref, raw_ref, inv_ref, cot_ref, cols_ref, p0, p1, p2, p3, h0, h1, h2, h3, out_ref):
    me = ids_ref[0]
    first = ids_ref[1]
    scale = cols_ref[:, 0:1]
    bias = cols_ref[:, 1:2]
    lane = lax.broadcasted_iota(jnp.int32, (1, LANES), 1)
    hg = jnp.concatenate([h0[...], h1[...], h2[...], h3[...]], axis=0)
    scaled, coefs = [], []
    for b in range(BATCH):
        cols = slice(b * LANES, (b + 1) * LANES)
        raw = raw_ref[:, cols]
        inv = inv_ref[0:1, cols]
        live = (first + lane < valid_ref[b]).astype(F32)
        gate = 0.5 * jnp.tanh(0.5 * (inv * raw + bias)) + 0.5
        cot = cot_ref[:, b * 32 : (b + 1) * 32, :].reshape(TRACKS, LANES).astype(F32)
        d_logits = (cot * scale) * gate
        d_rms = live * jnp.sum(d_logits * raw, axis=0, keepdims=True)
        scaled.append(((inv * live) * d_logits).astype(BF))
        coefs.append(inv * inv * inv * d_rms * (1.0 / C_OUT))
    d = dot(hg, jnp.concatenate(scaled, axis=1), (1, 0))
    for r, p in enumerate((p0, p1, p2, p3)):
        rows = pl.ds(pl.multiple_of((me ^ r) * 192, 64), 192)
        for b in range(BATCH):
            block = d[r * 192 : (r + 1) * 192, b * LANES : (b + 1) * LANES]
            out_ref[b, rows, :] = (block - coefs[b] * p[b].astype(F32)).astype(BF)


def head(ids, valid, raw, inv, cot, cols, pieces, heads):
    return pl.pallas_call(
        head_kernel,
        out_shape=jax.ShapeDtypeStruct((BATCH, C_OUT, LANES), BF),
        in_specs=[SM, SM] + [VM] * 12,
        out_specs=VM,
        compiler_params=params(),
        name="head",
    )(ids, valid, raw, inv, cot, cols, *pieces, *heads)


def gather_positions(me, pieces, full, sems):
    copies = []
    for r, piece in enumerate(pieces):
        start = pl.multiple_of((me ^ r) * LANES, LANES)
        copies.append(pltpu.make_async_copy(piece, full.at[:, :, pl.ds(start, LANES)], sems.at[r]))
    for copy in copies:
        copy.start()
    for copy in copies:
        copy.wait()


ROWS = 368


def weight_kernel(ids_ref, d0, d1, d2, d3, tr_ref, trx_ref, out_ref, edge_ref, full, sems):
    me = ids_ref[0]

    @pl.when(pl.program_id(0) == 0)
    def _():
        gather_positions(me, (d0, d1, d2, d3), full, sems)

    step = pl.program_id(0)
    rows = pl.ds(pl.multiple_of(step * 384, 384), 384)
    p = lax.broadcasted_iota(jnp.int32, (256, 256), 0)
    q = lax.broadcasted_iota(jnp.int32, (256, 256), 1)
    even = (q < 128) & (p // 2 == q)
    odd = (q >= 128) & ((p + 1) // 2 == q - 128)
    pick = (even | odd).astype(BF)
    p1 = lax.broadcasted_iota(jnp.int32, (LANES, LANES), 0)
    q1 = lax.broadcasted_iota(jnp.int32, (LANES, LANES), 1)
    evens, odds = [], []
    last = jnp.zeros((384, LANES), F32)
    for b in range(BATCH):
        for h in range(2):
            block = full[b, rows, h * 256 : (h + 1) * 256]
            e = dot(block, pick, (1, 0)).astype(BF)
            evens.append(e[:, :128])
            odds.append(e[:, 128:])
            sel = ((p1 == LANES - 1) & (q1 == b * 2 + h)).astype(BF)
            last = last + dot(block[:, 128:], sel, (1, 0))
    even_all = jnp.concatenate(evens, axis=1)
    odd_all = jnp.concatenate(odds, axis=1)
    g_even = dot(even_all, tr_ref[...], (1, 0))
    g_odd = dot(odd_all, tr_ref[:, :768], (1, 0)) + dot(last.astype(BF), trx_ref[...], (1, 0))
    pad = jnp.zeros((ROWS - 360, LANES), F32)
    taps = (g_even[:, :384], g_odd[:, :384], g_even[:, 384:768], g_odd[:, 384:], g_even[:, 768:])
    for s in range(16):
        blocks = []
        for l in range(3):
            for tap in taps:
                blocks.append(tap[s * 24 : (s + 1) * 24, l * LANES : (l + 1) * LANES])
        out_ref[s] = jnp.concatenate(blocks + [pad], axis=0).astype(BF)
    row = lax.broadcasted_iota(jnp.int32, (32, LANES), 0)
    col = lax.broadcasted_iota(jnp.int32, (32, LANES), 1)
    edge = jnp.zeros((32, 384), F32)
    for b in range(BATCH):
        head_sel = ((row < 16) & (row == b * 2 + col) & (col < 2)).astype(BF)
        tail_sel = ((row >= 16) & (row - 16 == b * 2 + col - 126) & (col >= 126)).astype(BF)
        edge = edge + dot(head_sel, full[b, rows, 0:LANES], (1, 1))
        edge = edge + dot(tail_sel, full[b, rows, 384:512], (1, 1))
    edge_ref[...] = edge.astype(BF)


def weight_grad(ids, pieces, tr, trx):
    return pl.pallas_call(
        weight_kernel,
        grid=(2,),
        out_shape=(jax.ShapeDtypeStruct((SEQ, ROWS, LANES), BF), jax.ShapeDtypeStruct((32, C_OUT), BF)),
        in_specs=[SM] + [ANY] * 4 + [
            pl.BlockSpec((1024, 1152), lambda i: (0, 0)),
            pl.BlockSpec((LANES, 768), lambda i: (0, 0)),
        ],
        out_specs=(pl.BlockSpec((16, ROWS, LANES), lambda i: (i, 0, 0)),
                   pl.BlockSpec((32, 384), lambda i: (0, i))),
        scratch_shapes=[pltpu.VMEM((BATCH, C_OUT, 512), BF), pltpu.SemaphoreType.DMA((4,))],
        compiler_params=params(),
        name="weight_grad",
    )(ids, *pieces, tr, trx)


def trunk_kernel(ids_ref, d0, d1, d2, d3, conv_ref, rim_ref, out_ref, skip_ref, full, sems, skip_sem):
    me = ids_ref[0]
    b = pl.program_id(0)
    skip = pltpu.make_async_copy(
        full.at[:, pl.ds(pl.multiple_of(me * 192, 64), 192), :], skip_ref, skip_sem
    )

    @pl.when(b == 0)
    def _():
        gather_positions(me, (d0, d1, d2, d3), full, sems)
        skip.start()

    j = lax.broadcasted_iota(jnp.int32, (256, 512), 0)
    p = lax.broadcasted_iota(jnp.int32, (256, 512), 1)
    jr = lax.broadcasted_iota(jnp.int32, (256, 32), 0)
    col = lax.broadcasted_iota(jnp.int32, (256, 32), 1)
    rim_pos = jnp.where(col < 16, col - 2 * b - 2, col - 16 - 2 * b + 512)
    rim_ok = ((col >= 2 * b) & (col < 2 * b + 2)) | ((col >= 16 + 2 * b) & (col < 18 + 2 * b))
    d = full[b]
    total = jnp.zeros((256, 384), F32)
    for k in range(KERNEL):
        lo = 2 * j - k + 2
        pick = ((p == lo) | (p == lo + 1)).astype(BF)
        lo_r = 2 * jr - k + 2
        pick_r = (rim_ok & ((rim_pos == lo_r) | (rim_pos == lo_r + 1))).astype(BF)
        window = dot(pick, d, (1, 1)) + dot(pick_r, rim_ref[...], (1, 0))
        total = total + dot(window.astype(BF), conv_ref[k], (1, 1))
    out_ref[0] = total.astype(BF)

    @pl.when(b == BATCH - 1)
    def _():
        skip.wait()


def trunk_grad(ids, pieces, conv_w, rim):
    return pl.pallas_call(
        trunk_kernel,
        grid=(BATCH,),
        out_shape=(jax.ShapeDtypeStruct((BATCH, 256, 384), BF), jax.ShapeDtypeStruct((BATCH, 192, 512), BF)),
        in_specs=[SM] + [ANY] * 4 + [
            pl.BlockSpec((KERNEL, 384, C_OUT), lambda i: (0, 0, 0)),
            pl.BlockSpec((32, C_OUT), lambda i: (0, 0)),
        ],
        out_specs=(pl.BlockSpec((1, 256, 384), lambda i: (i, 0, 0)), ANY),
        scratch_shapes=[pltpu.VMEM((BATCH, C_OUT, 512), BF), pltpu.SemaphoreType.DMA((4,)),
                        pltpu.SemaphoreType.DMA],
        compiler_params=params(),
        cost_estimate=pl.CostEstimate(flops=8 * 10**9, bytes_accessed=16 * 2**20, transcendentals=0),
        name="trunk_grad",
    )(ids, *pieces, conv_w, rim)


def sum_kernel(scale, in_ref, out_ref):
    total = in_ref[0].astype(F32)
    for s in range(1, SEQ):
        total = total + in_ref[s].astype(F32)
    total = total * scale
    for l in range(3):
        for k in range(KERNEL):
            start = l * 120 + k * 24
            out_ref[k, :, l * LANES : (l + 1) * LANES] = total[start : start + 24]


def sum_weights(terms, scale):
    return pl.pallas_call(
        lambda i, o: sum_kernel(scale, i, o),
        out_shape=jax.ShapeDtypeStruct((KERNEL, 24, 384), F32),
        in_specs=[VM],
        out_specs=VM,
        compiler_params=params(),
        name="sum_weights",
    )(terms)


def flip(x, r):
    return lax.ppermute(x, "chan", [(i, i ^ r) for i in range(CHAN)])


def shift(x, step):
    return lax.ppermute(x, "seq", [(i, i + step) for i in range(SEQ) if 0 <= i + step < SEQ])


def across(x):
    pairs = [(s * CHAN + c, (s ^ 16) * CHAN + (c ^ 2)) for s in range(SEQ) for c in range(CHAN)]
    return lax.ppermute(x, ("seq", "chan"), pairs)


def local(
    trunk, merged, conv_w, norm_gain, head_w, head_bias, head_scale, head_of_track, valid_len, cot
):
    me = lax.axis_index("chan").astype(jnp.int32)
    first = lax.axis_index("seq").astype(jnp.int32) * 512 + me * LANES
    ids = jnp.stack([me, first])
    send, p0, p1, p2, p3, hg = prep(ids, cot, merged, head_w, norm_gain[:, None])
    pieces = (p0, flip(p1, 1), flip(p2, 2), flip(p3, 3))
    hg_far = across(hg)
    heads = (hg, flip(hg, 1), hg_far, flip(hg_far, 1))
    got = lax.all_to_all(send, "seq", 0, 0, tiled=True)

    onehot = (
        head_of_track[:, None] == jnp.arange(head_scale.shape[0], dtype=jnp.int32)[None, :]
    ).astype(F32)
    track_scale = jnp.sum(onehot * head_scale[None, :], axis=1)
    cols = jnp.stack([track_scale, head_bias], axis=1)

    before = shift(trunk[:, 255:], 1)
    after = shift(trunk[:, :1], -1)
    tr_m = jnp.concatenate([before, trunk[:, :255]], axis=1)
    tr_p = jnp.concatenate([trunk[:, 1:], after], axis=1)
    tr = jnp.concatenate([tr_m, trunk, tr_p], axis=2).reshape(1024, 1152)
    trx = jnp.concatenate([trunk[:, 127::128], tr_p[:, 127::128]], axis=2).reshape(8, 768)
    trx = jnp.pad(trx, ((0, LANES - 8), (0, 0)))

    raw, inv = scores(pieces, heads)
    d_own = head(ids, valid_len, raw, inv, got, cols, pieces, heads)

    d_far = flip(d_own, 2)
    blocks = (d_own, flip(d_own, 1), d_far, flip(d_far, 1))
    terms, edges = weight_grad(ids, blocks, tr, trx)
    summed = lax.all_to_all(terms, "seq", 0, 0, tiled=True)
    rim = jnp.concatenate([shift(edges[16:], 1), shift(edges[:16], -1)], axis=0)
    d_trunk, d_skip = trunk_grad(ids, blocks, conv_w, rim)
    grad_scale = 1.0 / math.sqrt(BATCH * 512 * SEQ)
    d_conv_w = sum_weights(summed, grad_scale)
    return (d_trunk, d_skip, d_conv_w)


def solution(mesh):
    placed = (
        P(None, "seq", "chan"),
        P(None, "chan", "seq"),
        P(None, "chan", None),
        P("chan"),
        P("chan", None),
        P(),
        P(),
        P(),
        P(),
        P(None, "seq", None),
    )
    return jax.shard_map(
        local,
        mesh=mesh,
        in_specs=placed,
        out_specs=(P(None, "seq", "chan"), P(None, "chan", "seq"), P(None, "seq", "chan")),
        check_vma=False,
    )
```

```python
import math

import jax
import jax.numpy as jnp
from jax import lax
from jax.experimental import pallas as pl
from jax.experimental.pallas import tpu as pltpu
from jax.sharding import PartitionSpec as P

BATCH = 4
C_OUT = 768
TRACKS = 1024
KERNEL = 5
SEQ = 32
CHAN = 4
LANES = 128
epsilon = 1e-06

BF = jnp.bfloat16
F32 = jnp.float32
VMEM_BYTES = 56 * 1024 * 1024


def params():
    return pltpu.CompilerParams(vmem_limit_bytes=VMEM_BYTES)


def dot(a, b, contract):
    return lax.dot_general(a, b, ((contract[:1], contract[1:]), ((), ())), preferred_element_type=F32)


ANY = pl.BlockSpec(memory_space=pl.ANY)
VM = pl.BlockSpec(memory_space=pltpu.VMEM)
SM = pl.BlockSpec(memory_space=pltpu.SMEM)


def pieces_kernel(me_ref, merged_ref, head_ref, gain_ref, p0, p1, p2, p3, payload_ref):
    me = me_ref[0]
    for r, piece in enumerate((p0, p1, p2, p3)):
        start = pl.multiple_of((me ^ r) * LANES, LANES)
        piece[...] = merged_ref[:, :, pl.ds(start, LANES)]
    payload_ref[0:192, :] = head_ref[...]
    payload_ref[192:208, :] = gain_ref[...]


def cut_pieces(me, merged, head_w, gains):
    piece = jax.ShapeDtypeStruct((BATCH, 192, LANES), BF)
    return pl.pallas_call(
        pieces_kernel,
        out_shape=(piece,) * CHAN + (jax.ShapeDtypeStruct((208, TRACKS), BF),),
        in_specs=[SM, VM, VM, VM],
        out_specs=(VM,) * (CHAN + 1),
        compiler_params=params(),
        name="cut_pieces",
    )(me, merged, head_w, gains)


def cot_kernel(me_ref, cot_ref, send_ref, sems):
    copies = []
    for d in range(SEQ):
        start = pl.multiple_of(d * CHAN * LANES + me_ref[0] * LANES, LANES)
        copies.append(
            pltpu.make_async_copy(cot_ref.at[:, :, pl.ds(start, LANES)], send_ref.at[d], sems.at[d])
        )
    for copy in copies:
        copy.start()
    for copy in copies:
        copy.wait()


def cut_cot(me, cot):
    return pl.pallas_call(
        cot_kernel,
        out_shape=jax.ShapeDtypeStruct((SEQ, BATCH, 32, LANES), BF),
        in_specs=[SM, ANY],
        out_specs=VM,
        scratch_shapes=[pltpu.SemaphoreType.DMA((SEQ,))],
        compiler_params=params(),
        cost_estimate=pl.CostEstimate(flops=0, bytes_accessed=5 * 2**20, transcendentals=0),
        name="cut_cot",
    )(me, cot)


def rows_of(pieces):
    return jnp.concatenate(
        [jnp.concatenate([p[b] for b in range(BATCH)], axis=1) for p in pieces], axis=0
    )


def weights_of(heads):
    return jnp.concatenate([h[0:192, :] for h in heads], axis=0)


def gains_of(heads):
    ones = jnp.ones((16, LANES), BF)
    return jnp.concatenate([dot(h[192:208, 0:256], ones, (0, 0))[:192, 0:1] for h in heads], axis=0)


def score_kernel(p0, p1, p2, p3, h0, h1, h2, h3, raw_ref, inv_ref):
    heads = (h0, h1, h2, h3)
    m32 = rows_of((p0, p1, p2, p3)).astype(F32)
    total = jnp.sum(m32 * m32, axis=0, keepdims=True)
    inv_ref[...] = jnp.broadcast_to(lax.rsqrt(total / C_OUT + epsilon), inv_ref.shape)
    normed = (m32 * gains_of(heads)).astype(BF)
    raw_ref[...] = dot(weights_of(heads), normed, (0, 0))


def scores(pieces, heads):
    return pl.pallas_call(
        score_kernel,
        out_shape=(jax.ShapeDtypeStruct((TRACKS, BATCH * LANES), F32),
                   jax.ShapeDtypeStruct((8, BATCH * LANES), F32)),
        in_specs=[VM] * 8,
        out_specs=(VM, VM),
        compiler_params=params(),
        name="scores",
    )(*pieces, *heads)


def head_kernel(
    ids_ref, valid_ref, raw_ref, inv_ref, cot_ref, cols_ref, p0, p1, p2, p3, h0, h1, h2, h3, out_ref, edge_ref
):
    me = ids_ref[0]
    first = ids_ref[1]
    scale = cols_ref[:, 0:1]
    bias = cols_ref[:, 1:2]
    lane = lax.broadcasted_iota(jnp.int32, (1, LANES), 1)
    heads = (h0, h1, h2, h3)
    scaled, coefs = [], []
    for b in range(BATCH):
        cols = slice(b * LANES, (b + 1) * LANES)
        raw = raw_ref[:, cols]
        inv = inv_ref[0:1, cols]
        live = (first + lane < valid_ref[b]).astype(F32)
        gate = 0.5 * jnp.tanh(0.5 * (inv * raw + bias)) + 0.5
        cot = cot_ref[:, b * 32 : (b + 1) * 32, :].reshape(TRACKS, LANES).astype(F32)
        d_logits = (cot * scale) * gate
        d_rms = live * jnp.sum(d_logits * raw, axis=0, keepdims=True)
        scaled.append(((inv * live) * d_logits).astype(BF))
        coefs.append(inv * inv * inv * d_rms * (1.0 / C_OUT))
    d = dot(weights_of(heads), jnp.concatenate(scaled, axis=1), (1, 0)) * gains_of(heads)
    for r, p in enumerate((p0, p1, p2, p3)):
        rows = pl.ds(pl.multiple_of((me ^ r) * 192, 64), 192)
        for b in range(BATCH):
            block = d[r * 192 : (r + 1) * 192, b * LANES : (b + 1) * LANES]
            out_ref[b, rows, :] = (block - coefs[b] * p[b].astype(F32)).astype(BF)
    start = jnp.where(me == CHAN - 1, LANES - 2, 0)
    row = lax.broadcasted_iota(jnp.int32, (16, LANES), 0)
    col = lax.broadcasted_iota(jnp.int32, (16, LANES), 1) - start
    edge = jnp.zeros((16, C_OUT), F32)
    for b in range(BATCH):
        sel = ((col >= 0) & (col < 2) & (row == b * 2 + col)).astype(BF)
        edge = edge + dot(sel, out_ref[b], (1, 1))
    edge_ref[...] = edge.astype(BF)


def head(ids, valid, raw, inv, cot, cols, pieces, heads):
    return pl.pallas_call(
        head_kernel,
        out_shape=(jax.ShapeDtypeStruct((BATCH, C_OUT, LANES), BF), jax.ShapeDtypeStruct((16, C_OUT), BF)),
        in_specs=[SM, SM] + [VM] * 12,
        out_specs=(VM, VM),
        compiler_params=params(),
        name="head",
    )(ids, valid, raw, inv, cot, cols, *pieces, *heads)


def gather_positions(me, pieces, full, sems):
    copies = []
    for r, piece in enumerate(pieces):
        start = pl.multiple_of((me ^ r) * LANES, LANES)
        copies.append(pltpu.make_async_copy(piece, full.at[:, :, pl.ds(start, LANES)], sems.at[r]))
    for copy in copies:
        copy.start()
    for copy in copies:
        copy.wait()


ROWS = 368


def weight_kernel(ids_ref, d0, d1, d2, d3, tr_ref, trx_ref, out_ref, full, sems):
    me = ids_ref[0]

    @pl.when(pl.program_id(0) == 0)
    def _():
        gather_positions(me, (d0, d1, d2, d3), full, sems)

    step = pl.program_id(0)
    rows = pl.ds(pl.multiple_of(step * 384, 384), 384)
    p = lax.broadcasted_iota(jnp.int32, (256, 256), 0)
    q = lax.broadcasted_iota(jnp.int32, (256, 256), 1)
    even = (q < 128) & (p // 2 == q)
    odd = (q >= 128) & ((p + 1) // 2 == q - 128)
    pick = (even | odd).astype(BF)
    p1 = lax.broadcasted_iota(jnp.int32, (LANES, LANES), 0)
    q1 = lax.broadcasted_iota(jnp.int32, (LANES, LANES), 1)
    evens, odds = [], []
    last = jnp.zeros((384, LANES), F32)
    for b in range(BATCH):
        for h in range(2):
            block = full[b, rows, h * 256 : (h + 1) * 256]
            e = dot(block, pick, (1, 0)).astype(BF)
            evens.append(e[:, :128])
            odds.append(e[:, 128:])
            sel = ((p1 == LANES - 1) & (q1 == b * 2 + h)).astype(BF)
            last = last + dot(block[:, 128:], sel, (1, 0))
    even_all = jnp.concatenate(evens, axis=1)
    odd_all = jnp.concatenate(odds, axis=1)
    g_even = dot(even_all, tr_ref[...], (1, 0))
    g_odd = dot(odd_all, tr_ref[:, :768], (1, 0)) + dot(last.astype(BF), trx_ref[...], (1, 0))
    pad = jnp.zeros((ROWS - 360, LANES), F32)
    taps = (g_even[:, :384], g_odd[:, :384], g_even[:, 384:768], g_odd[:, 384:], g_even[:, 768:])
    for s in range(16):
        blocks = []
        for l in range(3):
            for tap in taps:
                blocks.append(tap[s * 24 : (s + 1) * 24, l * LANES : (l + 1) * LANES])
        out_ref[s] = jnp.concatenate(blocks + [pad], axis=0).astype(BF)


def weight_grad(ids, pieces, tr, trx):
    return pl.pallas_call(
        weight_kernel,
        grid=(2,),
        out_shape=jax.ShapeDtypeStruct((SEQ, ROWS, LANES), BF),
        in_specs=[SM] + [ANY] * 4 + [
            pl.BlockSpec((1024, 1152), lambda i: (0, 0)),
            pl.BlockSpec((LANES, 768), lambda i: (0, 0)),
        ],
        out_specs=pl.BlockSpec((16, ROWS, LANES), lambda i: (i, 0, 0)),
        scratch_shapes=[pltpu.VMEM((BATCH, C_OUT, 512), BF), pltpu.SemaphoreType.DMA((4,))],
        compiler_params=params(),
        name="weight_grad",
    )(ids, *pieces, tr, trx)


def trunk_kernel(ids_ref, d0, d1, d2, d3, conv_ref, r0, r1, r2, r3, out_ref, skip_ref, full, sems, skip_sem):
    me = ids_ref[0]
    b = pl.program_id(0)
    skip = pltpu.make_async_copy(
        full.at[:, pl.ds(pl.multiple_of(me * 192, 64), 192), :], skip_ref, skip_sem
    )

    @pl.when(b == 0)
    def _():
        gather_positions(me, (d0, d1, d2, d3), full, sems)
        skip.start()

    j = lax.broadcasted_iota(jnp.int32, (256, 512), 0)
    p = lax.broadcasted_iota(jnp.int32, (256, 512), 1)
    jr = lax.broadcasted_iota(jnp.int32, (256, 64), 0)
    col = lax.broadcasted_iota(jnp.int32, (256, 64), 1)
    offset = col % 16 - 2 * b
    rim_ok = (offset >= 0) & (offset < 2)
    rim_pos = jnp.where(col // 16 == (me ^ 3), offset - 2, jnp.where(col // 16 == me, 512 + offset, -9))
    rim = jnp.concatenate([r0[...], r1[...], r2[...], r3[...]], axis=0)
    d = full[b]
    total = jnp.zeros((256, 384), F32)
    for k in range(KERNEL):
        lo = 2 * j - k + 2
        pick = ((p == lo) | (p == lo + 1)).astype(BF)
        lo_r = 2 * jr - k + 2
        pick_r = (rim_ok & ((rim_pos == lo_r) | (rim_pos == lo_r + 1))).astype(BF)
        window = dot(pick, d, (1, 1)) + dot(pick_r, rim, (1, 0))
        total = total + dot(window.astype(BF), conv_ref[k], (1, 1))
    out_ref[0] = total.astype(BF)

    @pl.when(b == BATCH - 1)
    def _():
        skip.wait()


def trunk_grad(ids, pieces, conv_w, rims):
    return pl.pallas_call(
        trunk_kernel,
        grid=(BATCH,),
        out_shape=(jax.ShapeDtypeStruct((BATCH, 256, 384), BF), jax.ShapeDtypeStruct((BATCH, 192, 512), BF)),
        in_specs=[SM] + [ANY] * 4 + [
            pl.BlockSpec((KERNEL, 384, C_OUT), lambda i: (0, 0, 0)),
        ] + [pl.BlockSpec((16, C_OUT), lambda i: (0, 0))] * CHAN,
        out_specs=(pl.BlockSpec((1, 256, 384), lambda i: (i, 0, 0)), ANY),
        scratch_shapes=[pltpu.VMEM((BATCH, C_OUT, 512), BF), pltpu.SemaphoreType.DMA((4,)),
                        pltpu.SemaphoreType.DMA],
        compiler_params=params(),
        cost_estimate=pl.CostEstimate(flops=8 * 10**9, bytes_accessed=16 * 2**20, transcendentals=0),
        name="trunk_grad",
    )(ids, *pieces, conv_w, *rims)


def sum_kernel(scale, in_ref, out_ref):
    total = in_ref[0].astype(F32)
    for s in range(1, SEQ):
        total = total + in_ref[s].astype(F32)
    total = total * scale
    for l in range(3):
        for k in range(KERNEL):
            start = l * 120 + k * 24
            out_ref[k, :, l * LANES : (l + 1) * LANES] = total[start : start + 24]


def sum_weights(terms, scale):
    return pl.pallas_call(
        lambda i, o: sum_kernel(scale, i, o),
        out_shape=jax.ShapeDtypeStruct((KERNEL, 24, 384), F32),
        in_specs=[VM],
        out_specs=VM,
        compiler_params=params(),
        name="sum_weights",
    )(terms)


def flip(x, r):
    return lax.ppermute(x, "chan", [(i, i ^ r) for i in range(CHAN)])


def shift(x, step):
    return lax.ppermute(x, "seq", [(i, i + step) for i in range(SEQ) if 0 <= i + step < SEQ])


def rim_to(x, r):
    up = [(s * CHAN + 3, (s + 1) * CHAN + (3 ^ r)) for s in range(SEQ - 1)]
    down = [(s * CHAN, (s - 1) * CHAN + r) for s in range(1, SEQ)]
    return lax.ppermute(x, ("seq", "chan"), up + down)


def across(x):
    pairs = [(s * CHAN + c, (s ^ 16) * CHAN + (c ^ 2)) for s in range(SEQ) for c in range(CHAN)]
    return lax.ppermute(x, ("seq", "chan"), pairs)


def local(
    trunk, merged, conv_w, norm_gain, head_w, head_bias, head_scale, head_of_track, valid_len, cot
):
    me = lax.axis_index("chan").astype(jnp.int32)
    first = lax.axis_index("seq").astype(jnp.int32) * 512 + me * LANES
    ids = jnp.stack([me, first])
    hi = lax.reduce_precision(norm_gain, 8, 7)
    mid = lax.reduce_precision(norm_gain - hi, 8, 7)
    gains = jnp.pad(jnp.stack([hi, mid, norm_gain - hi - mid]).astype(BF), ((0, 13), (0, TRACKS - 192)))
    p0, p1, p2, p3, own_head = cut_pieces(ids, merged, head_w, gains)
    p1, p2, p3 = flip(p1, 1), flip(p2, 2), flip(p3, 3)
    far_head = across(own_head)
    send = cut_cot(ids, cot)
    send, p2, p3, far_head = lax.optimization_barrier((send, p2, p3, far_head))
    got = lax.all_to_all(send, "seq", 0, 0, tiled=True).reshape(SEQ, BATCH * 32, LANES)
    pieces = (p0, p1, p2, p3)
    heads = (own_head, flip(own_head, 1), far_head, flip(far_head, 1))

    onehot = (
        head_of_track[:, None] == jnp.arange(head_scale.shape[0], dtype=jnp.int32)[None, :]
    ).astype(F32)
    track_scale = jnp.sum(onehot * head_scale[None, :], axis=1)
    cols = jnp.stack([track_scale, head_bias], axis=1)

    before = shift(trunk[:, 255:], 1)
    after = shift(trunk[:, :1], -1)
    tr_m = jnp.concatenate([before, trunk[:, :255]], axis=1)
    tr_p = jnp.concatenate([trunk[:, 1:], after], axis=1)
    tr = jnp.concatenate([tr_m, trunk, tr_p], axis=2).reshape(1024, 1152)
    trx = jnp.concatenate([trunk[:, 127::128], tr_p[:, 127::128]], axis=2).reshape(8, 768)
    trx = jnp.pad(trx, ((0, LANES - 8), (0, 0)))

    heads, tr, trx, cols = lax.optimization_barrier((heads, tr, trx, cols))
    raw, inv = scores(pieces, heads)
    d_own, edge = head(ids, valid_len, raw, inv, got, cols, pieces, heads)

    rims = [rim_to(edge, r) for r in range(CHAN)]
    d_far, *rims = lax.optimization_barrier((flip(d_own, 2), *rims))
    blocks = (d_own, flip(d_own, 1), d_far, flip(d_far, 1))
    terms = weight_grad(ids, blocks, tr, trx)
    summed = lax.all_to_all(terms, "seq", 0, 0, tiled=True)
    d_trunk, d_skip = trunk_grad(ids, blocks, conv_w, rims)
    grad_scale = 1.0 / math.sqrt(BATCH * 512 * SEQ)
    d_conv_w = sum_weights(summed, grad_scale)
    return (d_trunk, d_skip, d_conv_w)


def solution(mesh):
    placed = (
        P(None, "seq", "chan"),
        P(None, "chan", "seq"),
        P(None, "chan", None),
        P("chan"),
        P("chan", None),
        P(),
        P(),
        P(),
        P(),
        P(None, "seq", None),
    )
    return jax.shard_map(
        local,
        mesh=mesh,
        in_specs=placed,
        out_specs=(P(None, "seq", "chan"), P(None, "chan", "seq"), P(None, "seq", "chan")),
        check_vma=False,
    )
```

```python
import math

import jax
import jax.numpy as jnp
from jax import lax
from jax.experimental import pallas as pl
from jax.experimental.pallas import tpu as pltpu
from jax.sharding import PartitionSpec as P

BATCH = 4
C_OUT = 768
TRACKS = 1024
KERNEL = 5
SEQ = 32
CHAN = 4
LANES = 128
epsilon = 1e-06

BF = jnp.bfloat16
F32 = jnp.float32
VMEM_BYTES = 56 * 1024 * 1024


def params():
    return pltpu.CompilerParams(vmem_limit_bytes=VMEM_BYTES)


def dot(a, b, contract):
    return lax.dot_general(a, b, ((contract[:1], contract[1:]), ((), ())), preferred_element_type=F32)


ANY = pl.BlockSpec(memory_space=pl.ANY)
VM = pl.BlockSpec(memory_space=pltpu.VMEM)
SM = pl.BlockSpec(memory_space=pltpu.SMEM)


PIECE = BATCH * 192 + 16


def pieces_kernel(me_ref, merged_ref, gain_ref, *outs):
    me = me_ref[0]
    tail = jnp.concatenate([gain_ref[:, LANES:], jnp.zeros((1, 2 * LANES - 192), F32)], axis=1)
    rest = jnp.concatenate([gain_ref[:, :LANES], tail], axis=0)
    rows = []
    for _ in range(3):
        part = rest.astype(BF).astype(F32)
        rows.append(part)
        rest = rest - part
    gains = jnp.concatenate(rows + [jnp.zeros((10, LANES), F32)], axis=0).astype(BF)
    for r, piece in enumerate(outs):
        start = pl.multiple_of((me ^ r) * LANES, LANES)
        for b in range(BATCH):
            piece[b * 192 : (b + 1) * 192, :] = merged_ref[b, :, pl.ds(start, LANES)]
        piece[BATCH * 192 :, :] = gains


def cut_pieces(me, merged, gain):
    return pl.pallas_call(
        pieces_kernel,
        out_shape=(jax.ShapeDtypeStruct((PIECE, LANES), BF),) * CHAN,
        in_specs=[SM, VM, VM],
        out_specs=(VM,) * CHAN,
        compiler_params=params(),
        name="cut_pieces",
    )(me, merged, gain)


def cot_kernel(me_ref, cot_ref, send_ref, sems):
    copies = []
    for d in range(SEQ):
        start = pl.multiple_of(d * CHAN * LANES + me_ref[0] * LANES, LANES)
        copies.append(
            pltpu.make_async_copy(cot_ref.at[:, :, pl.ds(start, LANES)], send_ref.at[d], sems.at[d])
        )
    for copy in copies:
        copy.start()
    for copy in copies:
        copy.wait()


def cut_cot(me, cot):
    return pl.pallas_call(
        cot_kernel,
        out_shape=jax.ShapeDtypeStruct((SEQ, BATCH, 32, LANES), BF),
        in_specs=[SM, ANY],
        out_specs=VM,
        scratch_shapes=[pltpu.SemaphoreType.DMA((SEQ,))],
        compiler_params=params(),
        cost_estimate=pl.CostEstimate(flops=0, bytes_accessed=5 * 2**20, transcendentals=0),
        name="cut_cot",
    )(me, cot)


def batch_of(piece, b):
    return piece[b * 192 : (b + 1) * 192, :]


def rows_of(pieces):
    return jnp.concatenate(
        [jnp.concatenate([batch_of(p, b) for b in range(BATCH)], axis=1) for p in pieces], axis=0
    )


def weights_of(heads):
    return jnp.concatenate([h[...] for h in heads], axis=0)


def gains_of(pieces):
    row = lax.broadcasted_iota(jnp.int32, (16, LANES), 0)
    blocks = []
    for p in pieces:
        parts = p[BATCH * 192 :, :]
        for side in range(2):
            pick = ((row < 6) & (row % 2 == side)).astype(BF)
            blocks.append(dot(parts, pick, (0, 0))[: LANES - side * 64, 0:1])
    return jnp.concatenate(blocks, axis=0)


def score_kernel(p0, p1, p2, p3, h0, h1, h2, h3, raw_ref, inv_ref):
    heads = (h0, h1, h2, h3)
    m32 = rows_of((p0, p1, p2, p3)).astype(F32)
    total = jnp.sum(m32 * m32, axis=0, keepdims=True)
    inv_ref[...] = jnp.broadcast_to(lax.rsqrt(total / C_OUT + epsilon), inv_ref.shape)
    normed = (m32 * gains_of((p0, p1, p2, p3))).astype(BF)
    raw_ref[...] = dot(weights_of(heads), normed, (0, 0))


def scores(pieces, heads):
    return pl.pallas_call(
        score_kernel,
        out_shape=(jax.ShapeDtypeStruct((TRACKS, BATCH * LANES), F32),
                   jax.ShapeDtypeStruct((8, BATCH * LANES), F32)),
        in_specs=[VM] * 8,
        out_specs=(VM, VM),
        compiler_params=params(),
        cost_estimate=pl.CostEstimate(flops=2 * 10**9, bytes_accessed=8 * 2**20, transcendentals=0),
        name="scores",
    )(*pieces, *heads)


def head_kernel(
    ids_ref, valid_ref, raw_ref, inv_ref, cot_ref, cols_ref, p0, p1, p2, p3, h0, h1, h2, h3,
    mine_ref, other_ref, edge_ref, full
):
    me = ids_ref[0]
    first = ids_ref[1]
    half = ids_ref[2]
    scale = cols_ref[:, 0:1]
    bias = cols_ref[:, 1:2]
    lane = lax.broadcasted_iota(jnp.int32, (1, LANES), 1)
    heads = (h0, h1, h2, h3)
    scaled, coefs = [], []
    for b in range(BATCH):
        cols = slice(b * LANES, (b + 1) * LANES)
        raw = raw_ref[:, cols]
        inv = inv_ref[0:1, cols]
        live = (first + lane < valid_ref[b]).astype(F32)
        gate = 0.5 * jnp.tanh(0.5 * (inv * raw + bias)) + 0.5
        cot = cot_ref[:, b * 32 : (b + 1) * 32, :].reshape(TRACKS, LANES).astype(F32)
        d_logits = (cot * scale) * gate
        d_rms = live * jnp.sum(d_logits * raw, axis=0, keepdims=True)
        scaled.append(((inv * live) * d_logits).astype(BF))
        coefs.append(inv * inv * inv * d_rms * (1.0 / C_OUT))
    d = dot(weights_of(heads), jnp.concatenate(scaled, axis=1), (1, 0)) * gains_of((p0, p1, p2, p3))
    for r, p in enumerate((p0, p1, p2, p3)):
        for b in range(BATCH):
            block = d[r * 192 : (r + 1) * 192, b * LANES : (b + 1) * LANES]
            full[b, me ^ r] = block - coefs[b] * batch_of(p, b).astype(F32)
    for b in range(BATCH):
        for g in range(CHAN):
            mine_ref[b, g] = full[b, g, pl.ds(pl.multiple_of(96 * half, 32), 96), :].astype(BF)
            other_ref[b, g] = full[b, g, pl.ds(pl.multiple_of(96 * (1 - half), 32), 96), :].astype(BF)
    start = jnp.where(me == CHAN - 1, LANES - 2, 0)
    row = lax.broadcasted_iota(jnp.int32, (16, LANES), 0)
    col = lax.broadcasted_iota(jnp.int32, (16, LANES), 1) - start
    edge = jnp.zeros((16, C_OUT), F32)
    for b in range(BATCH):
        sel = ((col >= 0) & (col < 2) & (row == b * 2 + col)).astype(BF)
        edge = edge + dot(sel, full[b].reshape(C_OUT, LANES).astype(BF), (1, 1))
    edge_ref[...] = edge.astype(BF)


def head(ids, valid, raw, inv, cot, cols, pieces, heads):
    return pl.pallas_call(
        head_kernel,
        out_shape=(jax.ShapeDtypeStruct((BATCH, CHAN, 96, LANES), BF),) * 2
        + (jax.ShapeDtypeStruct((16, C_OUT), BF),),
        in_specs=[SM, SM] + [VM] * 12,
        out_specs=(VM,) * 3,
        scratch_shapes=[pltpu.VMEM((BATCH, CHAN, 192, LANES), F32)],
        compiler_params=params(),
        name="head",
    )(ids, valid, raw, inv, cot, cols, *pieces, *heads)


PAIR = 2


def rows_kernel(own_ref, far_ref, tr_ref, trx_ref):
    row = lax.broadcasted_iota(jnp.int32, (256, 384), 0)
    ends = [jnp.zeros((LANES, 384), F32) for _ in range(KERNEL)]
    at = lax.broadcasted_iota(jnp.int32, (LANES, 384), 0)
    for q, ref in enumerate((own_ref, far_ref)):
        for b in range(BATCH):
            t = ref[b].astype(F32)
            rows = slice(b * 256, (b + 1) * 256)
            tr_ref[q, rows, 0:384] = jnp.where(row == 0, 0.0, pltpu.roll(t, 1, 0)).astype(BF)
            tr_ref[q, rows, 384:768] = ref[b]
            tr_ref[q, rows, 768:1152] = jnp.where(row == 255, 0.0, pltpu.roll(t, 255, 0)).astype(BF)
            base = (q * BATCH + b) * 5
            for place, tap, j in ((0, 1, 127), (0, 3, 128), (1, 1, 255), (2, 0, 255), (3, 3, 0), (4, 4, 0)):
                ends[tap] = jnp.where(at == base + place, t[j : j + 1], ends[tap])
    for k in range(KERNEL):
        trx_ref[:, k * 384 : (k + 1) * 384] = ends[k].astype(BF)


def trunk_rows(own, far):
    return pl.pallas_call(
        rows_kernel,
        out_shape=(jax.ShapeDtypeStruct((PAIR, 1024, 1152), BF),
                   jax.ShapeDtypeStruct((LANES, KERNEL * 384), BF)),
        in_specs=[VM, VM],
        out_specs=(VM, VM),
        compiler_params=params(),
        cost_estimate=pl.CostEstimate(flops=10**7, bytes_accessed=8 * 2**20, transcendentals=0),
        name="trunk_rows",
    )(own, far)


ROWS = 368


def weight_kernel(ids_ref, *refs):
    pieces, (tr_ref, trx_ref, rim0, rim1, out_ref, full, tr, ends, sems, tr_sems) = refs[:8], refs[8:]
    me = ids_ref[0]
    half = ids_ref[2]
    copies = []
    for q in range(PAIR):
        for r in range(CHAN):
            lanes = pl.ds(pl.multiple_of((me ^ r) * LANES, LANES), LANES)
            copies.append(
                pltpu.make_async_copy(pieces[q * CHAN + r], full.at[q, :, :, :, lanes], sems.at[q, r])
            )
    loads = [pltpu.make_async_copy(tr_ref.at[q], tr.at[q], tr_sems.at[q]) for q in range(PAIR)]
    for copy in copies + loads:
        copy.start()
    p = lax.broadcasted_iota(jnp.int32, (256, 256), 0)
    q_ = lax.broadcasted_iota(jnp.int32, (256, 256), 1)
    even = (q_ < 128) & (p // 2 == q_)
    odd = (q_ >= 128) & ((p + 1) // 2 == q_ - 128)
    pick = (even | odd).astype(BF)
    row = lax.broadcasted_iota(jnp.int32, (64, LANES), 0)
    col = lax.broadcasted_iota(jnp.int32, (64, LANES), 1)
    batch, tap = (row % 16) // 2, row % 2
    before, after = row // 16 == (me ^ 3), row // 16 == me
    edge = jnp.zeros((C_OUT, LANES), F32)
    for q, rim in enumerate((rim0, rim1)):
        place = col - (q * BATCH + batch) * 5
        picks = (
            (before & (place == 4)) | (before & (place == 3) & (tap == 1))
            | (after & (place == 2)) | (after & (place == 1) & (tap == 0))
        )
        picks = (picks & (row % 16 < 8)).astype(BF)
        edge = edge + dot(rim[...], picks, (0, 0))
    ends[...] = edge
    last = jnp.concatenate(
        [ends[pl.ds(pl.multiple_of(192 * g + 96 * half, 32), 96), :] for g in range(CHAN)], axis=0
    )
    p1 = lax.broadcasted_iota(jnp.int32, (LANES, LANES), 0)
    q1 = lax.broadcasted_iota(jnp.int32, (LANES, LANES), 1)
    g_even = jnp.zeros((384, 1152), F32)
    g_odd = jnp.zeros((384, 768), F32)
    for q in range(PAIR):
        for copy in copies[q * CHAN : (q + 1) * CHAN]:
            copy.wait()
        evens, odds = [], []
        for b in range(BATCH):
            for h in range(2):
                block = full[q, b, :, :, h * 256 : (h + 1) * 256].reshape(384, 256)
                e = dot(block, pick, (1, 0)).astype(BF)
                evens.append(e[:, :128])
                odds.append(e[:, 128:])
                sel = ((p1 == LANES - 1) & (q1 == (q * BATCH + b) * 5 + h)).astype(BF)
                last = last + dot(block[:, 128:], sel, (1, 0))
        loads[q].wait()
        g_even = g_even + dot(jnp.concatenate(evens, axis=1), tr[q], (1, 0))
        g_odd = g_odd + dot(jnp.concatenate(odds, axis=1), tr[q, :, :768], (1, 0))
    last = last.astype(BF)
    side = [dot(last, trx_ref[:, k * 384 : (k + 1) * 384], (1, 0)) for k in range(KERNEL)]
    pad = jnp.zeros((ROWS - 360, LANES), F32)
    taps = (g_even[:, :384], g_odd[:, :384], g_even[:, 384:768], g_odd[:, 384:], g_even[:, 768:])
    taps = [tap + term for tap, term in zip(taps, side)]
    for s in range(16):
        blocks = []
        for l in range(3):
            for tap in taps:
                blocks.append(tap[s * 24 : (s + 1) * 24, l * LANES : (l + 1) * LANES])
        out_ref[s] = jnp.concatenate(blocks + [pad], axis=0).astype(BF)


def weight_grad(ids, pieces, tr, trx, rims, rims_far):
    return pl.pallas_call(
        weight_kernel,
        out_shape=jax.ShapeDtypeStruct((16, ROWS, LANES), BF),
        in_specs=[SM] + [ANY] * 9 + [VM] * 3,
        out_specs=VM,
        scratch_shapes=[
            pltpu.VMEM((PAIR, BATCH, CHAN, 96, 512), BF),
            pltpu.VMEM((PAIR, 1024, 1152), BF),
            pltpu.VMEM((C_OUT, LANES), F32),
            pltpu.SemaphoreType.DMA((PAIR, CHAN)),
            pltpu.SemaphoreType.DMA((PAIR,)),
        ],
        compiler_params=params(),
        cost_estimate=pl.CostEstimate(flops=4 * 10**9, bytes_accessed=10 * 2**20, transcendentals=0),
        name="weight_grad",
    )(ids, *pieces, tr, trx, rims, rims_far)


def trunk_kernel(ids_ref, *refs):
    mine, other = refs[:4], refs[4:8]
    conv_ref, rim_ref, out_ref, skip_ref, full, sums, sems, skip_sem = refs[8:]
    me = ids_ref[0]
    half = ids_ref[2]
    skip = pltpu.make_async_copy(full.at[:, me], skip_ref, skip_sem)
    copies = []
    for r in range(CHAN):
        lanes = pl.ds(pl.multiple_of((me ^ r) * LANES, LANES), LANES)
        copies.append(pltpu.make_async_copy(mine[r], full.at[:, :, half, :, lanes], sems.at[0, r]))
        copies.append(pltpu.make_async_copy(other[r], full.at[:, :, 1 - half, :, lanes], sems.at[1, r]))
    for copy in copies:
        copy.start()
    row = lax.broadcasted_iota(jnp.int32, (2 * EXT, 512), 0)
    p = lax.broadcasted_iota(jnp.int32, (2 * EXT, 512), 1)
    lo = jnp.where(row < EXT, 2 * (row - 8), 2 * (row - EXT - 8) - 1)
    pick = ((p == lo) | (p == lo + 1)).astype(BF)
    col = lax.broadcasted_iota(jnp.int32, (2 * EXT, 64), 1)
    lo = lo[:, :64]
    rim = rim_ref[...]
    for copy in copies:
        copy.wait()
    skip.start()
    for b in range(BATCH):
        offset = col % 16 - 2 * b
        rim_ok = (offset >= 0) & (offset < 2)
        rim_pos = jnp.where(col // 16 == (me ^ 3), offset - 2, jnp.where(col // 16 == me, 512 + offset, -99))
        pick_r = (rim_ok & ((rim_pos == lo) | (rim_pos == lo + 1))).astype(BF)
        e = (dot(pick, full[b].reshape(C_OUT, 512), (1, 1)) + dot(pick_r, rim, (1, 0))).astype(BF)
        sums[pl.ds(b * EXT, EXT), :C_OUT] = e[:EXT]
        sums[pl.ds(b * EXT, EXT), C_OUT:] = e[EXT:]
    even, odd = sums[:, :C_OUT], sums[:, C_OUT:]
    up = dot(even, conv_ref[0], (1, 1)) + dot(odd, conv_ref[1], (1, 1))
    here = dot(even, conv_ref[2], (1, 1)) + dot(odd, conv_ref[3], (1, 1))
    down = dot(even, conv_ref[4], (1, 1))
    for b in range(BATCH):
        o = b * EXT + 8
        total = up[o + 1 : o + 257] + here[o : o + 256] + down[o - 1 : o + 255]
        out_ref[b] = total.astype(BF)
    skip.wait()


EXT = 272


def trunk_grad(ids, mine, other, conv_w, rims):
    return pl.pallas_call(
        trunk_kernel,
        out_shape=(jax.ShapeDtypeStruct((BATCH, 256, 384), BF), jax.ShapeDtypeStruct((BATCH, 2, 96, 512), BF)),
        in_specs=[SM] + [ANY] * 8 + [VM] * 2,
        out_specs=(VM, ANY),
        scratch_shapes=[pltpu.VMEM((BATCH, CHAN, 2, 96, 512), BF), pltpu.VMEM((BATCH * EXT, 2 * C_OUT), BF),
                        pltpu.SemaphoreType.DMA((2, CHAN)), pltpu.SemaphoreType.DMA],
        compiler_params=params(),
        cost_estimate=pl.CostEstimate(flops=8 * 10**9, bytes_accessed=16 * 2**20, transcendentals=0),
        name="trunk_grad",
    )(ids, *mine, *other, conv_w, rims)


def sum_kernel(scale, in_ref, out_ref):
    total = in_ref[0].astype(F32)
    for s in range(1, in_ref.shape[0]):
        total = total + in_ref[s].astype(F32)
    total = total * scale
    for l in range(3):
        for k in range(KERNEL):
            start = l * 120 + k * 24
            out_ref[k, :, l * LANES : (l + 1) * LANES] = total[start : start + 24]


def sum_weights(terms, scale):
    return pl.pallas_call(
        lambda i, o: sum_kernel(scale, i, o),
        out_shape=jax.ShapeDtypeStruct((KERNEL, 24, 384), F32),
        in_specs=[VM],
        out_specs=VM,
        compiler_params=params(),
        name="sum_weights",
    )(terms)


def flip(x, r):
    return lax.ppermute(x, "chan", [(i, i ^ r) for i in range(CHAN)])


def shift(x, step):
    return lax.ppermute(x, "seq", [(i, i + step) for i in range(SEQ) if 0 <= i + step < SEQ])


def partner(x):
    return lax.ppermute(x, "seq", [(i, i ^ 4) for i in range(SEQ)])


def partner_far(x):
    pairs = [(s * CHAN + c, (s ^ 4) * CHAN + (c ^ 2)) for s in range(SEQ) for c in range(CHAN)]
    return lax.ppermute(x, ("seq", "chan"), pairs)


def rim_to(x, r):
    up = [(s * CHAN + 3, (s + 1) * CHAN + (3 ^ r)) for s in range(SEQ - 1)]
    down = [(s * CHAN, (s - 1) * CHAN + r) for s in range(1, SEQ)]
    return lax.ppermute(x, ("seq", "chan"), up + down)


def across(x):
    pairs = [(s * CHAN + c, (s ^ 16) * CHAN + (c ^ 2)) for s in range(SEQ) for c in range(CHAN)]
    return lax.ppermute(x, ("seq", "chan"), pairs)


def local(
    trunk, merged, conv_w, norm_gain, head_w, head_bias, head_scale, head_of_track, valid_len, cot
):
    me = lax.axis_index("chan").astype(jnp.int32)
    place = lax.axis_index("seq").astype(jnp.int32)
    half = (place // 4) % 2
    ids = jnp.stack([me, place * 512 + me * LANES, half])
    far_head = across(head_w)
    trunk_far = partner(trunk)
    p0, p1, p2, p3 = cut_pieces(ids, merged, norm_gain[None])
    p1, p2, p3 = flip(p1, 1), flip(p2, 2), flip(p3, 3)
    send = cut_cot(ids, cot)
    send, p1, p2, p3, far_head, trunk_far = lax.optimization_barrier((send, p1, p2, p3, far_head, trunk_far))
    got = lax.all_to_all(send, "seq", 0, 0, tiled=True).reshape(SEQ, BATCH * 32, LANES)
    heads = (head_w, flip(head_w, 1), far_head, flip(far_head, 1))
    pieces = (p0, p1, p2, p3)

    onehot = (
        head_of_track[:, None] == jnp.arange(head_scale.shape[0], dtype=jnp.int32)[None, :]
    ).astype(F32)
    track_scale = jnp.sum(onehot * head_scale[None, :], axis=1)
    cols = jnp.stack([track_scale, head_bias], axis=1)

    tr, trx = trunk_rows(trunk, trunk_far)
    heads, tr, trx, cols = lax.optimization_barrier((heads, tr, trx, cols))
    raw, inv = scores(pieces, heads)
    mine, other, edge = head(ids, valid_len, raw, inv, got, cols, pieces, heads)

    rims = [rim_to(edge, r) for r in range(CHAN)]
    mine_far, other_x, other_far_x = flip(mine, 2), partner(other), partner_far(other)
    mine_far, other_x, other_far_x, *rims = lax.optimization_barrier((mine_far, other_x, other_far_x, *rims))
    rims = jnp.concatenate(rims)
    mine_all = (mine, flip(mine, 1), mine_far, flip(mine_far, 1))
    blocks = mine_all + (other_x, flip(other_x, 1), other_far_x, flip(other_far_x, 1))
    terms = weight_grad(ids, blocks, tr, trx, rims, partner(rims))
    other_late, _ = lax.optimization_barrier((other, mine_far))
    other_far = flip(other_late, 2)
    other_all = (other, flip(other, 1), other_far, flip(other_far, 1))
    groups = [[s for s in range(SEQ) if (s // 4) % 2 == u] for u in range(2)]
    summed = lax.all_to_all(terms, "seq", 0, 0, tiled=True, axis_index_groups=groups)
    d_trunk, d_skip = trunk_grad(ids, mine_all, other_all, conv_w, rims)
    grad_scale = 1.0 / math.sqrt(BATCH * 512 * SEQ)
    d_conv_w = sum_weights(summed, grad_scale)
    return (d_trunk, d_skip.reshape(BATCH, 192, 512), d_conv_w)


def solution(mesh):
    placed = (
        P(None, "seq", "chan"),
        P(None, "chan", "seq"),
        P(None, "chan", None),
        P("chan"),
        P("chan", None),
        P(),
        P(),
        P(),
        P(),
        P(None, "seq", None),
    )
    return jax.shard_map(
        local,
        mesh=mesh,
        in_specs=placed,
        out_specs=(P(None, "seq", "chan"), P(None, "chan", "seq"), P(None, "seq", "chan")),
        check_vma=False,
    )
```

```python
import math

import jax
import jax.numpy as jnp
from jax import lax
from jax.experimental import pallas as pl
from jax.experimental.pallas import tpu as pltpu
from jax.sharding import PartitionSpec as P

BATCH = 4
C_OUT = 768
TRACKS = 1024
KERNEL = 5
SEQ = 32
CHAN = 4
LANES = 128
epsilon = 1e-06

BF = jnp.bfloat16
F32 = jnp.float32
MIB = 1024 * 1024


def params(limit=62 * MIB):
    return pltpu.CompilerParams(vmem_limit_bytes=limit)


def dot(a, b, contract):
    return lax.dot_general(a, b, ((contract[:1], contract[1:]), ((), ())), preferred_element_type=F32)


ANY = pl.BlockSpec(memory_space=pl.ANY)
VM = pl.BlockSpec(memory_space=pltpu.VMEM)
HBM = pl.BlockSpec(memory_space=pltpu.HBM)
SM = pl.BlockSpec(memory_space=pltpu.SMEM)


PIECE = BATCH * 192 + 16


def pieces_kernel(ids_ref, merged_ref, gain_ref, p0, p1, p2, p3, line, sems, line_sem):
    me = ids_ref[0]
    load = pltpu.make_async_copy(gain_ref, line, line_sem)
    load.start()
    copies = []
    for r, piece in enumerate((p0, p1, p2, p3)):
        lanes = pl.ds(pl.multiple_of((me ^ r) * LANES, LANES), LANES)
        for b in range(BATCH):
            rows = pl.ds(b * 192, 192)
            copies.append(pltpu.make_async_copy(merged_ref.at[b, :, lanes], piece.at[rows, :], sems.at[r, b]))
    for copy in copies:
        copy.start()
    load.wait()
    tail = jnp.concatenate([line[:, LANES:], jnp.zeros((1, 2 * LANES - 192), F32)], axis=1)
    rest = jnp.concatenate([line[:, :LANES], tail], axis=0)
    rows = []
    for _ in range(3):
        part = rest.astype(BF).astype(F32)
        rows.append(part)
        rest = rest - part
    gains = jnp.concatenate(rows + [jnp.zeros((10, LANES), F32)], axis=0).astype(BF)
    for piece in (p0, p1, p2, p3):
        piece[BATCH * 192 :, :] = gains
    for copy in copies:
        copy.wait()


def cut_pieces(ids, merged, gain):
    return pl.pallas_call(
        pieces_kernel,
        out_shape=(jax.ShapeDtypeStruct((PIECE, LANES), BF),) * CHAN,
        in_specs=[SM, HBM, HBM],
        out_specs=(VM,) * CHAN,
        scratch_shapes=[pltpu.VMEM((1, 192), F32), pltpu.SemaphoreType.DMA((CHAN, BATCH)), pltpu.SemaphoreType.DMA],
        compiler_params=params(),
        name="cut_pieces",
    )(ids, merged, gain)


COT_ROWS = 9 * 16


def cot_kernel(ids_ref, cot_ref, trunk_ref, send_ref, edges, sems, edge_sems):
    me, place = ids_ref[0], ids_ref[3]
    copies = []
    for d in range(SEQ):
        start = pl.multiple_of(d * CHAN * LANES + me * LANES, LANES)
        copies.append(
            pltpu.make_async_copy(cot_ref.at[:, :, pl.ds(start, LANES)], send_ref.at[d, pl.ds(0, 8)], sems.at[d])
        )
    loads = [
        pltpu.make_async_copy(trunk_ref.at[:, pl.ds(row, 16), :], edges.at[i], edge_sems.at[i])
        for i, row in enumerate((0, 240))
    ]
    for copy in loads + copies:
        copy.start()
    for load in loads:
        load.wait()
    rows = []
    for i, row in enumerate((0, 15)):
        parts = []
        for b in range(BATCH):
            line = edges[i, b].astype(F32)[row : row + 1]
            parts += [line[:, l * LANES : (l + 1) * LANES] for l in range(3)]
        rows.append(jnp.concatenate(parts + [jnp.zeros((4, LANES), F32)], axis=0))
    for d in range(SEQ):
        up = ((place + 1 == d) | (place + 1 == (d ^ 4))).astype(F32)
        down = ((place - 1 == d) | (place - 1 == (d ^ 4))).astype(F32)
        send_ref[d, 8] = (rows[1] * up + rows[0] * down).astype(BF)
    for copy in copies:
        copy.wait()


def cut_cot(ids, cot, trunk):
    return pl.pallas_call(
        cot_kernel,
        out_shape=jax.ShapeDtypeStruct((SEQ, 9, 16, LANES), BF),
        in_specs=[SM, HBM, HBM],
        out_specs=VM,
        scratch_shapes=[pltpu.VMEM((2, BATCH, 16, 384), BF), pltpu.SemaphoreType.DMA((SEQ,)),
                        pltpu.SemaphoreType.DMA((2,))],
        compiler_params=params(),
        cost_estimate=pl.CostEstimate(flops=0, bytes_accessed=5 * 2**20, transcendentals=0),
        name="cut_cot",
    )(ids, cot.reshape(BATCH * 2, 16, -1), trunk)


def score_kernel(*refs):
    pieces, heads, (bias_ref, of_track_ref, scale_ref) = refs[:4], refs[4:8], refs[8:11]
    raw_ref, inv_ref, weights_ref, merged_ref, gain_ref, cols_ref, parts, sems, head_sems, part_sems = refs[11:]
    copies = []
    for r in range(CHAN):
        rows = pl.ds(r * 192, 192)
        for b in range(BATCH):
            copies.append(
                pltpu.make_async_copy(
                    pieces[r].at[pl.ds(b * 192, 192), :],
                    merged_ref.at[rows, pl.ds(b * LANES, LANES)],
                    sems.at[r, b],
                )
            )
        copies.append(
            pltpu.make_async_copy(pieces[r].at[pl.ds(BATCH * 192, 16), :], parts.at[r], part_sems.at[r])
        )
    loads = [
        pltpu.make_async_copy(heads[r], weights_ref.at[pl.ds(r * 192, 192), :], head_sems.at[r])
        for r in range(CHAN)
    ]
    for copy in copies + loads:
        copy.start()
    track_scale = jnp.zeros((1, TRACKS), F32)
    for h in range(scale_ref.shape[0]):
        track_scale = jnp.where(of_track_ref[...] == h, scale_ref[h], track_scale)
    lines = []
    for rest in (bias_ref[...], track_scale):
        for _ in range(3):
            part = rest.astype(BF).astype(F32)
            lines.append(part)
            rest = rest - part
    lines = jnp.concatenate(lines + [jnp.zeros((10, TRACKS), F32)], axis=0).astype(BF)
    row = lax.broadcasted_iota(jnp.int32, (16, LANES), 0)
    lane = lax.broadcasted_iota(jnp.int32, (16, LANES), 1)
    cols_ref[...] = dot(lines, ((row < 6) & (row // 3 == lane)).astype(BF), (0, 0))
    for copy in copies:
        copy.wait()
    for r in range(CHAN):
        for side in range(2):
            pick = ((row < 6) & (row % 2 == side)).astype(BF)
            size = LANES - side * 64
            start = r * 192 + side * LANES
            gain_ref[start : start + size, :] = dot(parts[r], pick, (0, 0))[:size]
    m32 = merged_ref[...].astype(F32)
    total = jnp.sum(m32 * m32, axis=0, keepdims=True)
    inv_ref[...] = jnp.broadcast_to(lax.rsqrt(total / C_OUT + epsilon), inv_ref.shape)
    normed = (m32 * gain_ref[:, 0:1]).astype(BF)
    for load in loads:
        load.wait()
    raw_ref[...] = dot(weights_ref[...], normed, (0, 0))


def scores(pieces, heads, bias, of_track, scale):
    return pl.pallas_call(
        score_kernel,
        out_shape=(jax.ShapeDtypeStruct((TRACKS, BATCH * LANES), F32),
                   jax.ShapeDtypeStruct((8, BATCH * LANES), F32),
                   jax.ShapeDtypeStruct((C_OUT, TRACKS), BF),
                   jax.ShapeDtypeStruct((C_OUT, BATCH * LANES), BF),
                   jax.ShapeDtypeStruct((C_OUT, LANES), F32),
                   jax.ShapeDtypeStruct((TRACKS, LANES), F32)),
        in_specs=[HBM] * 8 + [VM, VM, SM],
        out_specs=(VM,) * 6,
        scratch_shapes=[pltpu.VMEM((CHAN, 16, LANES), BF), pltpu.SemaphoreType.DMA((CHAN, BATCH)),
                        pltpu.SemaphoreType.DMA((CHAN,)), pltpu.SemaphoreType.DMA((CHAN,))],
        compiler_params=params(),
        cost_estimate=pl.CostEstimate(flops=45 * 10**8, bytes_accessed=8 * 2**20, transcendentals=0),
        name="scores",
    )(*pieces, *heads, bias, of_track, scale)


def head_kernel(
    ids_ref, valid_ref, raw_hbm, inv_ref, weights_hbm, merged_hbm, gain_ref, cols_ref, cot_ref,
    mine_ref, other_ref, edge_ref, full, raw_ref, weights_ref, merged_ref, sems
):
    loads = []
    for b in range(BATCH):
        loads.append(
            pltpu.make_async_copy(raw_hbm.at[:, pl.ds(b * LANES, LANES)], raw_ref.at[b], sems.at[0, b])
        )
    load_weights = pltpu.make_async_copy(weights_hbm, weights_ref, sems.at[1, 0])
    load_merged = pltpu.make_async_copy(merged_hbm, merged_ref, sems.at[1, 1])
    for copy in loads:
        copy.start()
    load_weights.start()
    load_merged.start()
    me = ids_ref[0]
    first = ids_ref[1]
    half = ids_ref[2]
    scale = cols_ref[:, 1:2]
    bias = cols_ref[:, 0:1]
    lane = lax.broadcasted_iota(jnp.int32, (1, LANES), 1)
    scaled, coefs = [], []
    for b in range(BATCH):
        cols = slice(b * LANES, (b + 1) * LANES)
        loads[b].wait()
        raw = raw_ref[b]
        inv = inv_ref[0:1, cols]
        live = (first + lane < valid_ref[b]).astype(F32)
        gate = 0.5 * jnp.tanh(0.5 * (inv * raw + bias)) + 0.5
        cot = cot_ref[:, b * 32 : (b + 1) * 32, :].reshape(TRACKS, LANES).astype(F32)
        d_logits = (cot * scale) * gate
        d_rms = live * jnp.sum(d_logits * raw, axis=0, keepdims=True)
        scaled.append(((inv * live) * d_logits).astype(BF))
        coefs.append(inv * inv * inv * d_rms * (1.0 / C_OUT))
    load_weights.wait()
    load_merged.wait()
    d = dot(weights_ref[...], jnp.concatenate(scaled, axis=1), (1, 0)) * gain_ref[:, 0:1]
    for r in range(CHAN):
        rows = slice(r * 192, (r + 1) * 192)
        for b in range(BATCH):
            cols = slice(b * LANES, (b + 1) * LANES)
            full[b, me ^ r] = d[rows, cols] - coefs[b] * merged_ref[rows, cols].astype(F32)
    for b in range(BATCH):
        for g in range(CHAN):
            mine_ref[b, g] = full[b, g, pl.ds(pl.multiple_of(96 * half, 32), 96), :].astype(BF)
            other_ref[b, g] = full[b, g, pl.ds(pl.multiple_of(96 * (1 - half), 32), 96), :].astype(BF)
    start = jnp.where(me == CHAN - 1, LANES - 2, 0)
    row = lax.broadcasted_iota(jnp.int32, (16, LANES), 0)
    col = lax.broadcasted_iota(jnp.int32, (16, LANES), 1) - start
    edge = jnp.zeros((16, C_OUT), F32)
    for b in range(BATCH):
        sel = ((col >= 0) & (col < 2) & (row == b * 2 + col)).astype(BF)
        edge = edge + dot(sel, full[b].reshape(C_OUT, LANES).astype(BF), (1, 1))
    for l in range(6):
        edge_ref[l * 16 : (l + 1) * 16, :] = edge[:, l * LANES : (l + 1) * LANES].astype(BF)


def head(ids, valid, scored, cot):
    return pl.pallas_call(
        head_kernel,
        out_shape=(jax.ShapeDtypeStruct((BATCH, CHAN, 96, LANES), BF),) * 2
        + (jax.ShapeDtypeStruct((96, LANES), BF),),
        in_specs=[SM, SM, HBM, VM, HBM, HBM, VM, VM, VM],
        out_specs=(VM,) * 3,
        scratch_shapes=[
            pltpu.VMEM((BATCH, CHAN, 192, LANES), F32),
            pltpu.VMEM((BATCH, TRACKS, LANES), F32),
            pltpu.VMEM((C_OUT, TRACKS), BF),
            pltpu.VMEM((C_OUT, BATCH * LANES), BF),
            pltpu.SemaphoreType.DMA((2, BATCH)),
        ],
        compiler_params=params(61 * MIB),
        name="head",
    )(ids, valid, *scored, cot)


PAIR = 2


def rows_kernel(ids_ref, own_ref, far_ref, got_ref, tr_ref, trx_ref, edges, trunks, sems, trunk_sems):
    place = ids_ref[3]
    copies = [
        pltpu.make_async_copy(ref, trunks.at[q], trunk_sems.at[q]) for q, ref in enumerate((own_ref, far_ref))
    ]
    for q in range(PAIR):
        for i, step in enumerate((-1, 1)):
            source = jnp.clip((place ^ (4 * q)) + step, 0, SEQ - 1)
            copies.append(
                pltpu.make_async_copy(got_ref.at[source, pl.ds(128, 16)], edges.at[q, i], sems.at[q, i])
            )
    for copy in copies:
        copy.start()
    for copy in copies:
        copy.wait()
    row = lax.broadcasted_iota(jnp.int32, (256, 384), 0)
    ends = [jnp.zeros((LANES, 384), F32) for _ in range(KERNEL)]
    at = lax.broadcasted_iota(jnp.int32, (LANES, 384), 0)
    for q in range(PAIR):
        before = edges[q, 0].astype(F32) * ((place ^ (4 * q)) > 0).astype(F32)
        after = edges[q, 1].astype(F32) * ((place ^ (4 * q)) < SEQ - 1).astype(F32)
        for b in range(BATCH):
            t = trunks[q, b].astype(F32)
            rows = slice(b * 256, (b + 1) * 256)
            tr_ref[q, rows, 0:384] = jnp.where(row == 0, 0.0, pltpu.roll(t, 1, 0)).astype(BF)
            tr_ref[q, rows, 384:768] = trunks[q, b]
            tr_ref[q, rows, 768:1152] = jnp.where(row == 255, 0.0, pltpu.roll(t, 255, 0)).astype(BF)
            base = (q * BATCH + b) * 5
            first, last = (
                jnp.concatenate([x[b * 3 + l : b * 3 + l + 1] for l in range(3)], axis=1)
                for x in (before, after)
            )
            for column, tap, x in (
                (0, 1, t[127:128]), (0, 3, t[128:129]), (1, 1, t[255:256]), (1, 3, last),
                (2, 4, last), (3, 0, first), (4, 1, first),
            ):
                ends[tap] = jnp.where(at == base + column, x, ends[tap])
    for k in range(KERNEL):
        trx_ref[:, k * 384 : (k + 1) * 384] = ends[k].astype(BF)


def trunk_rows(ids, own, far, got):
    return pl.pallas_call(
        rows_kernel,
        out_shape=(jax.ShapeDtypeStruct((PAIR, 1024, 1152), BF),
                   jax.ShapeDtypeStruct((LANES, KERNEL * 384), BF)),
        in_specs=[SM, HBM, HBM, ANY],
        out_specs=(VM, VM),
        scratch_shapes=[pltpu.VMEM((PAIR, 2, 16, LANES), BF), pltpu.VMEM((PAIR, BATCH, 256, 384), BF),
                        pltpu.SemaphoreType.DMA((PAIR, 2)), pltpu.SemaphoreType.DMA((PAIR,))],
        compiler_params=params(30 * MIB),
        cost_estimate=pl.CostEstimate(flops=10**7, bytes_accessed=8 * 2**20, transcendentals=0),
        name="trunk_rows",
    )(ids, own, far, got)


ROWS = 368


def weight_kernel(ids_ref, *refs):
    pieces, (tr_ref, trx_ref, out_hbm, own_ref, full, out_ref, sems, own_sem, out_sems) = refs[:8], refs[8:]
    me = ids_ref[0]
    copies = []
    for q in range(PAIR):
        for r in range(CHAN):
            lanes = pl.ds(pl.multiple_of((me ^ r) * LANES, LANES), LANES)
            copies.append(
                pltpu.make_async_copy(pieces[q * CHAN + r], full.at[q, :, :, :, lanes], sems.at[q, r])
            )
    for copy in copies:
        copy.start()
    keep = pltpu.make_async_copy(full.at[0], own_ref, own_sem)
    p = lax.broadcasted_iota(jnp.int32, (256, 256), 0)
    q_ = lax.broadcasted_iota(jnp.int32, (256, 256), 1)
    even = (q_ < 128) & (p // 2 == q_)
    odd = (q_ >= 128) & ((p + 1) // 2 == q_ - 128)
    pick = (even | odd).astype(BF)
    last = jnp.zeros((384, LANES), F32)
    p1 = lax.broadcasted_iota(jnp.int32, (LANES, LANES), 0)
    q1 = lax.broadcasted_iota(jnp.int32, (LANES, LANES), 1)
    g_even = jnp.zeros((384, 1152), F32)
    g_odd = jnp.zeros((384, 768), F32)
    for q in range(PAIR):
        for copy in copies[q * CHAN : (q + 1) * CHAN]:
            copy.wait()
        if q == 0:
            keep.start()
        evens, odds = [], []
        for b in range(BATCH):
            for h in range(2):
                block = full[q, b, :, :, h * 256 : (h + 1) * 256].reshape(384, 256)
                e = dot(block, pick, (1, 0)).astype(BF)
                evens.append(e[:, :128])
                odds.append(e[:, 128:])
                place = q1 - (q * BATCH + b) * 5
                if h == 0:
                    sel = (((p1 < 2) & (place == 3)) | ((p1 == 0) & (place == 4))).astype(BF)
                    last = last + dot(block[:, :128], sel, (1, 0))
                    sel = (p1 == 127) & (place == 0)
                else:
                    sel = ((p1 == 127) & (place == 1)) | ((p1 >= 126) & (place == 2))
                last = last + dot(block[:, 128:], sel.astype(BF), (1, 0))
        g_even = g_even + dot(jnp.concatenate(evens, axis=1), tr_ref[q], (1, 0))
        g_odd = g_odd + dot(jnp.concatenate(odds, axis=1), tr_ref[q, :, :768], (1, 0))
    last = last.astype(BF)
    side = [dot(last, trx_ref[:, k * 384 : (k + 1) * 384], (1, 0)) for k in range(KERNEL)]
    pad = jnp.zeros((ROWS - 360, LANES), F32)
    taps = (g_even[:, :384], g_odd[:, :384], g_even[:, 384:768], g_odd[:, 384:], g_even[:, 768:])
    taps = [tap + term for tap, term in zip(taps, side)]
    stores = []
    for s in range(16):
        blocks = []
        for l in range(3):
            for tap in taps:
                blocks.append(tap[s * 24 : (s + 1) * 24, l * LANES : (l + 1) * LANES])
        out_ref[s] = jnp.concatenate(blocks + [pad], axis=0).astype(BF)
        if s % 4 == 3:
            part = pl.ds(s - 3, 4)
            stores.append(pltpu.make_async_copy(out_ref.at[part], out_hbm.at[part], out_sems.at[s // 4]))
            stores[-1].start()
    for store in stores:
        store.wait()
    keep.wait()


def weight_grad(ids, pieces, tr, trx):
    return pl.pallas_call(
        weight_kernel,
        out_shape=(jax.ShapeDtypeStruct((16, ROWS, LANES), BF),
                   jax.ShapeDtypeStruct((BATCH, CHAN, 96, 512), BF)),
        in_specs=[SM] + [ANY] * 8 + [VM] * 2,
        out_specs=(HBM, HBM),
        scratch_shapes=[pltpu.VMEM((PAIR, BATCH, CHAN, 96, 512), BF), pltpu.VMEM((16, ROWS, LANES), BF),
                        pltpu.SemaphoreType.DMA((PAIR, CHAN)), pltpu.SemaphoreType.DMA,
                        pltpu.SemaphoreType.DMA((4,))],
        compiler_params=params(30 * MIB),
        cost_estimate=pl.CostEstimate(flops=4 * 10**9, bytes_accessed=10 * 2**20, transcendentals=0),
        name="weight_grad",
    )(ids, *pieces, tr, trx)


def trunk_kernel(ids_ref, *refs):
    mine, other = refs[0], refs[1:5]
    conv_hbm, out_ref, skip_ref, full, sums, rims, conv_ref, sems, other_sems, skip_sem, conv_sem = refs[5:]
    me = ids_ref[0]
    half = ids_ref[2]
    skip = pltpu.make_async_copy(full.at[:, me], skip_ref, skip_sem)
    copies = [pltpu.make_async_copy(mine, full.at[:, :, half], sems.at[0, 0])]
    for r in range(CHAN):
        lanes = pl.ds(pl.multiple_of((me ^ r) * LANES, LANES), LANES)
        copies.append(pltpu.make_async_copy(other[r].at[BATCH * CHAN], rims.at[r], sems.at[1, r]))
        for b in range(BATCH):
            copies.append(
                pltpu.make_async_copy(
                    other[r].at[pl.ds(b * CHAN, CHAN)], full.at[b, :, 1 - half, :, lanes], other_sems.at[r, b]
                )
            )
    load = pltpu.make_async_copy(conv_hbm, conv_ref, conv_sem)
    for copy in copies + [load]:
        copy.start()
    row = lax.broadcasted_iota(jnp.int32, (2 * EXT, 512), 0)
    p = lax.broadcasted_iota(jnp.int32, (2 * EXT, 512), 1)
    lo = jnp.where(row < EXT, 2 * (row - 8), 2 * (row - EXT - 8) - 1)
    pick = ((p == lo) | (p == lo + 1)).astype(BF)
    col = lax.broadcasted_iota(jnp.int32, (2 * EXT, 32), 1)
    lo = lo[:, :32]
    for copy in copies:
        copy.wait()
    skip.start()
    rim = jnp.concatenate(
        [jnp.concatenate([rims[x, l * 16 : (l + 1) * 16, :] for l in range(6)], axis=1) for x in (me, me ^ 3)],
        axis=0,
    )
    for b in range(BATCH):
        offset = col % 16 - 2 * b
        rim_ok = (offset >= 0) & (offset < 2)
        rim_pos = jnp.where(col < 16, offset - 2, 512 + offset)
        pick_r = (rim_ok & ((rim_pos == lo) | (rim_pos == lo + 1))).astype(BF)
        e = (dot(pick, full[b].reshape(C_OUT, 512), (1, 1)) + dot(pick_r, rim, (1, 0))).astype(BF)
        sums[pl.ds(b * EXT, EXT), :C_OUT] = e[:EXT]
        sums[pl.ds(b * EXT, EXT), C_OUT:] = e[EXT:]
    load.wait()
    even, odd = sums[:, :C_OUT], sums[:, C_OUT:]
    up = dot(even, conv_ref[0], (1, 1)) + dot(odd, conv_ref[1], (1, 1))
    here = dot(even, conv_ref[2], (1, 1)) + dot(odd, conv_ref[3], (1, 1))
    down = dot(even, conv_ref[4], (1, 1))
    for b in range(BATCH):
        o = b * EXT + 8
        total = up[o + 1 : o + 257] + here[o : o + 256] + down[o - 1 : o + 255]
        out_ref[b] = total.astype(BF)
    skip.wait()


EXT = 272


def trunk_grad(ids, mine, other, conv_w):
    return pl.pallas_call(
        trunk_kernel,
        out_shape=(jax.ShapeDtypeStruct((BATCH, 256, 384), BF), jax.ShapeDtypeStruct((BATCH, 2, 96, 512), BF)),
        in_specs=[SM] + [HBM] * 6,
        out_specs=(VM, HBM),
        scratch_shapes=[pltpu.VMEM((BATCH, CHAN, 2, 96, 512), BF), pltpu.VMEM((BATCH * EXT, 2 * C_OUT), BF),
                        pltpu.VMEM((CHAN, 96, LANES), BF), pltpu.VMEM((KERNEL, 384, C_OUT), BF),
                        pltpu.SemaphoreType.DMA((2, CHAN)), pltpu.SemaphoreType.DMA((CHAN, BATCH)),
                        pltpu.SemaphoreType.DMA, pltpu.SemaphoreType.DMA],
        compiler_params=params(),
        cost_estimate=pl.CostEstimate(flops=8 * 10**9, bytes_accessed=16 * 2**20, transcendentals=0),
        name="trunk_grad",
    )(ids, mine, *other, conv_w)


def sum_kernel(scale, in_hbm, out_ref, terms, sems):
    copies = [
        pltpu.make_async_copy(in_hbm.at[pl.ds(i * 4, 4)], terms.at[pl.ds(i * 4, 4)], sems.at[i]) for i in range(4)
    ]
    for copy in copies:
        copy.start()
    total = jnp.zeros((ROWS, LANES), F32)
    for i in range(4):
        copies[i].wait()
        for s in range(i * 4, i * 4 + 4):
            total = total + terms[s].astype(F32)
    total = total * scale
    for l in range(3):
        for k in range(KERNEL):
            start = l * 120 + k * 24
            out_ref[k, :, l * LANES : (l + 1) * LANES] = total[start : start + 24]


def sum_weights(terms, scale):
    return pl.pallas_call(
        lambda *refs: sum_kernel(scale, *refs),
        out_shape=jax.ShapeDtypeStruct((KERNEL, 24, 384), F32),
        in_specs=[HBM],
        out_specs=VM,
        scratch_shapes=[pltpu.VMEM((16, ROWS, LANES), BF), pltpu.SemaphoreType.DMA((4,))],
        compiler_params=params(30 * MIB),
        name="sum_weights",
    )(terms)


def flip(x, r):
    return lax.ppermute(x, "chan", [(i, i ^ r) for i in range(CHAN)])


def partner(x):
    return lax.ppermute(x, "seq", [(i, i ^ 4) for i in range(SEQ)])


def partner_far(x):
    pairs = [(s * CHAN + c, (s ^ 4) * CHAN + (c ^ 2)) for s in range(SEQ) for c in range(CHAN)]
    return lax.ppermute(x, ("seq", "chan"), pairs)


def rim(x):
    up = [(s * CHAN + 3, (s + 1) * CHAN) for s in range(SEQ - 1)]
    down = [(s * CHAN, (s - 1) * CHAN + 3) for s in range(1, SEQ)]
    return lax.ppermute(x, ("seq", "chan"), up + down)


def across(x):
    pairs = [(s * CHAN + c, (s ^ 16) * CHAN + (c ^ 2)) for s in range(SEQ) for c in range(CHAN)]
    return lax.ppermute(x, ("seq", "chan"), pairs)


def local(
    trunk, merged, conv_w, norm_gain, head_w, head_bias, head_scale, head_of_track, valid_len, cot
):
    me = lax.axis_index("chan").astype(jnp.int32)
    place = lax.axis_index("seq").astype(jnp.int32)
    half = (place // 4) % 2
    ids = jnp.stack([me, place * 512 + me * LANES, half, place])
    trunk_far = partner(trunk)
    p0, p1, p2, p3 = cut_pieces(ids, merged, norm_gain[None])
    p1, p2, p3, cot = lax.optimization_barrier((p1, p2, p3, cot))
    send = cut_cot(ids, cot, trunk)
    p1, p2, p3 = flip(p1, 1), flip(p2, 2), flip(p3, 3)
    send, trunk, head_w = lax.optimization_barrier((send, trunk, head_w))
    far_head = across(head_w)
    near_head = flip(head_w, 1)
    send, p1, p2, p3, trunk_far = lax.optimization_barrier((send, p1, p2, p3, trunk_far))
    got = lax.all_to_all(send, "seq", 0, 0, tiled=True).reshape(SEQ, COT_ROWS, LANES)
    pieces = (p0, p1, p2, p3)
    heads = (head_w, near_head, far_head, flip(far_head, 1))

    scored = scores(pieces, heads, head_bias[None], head_of_track[None], head_scale)
    mine, other, edge = head(ids, valid_len, scored, got)
    trunk, _ = lax.optimization_barrier((trunk, mine))
    tr, trx = trunk_rows(ids, trunk, trunk_far, got)

    mine_far, other_x, other_far_x = flip(mine, 2), partner(other), partner_far(other)
    other = jnp.concatenate([other.reshape(BATCH * CHAN, 96, LANES), rim(edge)[None]])
    mine_far, other_x, other_far_x, other, tr, trx = lax.optimization_barrier(
        (mine_far, other_x, other_far_x, other, tr, trx)
    )
    mine_all = (mine, flip(mine, 1), mine_far, flip(mine_far, 1))
    blocks = mine_all + (other_x, flip(other_x, 1), other_far_x, flip(other_far_x, 1))
    terms, mine_rows = weight_grad(ids, blocks, tr, trx)
    other_late, _ = lax.optimization_barrier((other, mine_far))
    other_far = flip(other_late, 2)
    other_all = (other, flip(other, 1), other_far, flip(other_far, 1))
    groups = [[s for s in range(SEQ) if (s // 4) % 2 == u] for u in range(2)]
    summed = lax.all_to_all(terms, "seq", 0, 0, tiled=True, axis_index_groups=groups)
    d_trunk, d_skip = trunk_grad(ids, mine_rows, other_all, conv_w)
    grad_scale = 1.0 / math.sqrt(BATCH * 512 * SEQ)
    d_conv_w = sum_weights(summed, grad_scale)
    return (d_trunk, d_skip.reshape(BATCH, 192, 512), d_conv_w)


def solution(mesh):
    placed = (
        P(None, "seq", "chan"),
        P(None, "chan", "seq"),
        P(None, "chan", None),
        P("chan"),
        P("chan", None),
        P(),
        P(),
        P(),
        P(),
        P(None, "seq", None),
    )
    return jax.shard_map(
        local,
        mesh=mesh,
        in_specs=placed,
        out_specs=(P(None, "seq", "chan"), P(None, "chan", "seq"), P(None, "seq", "chan")),
        check_vma=False,
    )
```

```python
import math

import jax
import jax.numpy as jnp
from jax import lax
from jax.experimental import pallas as pl
from jax.experimental.pallas import tpu as pltpu
from jax.sharding import PartitionSpec as P

BATCH = 4
C_OUT = 768
TRACKS = 1024
KERNEL = 5
SEQ = 32
CHAN = 4
LANES = 128
epsilon = 1e-06

BF = jnp.bfloat16
F32 = jnp.float32
MIB = 1024 * 1024


def params(limit=62 * MIB):
    return pltpu.CompilerParams(vmem_limit_bytes=limit)


def dot(a, b, contract):
    return lax.dot_general(a, b, ((contract[:1], contract[1:]), ((), ())), preferred_element_type=F32)


ANY = pl.BlockSpec(memory_space=pl.ANY)
VM = pl.BlockSpec(memory_space=pltpu.VMEM)
HBM = pl.BlockSpec(memory_space=pltpu.HBM)
SM = pl.BlockSpec(memory_space=pltpu.SMEM)


PIECE = BATCH * 192 + 16


def pieces_kernel(ids_ref, merged_ref, gain_ref, p0, p1, p2, p3, line, sems, line_sem):
    me = ids_ref[0]
    load = pltpu.make_async_copy(gain_ref, line, line_sem)
    load.start()
    copies = []
    for r, piece in enumerate((p0, p1, p2, p3)):
        lanes = pl.ds(pl.multiple_of((me ^ r) * LANES, LANES), LANES)
        for b in range(BATCH):
            rows = pl.ds(b * 192, 192)
            copies.append(pltpu.make_async_copy(merged_ref.at[b, :, lanes], piece.at[rows, :], sems.at[r, b]))
    for copy in copies:
        copy.start()
    load.wait()
    tail = jnp.concatenate([line[:, LANES:], jnp.zeros((1, 2 * LANES - 192), F32)], axis=1)
    rest = jnp.concatenate([line[:, :LANES], tail], axis=0)
    rows = []
    for _ in range(3):
        part = rest.astype(BF).astype(F32)
        rows.append(part)
        rest = rest - part
    gains = jnp.concatenate(rows + [jnp.zeros((10, LANES), F32)], axis=0).astype(BF)
    for piece in (p0, p1, p2, p3):
        piece[BATCH * 192 :, :] = gains
    for copy in copies:
        copy.wait()


def cut_pieces(ids, merged, gain):
    return pl.pallas_call(
        pieces_kernel,
        out_shape=(jax.ShapeDtypeStruct((PIECE, LANES), BF),) * CHAN,
        in_specs=[SM, HBM, HBM],
        out_specs=(VM,) * CHAN,
        scratch_shapes=[pltpu.VMEM((1, 192), F32), pltpu.SemaphoreType.DMA((CHAN, BATCH)), pltpu.SemaphoreType.DMA],
        compiler_params=params(),
        name="cut_pieces",
    )(ids, merged, gain)


COT_ROWS = 9 * 16


def cot_kernel(ids_ref, cot_ref, trunk_ref, send_ref, edges, sems, edge_sems):
    me, place = ids_ref[0], ids_ref[3]
    copies = []
    for d in range(SEQ):
        start = pl.multiple_of(d * CHAN * LANES + me * LANES, LANES)
        copies.append(
            pltpu.make_async_copy(cot_ref.at[:, :, pl.ds(start, LANES)], send_ref.at[d, pl.ds(0, 8)], sems.at[d])
        )
    loads = [
        pltpu.make_async_copy(trunk_ref.at[:, pl.ds(row, 16), :], edges.at[i], edge_sems.at[i])
        for i, row in enumerate((0, 240))
    ]
    for copy in loads + copies:
        copy.start()
    for load in loads:
        load.wait()
    rows = []
    for i, row in enumerate((0, 15)):
        parts = []
        for b in range(BATCH):
            line = edges[i, b].astype(F32)[row : row + 1]
            parts += [line[:, l * LANES : (l + 1) * LANES] for l in range(3)]
        rows.append(jnp.concatenate(parts + [jnp.zeros((4, LANES), F32)], axis=0))
    for d in range(SEQ):
        up = ((place + 1 == d) | (place + 1 == (d ^ 8))).astype(F32)
        down = ((place - 1 == d) | (place - 1 == (d ^ 8))).astype(F32)
        send_ref[d, 8] = (rows[1] * up + rows[0] * down).astype(BF)
    for copy in copies:
        copy.wait()


def cut_cot(ids, cot, trunk):
    return pl.pallas_call(
        cot_kernel,
        out_shape=jax.ShapeDtypeStruct((SEQ, 9, 16, LANES), BF),
        in_specs=[SM, HBM, HBM],
        out_specs=VM,
        scratch_shapes=[pltpu.VMEM((2, BATCH, 16, 384), BF), pltpu.SemaphoreType.DMA((SEQ,)),
                        pltpu.SemaphoreType.DMA((2,))],
        compiler_params=params(),
        cost_estimate=pl.CostEstimate(flops=0, bytes_accessed=5 * 2**20, transcendentals=0),
        name="cut_cot",
    )(ids, cot.reshape(BATCH * 2, 16, -1), trunk)


WIDE, NARROW = 9, 12


def score_kernel(*refs):
    pieces, heads, (bias_ref, of_track_ref, scale_ref) = refs[:4], refs[4:8], refs[8:11]
    wide_hbm, narrow_hbm, raw_ref, small_ref, weights_ref, merged_ref = refs[11:17]
    parts, sems, head_sems, part_sems, out_sems = refs[17:]
    cols_ref = small_ref.at[:, 0:LANES]
    gain_ref = small_ref.at[0:C_OUT, LANES : 2 * LANES]
    copies = []
    for r in range(CHAN):
        rows = pl.ds(r * 192, 192)
        for b in range(BATCH):
            copies.append(
                pltpu.make_async_copy(
                    pieces[r].at[pl.ds(b * 192, 192), :],
                    merged_ref.at[rows, pl.ds(b * LANES, LANES)],
                    sems.at[r, b],
                )
            )
        copies.append(
            pltpu.make_async_copy(pieces[r].at[pl.ds(BATCH * 192, 16), :], parts.at[r], part_sems.at[r])
        )
    loads = [
        pltpu.make_async_copy(heads[r], weights_ref.at[pl.ds(r * 192, 192), :], head_sems.at[r])
        for r in range(CHAN)
    ]
    for copy in copies + loads:
        copy.start()
    track_scale = jnp.zeros((1, TRACKS), F32)
    for h in range(scale_ref.shape[0]):
        track_scale = jnp.where(of_track_ref[...] == h, scale_ref[h], track_scale)
    lines = []
    for rest in (bias_ref[...], track_scale):
        for _ in range(3):
            part = rest.astype(BF).astype(F32)
            lines.append(part)
            rest = rest - part
    lines = jnp.concatenate(lines + [jnp.zeros((10, TRACKS), F32)], axis=0).astype(BF)
    row = lax.broadcasted_iota(jnp.int32, (16, LANES), 0)
    lane = lax.broadcasted_iota(jnp.int32, (16, LANES), 1)
    cols_ref[...] = dot(lines, ((row < 6) & (row // 3 == lane)).astype(BF), (0, 0))
    for copy in copies:
        copy.wait()
    for r in range(CHAN):
        for side in range(2):
            pick = ((row < 6) & (row % 2 == side)).astype(BF)
            size = LANES - side * 64
            start = r * 192 + side * LANES
            gain_ref[start : start + size, :] = dot(parts[r], pick, (0, 0))[:size]
    m32 = merged_ref[...].astype(F32)
    total = jnp.sum(m32 * m32, axis=0, keepdims=True)
    inv = lax.rsqrt(total / C_OUT + epsilon)
    for b in range(BATCH):
        small_ref[8 * b : 8 * b + 8, 2 * LANES : 3 * LANES] = jnp.broadcast_to(
            inv[:, b * LANES : (b + 1) * LANES], (8, LANES)
        )
    normed = (m32 * gain_ref[:, 0:1]).astype(BF)
    for load in loads:
        load.wait()
    stores = [
        pltpu.make_async_copy(small_ref, wide_hbm.at[1, :, pl.ds(0, 3 * LANES)], out_sems.at[0]),
        pltpu.make_async_copy(weights_ref, narrow_hbm.at[0], out_sems.at[1]),
        pltpu.make_async_copy(merged_ref, narrow_hbm.at[1, :, pl.ds(0, BATCH * LANES)], out_sems.at[2]),
    ]
    for store in stores:
        store.start()
    raw_ref[...] = dot(weights_ref[...], normed, (0, 0))
    stores.append(pltpu.make_async_copy(raw_ref, wide_hbm.at[0], out_sems.at[3]))
    stores[-1].start()
    for store in stores:
        store.wait()


def scores(pieces, heads, bias, of_track, scale):
    return pl.pallas_call(
        score_kernel,
        out_shape=(jax.ShapeDtypeStruct((WIDE, TRACKS, BATCH * LANES), F32),
                   jax.ShapeDtypeStruct((NARROW, C_OUT, TRACKS), BF)),
        in_specs=[HBM] * 8 + [VM, VM, SM],
        out_specs=(HBM, HBM),
        scratch_shapes=[
            pltpu.VMEM((TRACKS, BATCH * LANES), F32),
            pltpu.VMEM((TRACKS, 3 * LANES), F32),
            pltpu.VMEM((C_OUT, TRACKS), BF),
            pltpu.VMEM((C_OUT, BATCH * LANES), BF),
            pltpu.VMEM((CHAN, 16, LANES), BF),
            pltpu.SemaphoreType.DMA((CHAN, BATCH)),
            pltpu.SemaphoreType.DMA((CHAN,)),
            pltpu.SemaphoreType.DMA((CHAN,)),
            pltpu.SemaphoreType.DMA((4,)),
        ],
        compiler_params=params(),
        cost_estimate=pl.CostEstimate(flops=45 * 10**8, bytes_accessed=8 * 2**20, transcendentals=0),
        name="scores",
    )(*pieces, *heads, bias, of_track, scale)


HALF = BATCH * 384


def head_kernel(
    ids_ref, valid_ref, wide_hbm, narrow_hbm, cot_ref,
    mine_ref, other_ref, edge_ref, full, raw_ref, small_ref, weights_ref, merged_ref, sems
):
    load_small = pltpu.make_async_copy(wide_hbm.at[1, :, pl.ds(0, 3 * LANES)], small_ref, sems.at[1, 2])
    load_small.start()
    loads = []
    for b in range(BATCH):
        loads.append(
            pltpu.make_async_copy(wide_hbm.at[0, :, pl.ds(b * LANES, LANES)], raw_ref.at[b], sems.at[0, b])
        )
    load_weights = pltpu.make_async_copy(narrow_hbm.at[0], weights_ref, sems.at[1, 0])
    load_merged = pltpu.make_async_copy(narrow_hbm.at[1, :, pl.ds(0, BATCH * LANES)], merged_ref, sems.at[1, 1])
    for copy in loads:
        copy.start()
    load_weights.start()
    load_merged.start()
    load_small.wait()
    me = ids_ref[0]
    first = ids_ref[1]
    half = ids_ref[2]
    scale = small_ref[:, 1:2]
    bias = small_ref[:, 0:1]
    lane = lax.broadcasted_iota(jnp.int32, (1, LANES), 1)
    scaled, coefs = [], []
    for b in range(BATCH):
        cols = slice(b * LANES, (b + 1) * LANES)
        loads[b].wait()
        raw = raw_ref[b]
        inv = small_ref[8 * b : 8 * b + 1, 2 * LANES : 3 * LANES]
        live = (first + lane < valid_ref[b]).astype(F32)
        gate = 0.5 * jnp.tanh(0.5 * (inv * raw + bias)) + 0.5
        cot = cot_ref[:, b * 32 : (b + 1) * 32, :].reshape(TRACKS, LANES).astype(F32)
        d_logits = (cot * scale) * gate
        d_rms = live * jnp.sum(d_logits * raw, axis=0, keepdims=True)
        scaled.append(((inv * live) * d_logits).astype(BF))
        coefs.append(inv * inv * inv * d_rms * (1.0 / C_OUT))
    load_weights.wait()
    load_merged.wait()
    d = dot(weights_ref[...], jnp.concatenate(scaled, axis=1), (1, 0)) * small_ref[0:C_OUT, LANES : LANES + 1]
    for r in range(CHAN):
        rows = slice(r * 192, (r + 1) * 192)
        for b in range(BATCH):
            cols = slice(b * LANES, (b + 1) * LANES)
            full[b, me ^ r] = d[rows, cols] - coefs[b] * merged_ref[rows, cols].astype(F32)
    for b in range(BATCH):
        for g in range(2):
            rows = slice((b * 2 + g) * 192, (b * 2 + g + 1) * 192)
            mine_ref[rows, :] = full[b, 2 * g + half].astype(BF)
            other_ref[rows, :] = full[b, 2 * g + 1 - half].astype(BF)
    start = jnp.where(me == CHAN - 1, LANES - 2, 0)
    row = lax.broadcasted_iota(jnp.int32, (16, LANES), 0)
    col = lax.broadcasted_iota(jnp.int32, (16, LANES), 1) - start
    edge = jnp.zeros((16, C_OUT), F32)
    for b in range(BATCH):
        sel = ((col >= 0) & (col < 2) & (row == b * 2 + col)).astype(BF)
        edge = edge + dot(sel, full[b].reshape(C_OUT, LANES).astype(BF), (1, 1))
    for l in range(6):
        edge_ref[l * 16 : (l + 1) * 16, :] = edge[:, l * LANES : (l + 1) * LANES].astype(BF)


def head(ids, valid, scored, cot):
    return pl.pallas_call(
        head_kernel,
        out_shape=(jax.ShapeDtypeStruct((HALF, LANES), BF),) * 2 + (jax.ShapeDtypeStruct((96, LANES), BF),),
        in_specs=[SM, SM, HBM, HBM, VM],
        out_specs=(VM,) * 3,
        scratch_shapes=[
            pltpu.VMEM((BATCH, CHAN, 192, LANES), F32),
            pltpu.VMEM((BATCH, TRACKS, LANES), F32),
            pltpu.VMEM((TRACKS, 3 * LANES), F32),
            pltpu.VMEM((C_OUT, TRACKS), BF),
            pltpu.VMEM((C_OUT, BATCH * LANES), BF),
            pltpu.SemaphoreType.DMA((2, BATCH)),
        ],
        compiler_params=params(48 * MIB),
        name="head",
    )(ids, valid, *scored, cot)


PAIR = 2


def rows_kernel(ids_ref, own_ref, far_ref, got_ref, tr_ref, trx_ref, edges, trunks, sems, trunk_sems):
    place = ids_ref[3]
    copies = [
        pltpu.make_async_copy(ref, trunks.at[q], trunk_sems.at[q]) for q, ref in enumerate((own_ref, far_ref))
    ]
    for q in range(PAIR):
        for i, step in enumerate((-1, 1)):
            source = jnp.clip((place ^ (8 * q)) + step, 0, SEQ - 1)
            copies.append(
                pltpu.make_async_copy(got_ref.at[source, pl.ds(128, 16)], edges.at[q, i], sems.at[q, i])
            )
    for copy in copies:
        copy.start()
    for copy in copies:
        copy.wait()
    row = lax.broadcasted_iota(jnp.int32, (256, 384), 0)
    ends = [jnp.zeros((LANES, 384), F32) for _ in range(KERNEL)]
    at = lax.broadcasted_iota(jnp.int32, (LANES, 384), 0)
    for q in range(PAIR):
        before = edges[q, 0].astype(F32) * ((place ^ (8 * q)) > 0).astype(F32)
        after = edges[q, 1].astype(F32) * ((place ^ (8 * q)) < SEQ - 1).astype(F32)
        for b in range(BATCH):
            t = trunks[q, b].astype(F32)
            rows = slice(b * 256, (b + 1) * 256)
            tr_ref[q, rows, 0:384] = jnp.where(row == 0, 0.0, pltpu.roll(t, 1, 0)).astype(BF)
            tr_ref[q, rows, 384:768] = trunks[q, b]
            tr_ref[q, rows, 768:1152] = jnp.where(row == 255, 0.0, pltpu.roll(t, 255, 0)).astype(BF)
            base = (q * BATCH + b) * 5
            first, last = (
                jnp.concatenate([x[b * 3 + l : b * 3 + l + 1] for l in range(3)], axis=1)
                for x in (before, after)
            )
            for column, tap, x in (
                (0, 1, t[127:128]), (0, 3, t[128:129]), (1, 1, t[255:256]), (1, 3, last),
                (2, 4, last), (3, 0, first), (4, 1, first),
            ):
                ends[tap] = jnp.where(at == base + column, x, ends[tap])
    for k in range(KERNEL):
        trx_ref[:, k * 384 : (k + 1) * 384] = ends[k].astype(BF)


def trunk_rows(ids, own, far, got):
    return pl.pallas_call(
        rows_kernel,
        out_shape=(jax.ShapeDtypeStruct((PAIR, 1024, 1152), BF),
                   jax.ShapeDtypeStruct((LANES, KERNEL * 384), BF)),
        in_specs=[SM, HBM, HBM, ANY],
        out_specs=(VM, VM),
        scratch_shapes=[pltpu.VMEM((PAIR, 2, 16, LANES), BF), pltpu.VMEM((PAIR, BATCH, 256, 384), BF),
                        pltpu.SemaphoreType.DMA((PAIR, 2)), pltpu.SemaphoreType.DMA((PAIR,))],
        compiler_params=params(30 * MIB),
        cost_estimate=pl.CostEstimate(flops=10**7, bytes_accessed=8 * 2**20, transcendentals=0),
        name="trunk_rows",
    )(ids, own, far, got)


ROWS = 368
KEPT = 18


def weight_kernel(ids_ref, *refs):
    pieces, (tr_ref, trx_ref, out_hbm, own_ref, full, out_ref, sems, own_sem, out_sems) = refs[:8], refs[8:]
    me = ids_ref[0]
    copies = []
    for q in range(PAIR):
        for r in range(CHAN):
            lanes = pl.ds(pl.multiple_of((me ^ r) * LANES, LANES), LANES)
            copies.append(pltpu.make_async_copy(pieces[q * CHAN + r], full.at[q, :, lanes], sems.at[q, r]))
    for copy in copies:
        copy.start()
    keep = pltpu.make_async_copy(full.at[0], own_ref.at[0], own_sem)
    p = lax.broadcasted_iota(jnp.int32, (256, 256), 0)
    q_ = lax.broadcasted_iota(jnp.int32, (256, 256), 1)
    even = (q_ < 128) & (p // 2 == q_)
    odd = (q_ >= 128) & ((p + 1) // 2 == q_ - 128)
    pick = (even | odd).astype(BF)
    last = jnp.zeros((384, LANES), F32)
    p1 = lax.broadcasted_iota(jnp.int32, (LANES, LANES), 0)
    q1 = lax.broadcasted_iota(jnp.int32, (LANES, LANES), 1)
    g_even = jnp.zeros((384, 1152), F32)
    g_odd = jnp.zeros((384, 768), F32)
    for q in range(PAIR):
        for copy in copies[q * CHAN : (q + 1) * CHAN]:
            copy.wait()
        if q == 0:
            keep.start()
        evens, odds = [], []
        for b in range(BATCH):
            for h in range(2):
                block = full[q, b * 384 : (b + 1) * 384, h * 256 : (h + 1) * 256]
                e = dot(block, pick, (1, 0)).astype(BF)
                evens.append(e[:, :128])
                odds.append(e[:, 128:])
                place = q1 - (q * BATCH + b) * 5
                if h == 0:
                    sel = (((p1 < 2) & (place == 3)) | ((p1 == 0) & (place == 4))).astype(BF)
                    last = last + dot(block[:, :128], sel, (1, 0))
                    sel = (p1 == 127) & (place == 0)
                else:
                    sel = ((p1 == 127) & (place == 1)) | ((p1 >= 126) & (place == 2))
                last = last + dot(block[:, 128:], sel.astype(BF), (1, 0))
        g_even = g_even + dot(jnp.concatenate(evens, axis=1), tr_ref[q], (1, 0))
        g_odd = g_odd + dot(jnp.concatenate(odds, axis=1), tr_ref[q, :, :768], (1, 0))
    last = last.astype(BF)
    side = [dot(last, trx_ref[:, k * 384 : (k + 1) * 384], (1, 0)) for k in range(KERNEL)]
    pad = jnp.zeros((ROWS - 360, LANES), F32)
    taps = (g_even[:, :384], g_odd[:, :384], g_even[:, 384:768], g_odd[:, 384:], g_even[:, 768:])
    taps = [tap + term for tap, term in zip(taps, side)]
    stores = []
    for s in range(16):
        blocks = []
        for l in range(3):
            for tap in taps:
                blocks.append(tap[s * 24 : (s + 1) * 24, l * LANES : (l + 1) * LANES])
        out_ref[s] = jnp.concatenate(blocks + [pad], axis=0).astype(BF)
        if s % 4 == 3:
            part = pl.ds(s - 3, 4)
            stores.append(pltpu.make_async_copy(out_ref.at[part], out_hbm.at[part], out_sems.at[s // 4]))
            stores[-1].start()
    for store in stores:
        store.wait()
    keep.wait()


def weight_grad(ids, pieces, tr, trx):
    return pl.pallas_call(
        weight_kernel,
        out_shape=(jax.ShapeDtypeStruct((16, ROWS, LANES), BF),
                   jax.ShapeDtypeStruct((KEPT, HALF, 512), BF)),
        in_specs=[SM] + [ANY] * 8 + [VM] * 2,
        out_specs=(HBM, HBM),
        scratch_shapes=[pltpu.VMEM((PAIR, HALF, 512), BF), pltpu.VMEM((16, ROWS, LANES), BF),
                        pltpu.SemaphoreType.DMA((PAIR, CHAN)), pltpu.SemaphoreType.DMA,
                        pltpu.SemaphoreType.DMA((4,))],
        compiler_params=params(40 * MIB),
        cost_estimate=pl.CostEstimate(flops=4 * 10**9, bytes_accessed=10 * 2**20, transcendentals=0),
        name="weight_grad",
    )(ids, *pieces, tr, trx)


def trunk_kernel(ids_ref, *refs):
    mine, other = refs[0], refs[1:5]
    conv_hbm, out_ref, skip_ref, full, sums, rims, conv_ref, sems, mine_sems, other_sems, skip_sem, conv_sem = refs[5:]
    me = ids_ref[0]
    half = ids_ref[2]
    skip = pltpu.make_async_copy(full.at[:, me // 2, me % 2], skip_ref, skip_sem)
    copies = []
    for b in range(BATCH):
        for g in range(2):
            rows = pl.ds((b * 2 + g) * 192, 192)
            copies.append(pltpu.make_async_copy(mine.at[0, rows, :], full.at[b, g, half], mine_sems.at[b, g]))
            for r in range(CHAN):
                lanes = pl.ds(pl.multiple_of((me ^ r) * LANES, LANES), LANES)
                copies.append(
                    pltpu.make_async_copy(
                        other[r].at[rows, :], full.at[b, g, 1 - half, :, lanes], other_sems.at[r, b, g]
                    )
                )
    for r in range(CHAN):
        copies.append(pltpu.make_async_copy(other[r].at[pl.ds(HALF, 96), :], rims.at[r], sems.at[r]))
    load = pltpu.make_async_copy(conv_hbm, conv_ref, conv_sem)
    for copy in copies + [load]:
        copy.start()
    row = lax.broadcasted_iota(jnp.int32, (2 * EXT, 512), 0)
    p = lax.broadcasted_iota(jnp.int32, (2 * EXT, 512), 1)
    lo = jnp.where(row < EXT, 2 * (row - 8), 2 * (row - EXT - 8) - 1)
    pick = ((p == lo) | (p == lo + 1)).astype(BF)
    col = lax.broadcasted_iota(jnp.int32, (2 * EXT, 32), 1)
    lo = lo[:, :32]
    for copy in copies:
        copy.wait()
    skip.start()
    rim = jnp.concatenate(
        [jnp.concatenate([rims[x, l * 16 : (l + 1) * 16, :] for l in range(6)], axis=1) for x in (me, me ^ 3)],
        axis=0,
    )
    for b in range(BATCH):
        offset = col % 16 - 2 * b
        rim_ok = (offset >= 0) & (offset < 2)
        rim_pos = jnp.where(col < 16, offset - 2, 512 + offset)
        pick_r = (rim_ok & ((rim_pos == lo) | (rim_pos == lo + 1))).astype(BF)
        e = (dot(pick, full[b].reshape(C_OUT, 512), (1, 1)) + dot(pick_r, rim, (1, 0))).astype(BF)
        sums[pl.ds(b * EXT, EXT), :C_OUT] = e[:EXT]
        sums[pl.ds(b * EXT, EXT), C_OUT:] = e[EXT:]
    load.wait()
    even, odd = sums[:, :C_OUT], sums[:, C_OUT:]
    up = dot(even, conv_ref[0], (1, 1)) + dot(odd, conv_ref[1], (1, 1))
    here = dot(even, conv_ref[2], (1, 1)) + dot(odd, conv_ref[3], (1, 1))
    down = dot(even, conv_ref[4], (1, 1))
    for b in range(BATCH):
        o = b * EXT + 8
        total = up[o + 1 : o + 257] + here[o : o + 256] + down[o - 1 : o + 255]
        out_ref[b] = total.astype(BF)
    skip.wait()


EXT = 272


def trunk_grad(ids, mine, other, conv_w):
    return pl.pallas_call(
        trunk_kernel,
        out_shape=(jax.ShapeDtypeStruct((BATCH, 256, 384), BF), jax.ShapeDtypeStruct((BATCH, 192, 512), BF)),
        in_specs=[SM] + [HBM] * 6,
        out_specs=(VM, HBM),
        scratch_shapes=[pltpu.VMEM((BATCH, 2, 2, 192, 512), BF), pltpu.VMEM((BATCH * EXT, 2 * C_OUT), BF),
                        pltpu.VMEM((CHAN, 96, LANES), BF), pltpu.VMEM((KERNEL, 384, C_OUT), BF),
                        pltpu.SemaphoreType.DMA((CHAN,)), pltpu.SemaphoreType.DMA((BATCH, 2)),
                        pltpu.SemaphoreType.DMA((CHAN, BATCH, 2)), pltpu.SemaphoreType.DMA,
                        pltpu.SemaphoreType.DMA],
        compiler_params=params(),
        cost_estimate=pl.CostEstimate(flops=8 * 10**9, bytes_accessed=16 * 2**20, transcendentals=0),
        name="trunk_grad",
    )(ids, mine, *other, conv_w)


def sum_kernel(scale, in_hbm, out_ref, terms, sems):
    copies = [
        pltpu.make_async_copy(in_hbm.at[pl.ds(i * 4, 4)], terms.at[pl.ds(i * 4, 4)], sems.at[i]) for i in range(4)
    ]
    for copy in copies:
        copy.start()
    total = jnp.zeros((ROWS, LANES), F32)
    for i in range(4):
        copies[i].wait()
        for s in range(i * 4, i * 4 + 4):
            total = total + terms[s].astype(F32)
    total = total * scale
    for l in range(3):
        for k in range(KERNEL):
            start = l * 120 + k * 24
            out_ref[k, :, l * LANES : (l + 1) * LANES] = total[start : start + 24]


def sum_weights(terms, scale):
    return pl.pallas_call(
        lambda *refs: sum_kernel(scale, *refs),
        out_shape=jax.ShapeDtypeStruct((KERNEL, 24, 384), F32),
        in_specs=[HBM],
        out_specs=VM,
        scratch_shapes=[pltpu.VMEM((16, ROWS, LANES), BF), pltpu.SemaphoreType.DMA((4,))],
        compiler_params=params(30 * MIB),
        name="sum_weights",
    )(terms)


def flip(x, r):
    return lax.ppermute(x, "chan", [(i, i ^ r) for i in range(CHAN)])


def partner(x):
    return lax.ppermute(x, "seq", [(i, i ^ 8) for i in range(SEQ)])


def partner_far(x):
    pairs = [(s * CHAN + c, (s ^ 8) * CHAN + (c ^ 2)) for s in range(SEQ) for c in range(CHAN)]
    return lax.ppermute(x, ("seq", "chan"), pairs)


def rim(x):
    up = [(s * CHAN + 3, (s + 1) * CHAN) for s in range(SEQ - 1)]
    down = [(s * CHAN, (s - 1) * CHAN + 3) for s in range(1, SEQ)]
    return lax.ppermute(x, ("seq", "chan"), up + down)


def across(x):
    pairs = [(s * CHAN + c, (s ^ 16) * CHAN + (c ^ 2)) for s in range(SEQ) for c in range(CHAN)]
    return lax.ppermute(x, ("seq", "chan"), pairs)


def local(
    trunk, merged, conv_w, norm_gain, head_w, head_bias, head_scale, head_of_track, valid_len, cot
):
    me = lax.axis_index("chan").astype(jnp.int32)
    place = lax.axis_index("seq").astype(jnp.int32)
    half = (place // 8) % 2
    ids = jnp.stack([me, place * 512 + me * LANES, half, place])
    trunk_far = partner(trunk)
    p0, p1, p2, p3 = cut_pieces(ids, merged, norm_gain[None])
    p1, p2, p3, cot = lax.optimization_barrier((p1, p2, p3, cot))
    send = cut_cot(ids, cot, trunk)
    p1, p2, p3 = flip(p1, 1), flip(p2, 2), flip(p3, 3)
    send, trunk, head_w = lax.optimization_barrier((send, trunk, head_w))
    far_head = across(head_w)
    near_head = flip(head_w, 1)
    send, p1, p2, p3, trunk_far = lax.optimization_barrier((send, p1, p2, p3, trunk_far))
    got = lax.all_to_all(send, "seq", 0, 0, tiled=True).reshape(SEQ, COT_ROWS, LANES)
    pieces = (p0, p1, p2, p3)
    heads = (head_w, near_head, far_head, flip(far_head, 1))

    scored = scores(pieces, heads, head_bias[None], head_of_track[None], head_scale)
    mine, other, edge = head(ids, valid_len, scored, got)
    trunk, _ = lax.optimization_barrier((trunk, mine))
    tr, trx = trunk_rows(ids, trunk, trunk_far, got)

    mine_far, other_x, other_far_x = flip(mine, 2), partner(other), partner_far(other)
    other = jnp.concatenate([other, rim(edge)])
    mine_far, other_x, other_far_x, other, tr, trx = lax.optimization_barrier(
        (mine_far, other_x, other_far_x, other, tr, trx)
    )
    mine_all = (mine, flip(mine, 1), mine_far, flip(mine_far, 1))
    blocks = mine_all + (other_x, flip(other_x, 1), other_far_x, flip(other_far_x, 1))
    terms, mine_rows = weight_grad(ids, blocks, tr, trx)
    other_late, _ = lax.optimization_barrier((other, mine_far))
    other_far = flip(other_late, 2)
    other_all = (other, flip(other, 1), other_far, flip(other_far, 1))
    groups = [[s for s in range(SEQ) if (s // 8) % 2 == u] for u in range(2)]
    summed = lax.all_to_all(terms, "seq", 0, 0, tiled=True, axis_index_groups=groups)
    d_trunk, d_skip = trunk_grad(ids, mine_rows, other_all, conv_w)
    grad_scale = 1.0 / math.sqrt(BATCH * 512 * SEQ)
    d_conv_w = sum_weights(summed, grad_scale)
    return (d_trunk, d_skip, d_conv_w)


def solution(mesh):
    placed = (
        P(None, "seq", "chan"),
        P(None, "chan", "seq"),
        P(None, "chan", None),
        P("chan"),
        P("chan", None),
        P(),
        P(),
        P(),
        P(),
        P(None, "seq", None),
    )
    return jax.shard_map(
        local,
        mesh=mesh,
        in_specs=placed,
        out_specs=(P(None, "seq", "chan"), P(None, "chan", "seq"), P(None, "seq", "chan")),
        check_vma=False,
    )
```

```python
import functools
import math

import jax
import jax.numpy as jnp
from jax import lax
from jax.experimental import pallas as pl
from jax.experimental.pallas import tpu as pltpu
from jax.sharding import PartitionSpec as P

BATCH = 4
C_OUT = 768
TRACKS = 1024
KERNEL = 5
SEQ = 32
CHAN = 4
LANES = 128
epsilon = 1e-06

BF = jnp.bfloat16
F32 = jnp.float32
MIB = 1024 * 1024


def params(limit=62 * MIB):
    return pltpu.CompilerParams(vmem_limit_bytes=limit)


def dot(a, b, contract):
    return lax.dot_general(a, b, ((contract[:1], contract[1:]), ((), ())), preferred_element_type=F32)


ANY = pl.BlockSpec(memory_space=pl.ANY)
VM = pl.BlockSpec(memory_space=pltpu.VMEM)
HBM = pl.BlockSpec(memory_space=pltpu.HBM)
SM = pl.BlockSpec(memory_space=pltpu.SMEM)


PIECE = BATCH * 192 + 16


def pieces_kernel(ids_ref, merged_ref, gain_ref, p0, p1, p2, p3, line, sems, line_sem):
    me = ids_ref[0]
    load = pltpu.make_async_copy(gain_ref, line, line_sem)
    load.start()
    copies = []
    for r, piece in enumerate((p0, p1, p2, p3)):
        lanes = pl.ds(pl.multiple_of((me ^ r) * LANES, LANES), LANES)
        for b in range(BATCH):
            rows = pl.ds(b * 192, 192)
            copies.append(pltpu.make_async_copy(merged_ref.at[b, :, lanes], piece.at[rows, :], sems.at[r, b]))
    for copy in copies:
        copy.start()
    load.wait()
    tail = jnp.concatenate([line[:, LANES:], jnp.zeros((1, 2 * LANES - 192), F32)], axis=1)
    rest = jnp.concatenate([line[:, :LANES], tail], axis=0)
    rows = []
    for _ in range(3):
        part = rest.astype(BF).astype(F32)
        rows.append(part)
        rest = rest - part
    gains = jnp.concatenate(rows + [jnp.zeros((10, LANES), F32)], axis=0).astype(BF)
    for piece in (p0, p1, p2, p3):
        piece[BATCH * 192 :, :] = gains
    for copy in copies:
        copy.wait()


def cut_pieces(ids, merged, gain):
    return pl.pallas_call(
        pieces_kernel,
        out_shape=(jax.ShapeDtypeStruct((PIECE, LANES), BF),) * CHAN,
        in_specs=[SM, HBM, HBM],
        out_specs=(VM,) * CHAN,
        scratch_shapes=[pltpu.VMEM((1, 192), F32), pltpu.SemaphoreType.DMA((CHAN, BATCH)), pltpu.SemaphoreType.DMA],
        compiler_params=params(),
        name="cut_pieces",
    )(ids, merged, gain)


COT_ROWS = 9 * 16


def cot_kernel(ids_ref, cot_ref, trunk_ref, send_ref, edges, sems, edge_sems):
    me, place = ids_ref[0], ids_ref[3]
    copies = []
    for d in range(SEQ):
        start = pl.multiple_of(d * CHAN * LANES + me * LANES, LANES)
        copies.append(
            pltpu.make_async_copy(cot_ref.at[:, :, pl.ds(start, LANES)], send_ref.at[d, pl.ds(0, 8)], sems.at[d])
        )
    loads = [
        pltpu.make_async_copy(trunk_ref.at[:, pl.ds(row, 16), :], edges.at[i], edge_sems.at[i])
        for i, row in enumerate((0, 240))
    ]
    for copy in loads + copies:
        copy.start()
    for load in loads:
        load.wait()
    rows = []
    for i, row in enumerate((0, 15)):
        parts = []
        for b in range(BATCH):
            line = edges[i, b].astype(F32)[row : row + 1]
            parts += [line[:, l * LANES : (l + 1) * LANES] for l in range(3)]
        rows.append(jnp.concatenate(parts + [jnp.zeros((4, LANES), F32)], axis=0))
    for d in range(SEQ):
        up = ((place + 1 == d) | (place + 1 == (d ^ 8))).astype(F32)
        down = ((place - 1 == d) | (place - 1 == (d ^ 8))).astype(F32)
        send_ref[d, 8] = (rows[1] * up + rows[0] * down).astype(BF)
    for copy in copies:
        copy.wait()


def cut_cot(ids, cot, trunk):
    return pl.pallas_call(
        cot_kernel,
        out_shape=jax.ShapeDtypeStruct((SEQ, 9, 16, LANES), BF),
        in_specs=[SM, HBM, HBM],
        out_specs=VM,
        scratch_shapes=[pltpu.VMEM((2, BATCH, 16, 384), BF), pltpu.SemaphoreType.DMA((SEQ,)),
                        pltpu.SemaphoreType.DMA((2,))],
        compiler_params=params(),
        cost_estimate=pl.CostEstimate(flops=0, bytes_accessed=5 * 2**20, transcendentals=0),
        name="cut_cot",
    )(ids, cot.reshape(BATCH * 2, 16, -1), trunk)


WIDE, NARROW = 9, 12


def score_kernel(*refs):
    pieces, heads, (bias_ref, of_track_ref, scale_ref) = refs[:4], refs[4:8], refs[8:11]
    wide_hbm, narrow_hbm, raw_ref, small_ref, weights_ref, merged_ref = refs[11:17]
    parts, sems, head_sems, part_sems, out_sems = refs[17:]
    cols_ref = small_ref.at[:, 0:LANES]
    gain_ref = small_ref.at[0:C_OUT, LANES : 2 * LANES]
    copies = []
    for r in range(CHAN):
        rows = pl.ds(r * 192, 192)
        for b in range(BATCH):
            copies.append(
                pltpu.make_async_copy(
                    pieces[r].at[pl.ds(b * 192, 192), :],
                    merged_ref.at[rows, pl.ds(b * LANES, LANES)],
                    sems.at[r, b],
                )
            )
        copies.append(
            pltpu.make_async_copy(pieces[r].at[pl.ds(BATCH * 192, 16), :], parts.at[r], part_sems.at[r])
        )
    loads = [
        pltpu.make_async_copy(heads[r], weights_ref.at[pl.ds(r * 192, 192), :], head_sems.at[r])
        for r in range(CHAN)
    ]
    for copy in copies + loads:
        copy.start()
    track_scale = jnp.zeros((1, TRACKS), F32)
    for h in range(scale_ref.shape[0]):
        track_scale = jnp.where(of_track_ref[...] == h, scale_ref[h], track_scale)
    lines = []
    for rest in (bias_ref[...], track_scale):
        for _ in range(3):
            part = rest.astype(BF).astype(F32)
            lines.append(part)
            rest = rest - part
    lines = jnp.concatenate(lines + [jnp.zeros((10, TRACKS), F32)], axis=0).astype(BF)
    row = lax.broadcasted_iota(jnp.int32, (16, LANES), 0)
    lane = lax.broadcasted_iota(jnp.int32, (16, LANES), 1)
    cols_ref[...] = dot(lines, ((row < 6) & (row // 3 == lane)).astype(BF), (0, 0))
    for copy in copies:
        copy.wait()
    for r in range(CHAN):
        for side in range(2):
            pick = ((row < 6) & (row % 2 == side)).astype(BF)
            size = LANES - side * 64
            start = r * 192 + side * LANES
            gain_ref[start : start + size, :] = dot(parts[r], pick, (0, 0))[:size]
    m32 = merged_ref[...].astype(F32)
    total = jnp.sum(m32 * m32, axis=0, keepdims=True)
    inv = lax.rsqrt(total / C_OUT + epsilon)
    for b in range(BATCH):
        small_ref[8 * b : 8 * b + 8, 2 * LANES : 3 * LANES] = jnp.broadcast_to(
            inv[:, b * LANES : (b + 1) * LANES], (8, LANES)
        )
    normed = (m32 * gain_ref[:, 0:1]).astype(BF)
    for load in loads:
        load.wait()
    stores = [
        pltpu.make_async_copy(small_ref, wide_hbm.at[1, :, pl.ds(0, 3 * LANES)], out_sems.at[0]),
        pltpu.make_async_copy(weights_ref, narrow_hbm.at[0], out_sems.at[1]),
        pltpu.make_async_copy(merged_ref, narrow_hbm.at[1, :, pl.ds(0, BATCH * LANES)], out_sems.at[2]),
    ]
    for store in stores:
        store.start()
    raw_ref[...] = dot(weights_ref[...], normed, (0, 0))
    stores.append(pltpu.make_async_copy(raw_ref, wide_hbm.at[0], out_sems.at[3]))
    stores[-1].start()
    for store in stores:
        store.wait()


def scores(pieces, heads, bias, of_track, scale):
    return pl.pallas_call(
        score_kernel,
        out_shape=(jax.ShapeDtypeStruct((WIDE, TRACKS, BATCH * LANES), F32),
                   jax.ShapeDtypeStruct((NARROW, C_OUT, TRACKS), BF)),
        in_specs=[HBM] * 8 + [VM, VM, SM],
        out_specs=(HBM, HBM),
        scratch_shapes=[
            pltpu.VMEM((TRACKS, BATCH * LANES), F32),
            pltpu.VMEM((TRACKS, 3 * LANES), F32),
            pltpu.VMEM((C_OUT, TRACKS), BF),
            pltpu.VMEM((C_OUT, BATCH * LANES), BF),
            pltpu.VMEM((CHAN, 16, LANES), BF),
            pltpu.SemaphoreType.DMA((CHAN, BATCH)),
            pltpu.SemaphoreType.DMA((CHAN,)),
            pltpu.SemaphoreType.DMA((CHAN,)),
            pltpu.SemaphoreType.DMA((4,)),
        ],
        compiler_params=params(),
        cost_estimate=pl.CostEstimate(flops=6500000000, bytes_accessed=8 * 2**20, transcendentals=0),
        name="scores",
    )(*pieces, *heads, bias, of_track, scale)


HALF = BATCH * 384


def head_kernel(
    ids_ref, valid_ref, wide_hbm, narrow_hbm, cot_ref,
    mine_ref, other_ref, edge_ref, full, raw_ref, small_ref, weights_ref, merged_ref, sems
):
    load_small = pltpu.make_async_copy(wide_hbm.at[1, :, pl.ds(0, 3 * LANES)], small_ref, sems.at[1, 2])
    load_small.start()
    loads = []
    for b in range(BATCH):
        loads.append(
            pltpu.make_async_copy(wide_hbm.at[0, :, pl.ds(b * LANES, LANES)], raw_ref.at[b], sems.at[0, b])
        )
    load_weights = pltpu.make_async_copy(narrow_hbm.at[0], weights_ref, sems.at[1, 0])
    load_merged = pltpu.make_async_copy(narrow_hbm.at[1, :, pl.ds(0, BATCH * LANES)], merged_ref, sems.at[1, 1])
    for copy in loads:
        copy.start()
    load_weights.start()
    load_merged.start()
    load_small.wait()
    me = ids_ref[0]
    first = ids_ref[1]
    half = ids_ref[2]
    scale = small_ref[:, 1:2]
    bias = small_ref[:, 0:1]
    lane = lax.broadcasted_iota(jnp.int32, (1, LANES), 1)
    scaled, coefs = [], []
    for b in range(BATCH):
        cols = slice(b * LANES, (b + 1) * LANES)
        loads[b].wait()
        raw = raw_ref[b]
        inv = small_ref[8 * b : 8 * b + 1, 2 * LANES : 3 * LANES]
        live = (first + lane < valid_ref[b]).astype(F32)
        gate = 0.5 * jnp.tanh(0.5 * (inv * raw + bias)) + 0.5
        cot = cot_ref[:, b * 32 : (b + 1) * 32, :].reshape(TRACKS, LANES).astype(F32)
        d_logits = (cot * scale) * gate
        d_rms = live * jnp.sum(d_logits * raw, axis=0, keepdims=True)
        scaled.append(((inv * live) * d_logits).astype(BF))
        coefs.append(inv * inv * inv * d_rms * (1.0 / C_OUT))
    load_weights.wait()
    load_merged.wait()
    d = dot(weights_ref[...], jnp.concatenate(scaled, axis=1), (1, 0)) * small_ref[0:C_OUT, LANES : LANES + 1]
    for r in range(CHAN):
        rows = slice(r * 192, (r + 1) * 192)
        for b in range(BATCH):
            cols = slice(b * LANES, (b + 1) * LANES)
            full[b, me ^ r] = d[rows, cols] - coefs[b] * merged_ref[rows, cols].astype(F32)
    for b in range(BATCH):
        for g in range(2):
            rows = slice((b * 2 + g) * 192, (b * 2 + g + 1) * 192)
            mine_ref[rows, :] = full[b, 2 * g + half].astype(BF)
            other_ref[rows, :] = full[b, 2 * g + 1 - half].astype(BF)
    start = jnp.where(me == CHAN - 1, LANES - 2, 0)
    row = lax.broadcasted_iota(jnp.int32, (16, LANES), 0)
    col = lax.broadcasted_iota(jnp.int32, (16, LANES), 1) - start
    edge = jnp.zeros((16, C_OUT), F32)
    for b in range(BATCH):
        sel = ((col >= 0) & (col < 2) & (row == b * 2 + col)).astype(BF)
        edge = edge + dot(sel, full[b].reshape(C_OUT, LANES).astype(BF), (1, 1))
    for l in range(6):
        edge_ref[l * 16 : (l + 1) * 16, :] = edge[:, l * LANES : (l + 1) * LANES].astype(BF)


def head(ids, valid, scored, cot):
    return pl.pallas_call(
        head_kernel,
        out_shape=(jax.ShapeDtypeStruct((HALF, LANES), BF),) * 2 + (jax.ShapeDtypeStruct((96, LANES), BF),),
        in_specs=[SM, SM, HBM, HBM, VM],
        out_specs=(VM,) * 3,
        scratch_shapes=[
            pltpu.VMEM((BATCH, CHAN, 192, LANES), F32),
            pltpu.VMEM((BATCH, TRACKS, LANES), F32),
            pltpu.VMEM((TRACKS, 3 * LANES), F32),
            pltpu.VMEM((C_OUT, TRACKS), BF),
            pltpu.VMEM((C_OUT, BATCH * LANES), BF),
            pltpu.SemaphoreType.DMA((2, BATCH)),
        ],
        compiler_params=params(48 * MIB),
        name="head",
    )(ids, valid, *scored, cot)


PAIR = 2


def rows_kernel(ids_ref, own_ref, far_ref, got_ref, tr_ref, trx_ref, edges, trunks, sems, trunk_sems):
    place = ids_ref[3]
    copies = [
        pltpu.make_async_copy(ref, trunks.at[q], trunk_sems.at[q]) for q, ref in enumerate((own_ref, far_ref))
    ]
    for q in range(PAIR):
        for i, step in enumerate((-1, 1)):
            source = jnp.clip((place ^ (8 * q)) + step, 0, SEQ - 1)
            copies.append(
                pltpu.make_async_copy(got_ref.at[source, pl.ds(128, 16)], edges.at[q, i], sems.at[q, i])
            )
    for copy in copies:
        copy.start()
    for copy in copies:
        copy.wait()
    row = lax.broadcasted_iota(jnp.int32, (256, 384), 0)
    ends = [jnp.zeros((LANES, 384), F32) for _ in range(KERNEL)]
    at = lax.broadcasted_iota(jnp.int32, (LANES, 384), 0)
    for q in range(PAIR):
        before = edges[q, 0].astype(F32) * ((place ^ (8 * q)) > 0).astype(F32)
        after = edges[q, 1].astype(F32) * ((place ^ (8 * q)) < SEQ - 1).astype(F32)
        for b in range(BATCH):
            t = trunks[q, b].astype(F32)
            rows = slice(b * 256, (b + 1) * 256)
            tr_ref[q, rows, 0:384] = jnp.where(row == 0, 0.0, pltpu.roll(t, 1, 0)).astype(BF)
            tr_ref[q, rows, 384:768] = trunks[q, b]
            tr_ref[q, rows, 768:1152] = jnp.where(row == 255, 0.0, pltpu.roll(t, 255, 0)).astype(BF)
            base = (q * BATCH + b) * 5
            first, last = (
                jnp.concatenate([x[b * 3 + l : b * 3 + l + 1] for l in range(3)], axis=1)
                for x in (before, after)
            )
            for column, tap, x in (
                (0, 1, t[127:128]), (0, 3, t[128:129]), (1, 1, t[255:256]), (1, 3, last),
                (2, 4, last), (3, 0, first), (4, 1, first),
            ):
                ends[tap] = jnp.where(at == base + column, x, ends[tap])
    for k in range(KERNEL):
        trx_ref[:, k * 384 : (k + 1) * 384] = ends[k].astype(BF)


def trunk_rows(ids, own, far, got):
    return pl.pallas_call(
        rows_kernel,
        out_shape=(jax.ShapeDtypeStruct((PAIR, 1024, 1152), BF),
                   jax.ShapeDtypeStruct((LANES, KERNEL * 384), BF)),
        in_specs=[SM, HBM, HBM, ANY],
        out_specs=(VM, VM),
        scratch_shapes=[pltpu.VMEM((PAIR, 2, 16, LANES), BF), pltpu.VMEM((PAIR, BATCH, 256, 384), BF),
                        pltpu.SemaphoreType.DMA((PAIR, 2)), pltpu.SemaphoreType.DMA((PAIR,))],
        compiler_params=params(30 * MIB),
        cost_estimate=pl.CostEstimate(flops=10**7, bytes_accessed=8 * 2**20, transcendentals=0),
        name="trunk_rows",
    )(ids, own, far, got)


ROWS = 368
KEPT = 18


def weight_kernel(ids_ref, *refs):
    pieces, (tr_ref, trx_ref, out_hbm, own_ref, full, out_ref, sems, own_sem, out_sems) = refs[:8], refs[8:]
    me = ids_ref[0]
    copies = []
    for q in range(PAIR):
        for r in range(CHAN):
            lanes = pl.ds(pl.multiple_of((me ^ r) * LANES, LANES), LANES)
            copies.append(pltpu.make_async_copy(pieces[q * CHAN + r], full.at[q, :, lanes], sems.at[q, r]))
    for copy in copies:
        copy.start()
    keep = pltpu.make_async_copy(full.at[0], own_ref.at[0], own_sem)
    p = lax.broadcasted_iota(jnp.int32, (256, 256), 0)
    q_ = lax.broadcasted_iota(jnp.int32, (256, 256), 1)
    even = (q_ < 128) & (p // 2 == q_)
    odd = (q_ >= 128) & ((p + 1) // 2 == q_ - 128)
    pick = (even | odd).astype(BF)
    last = jnp.zeros((384, LANES), F32)
    p1 = lax.broadcasted_iota(jnp.int32, (LANES, LANES), 0)
    q1 = lax.broadcasted_iota(jnp.int32, (LANES, LANES), 1)
    g_even = jnp.zeros((384, 1152), F32)
    g_odd = jnp.zeros((384, 768), F32)
    for q in range(PAIR):
        for copy in copies[q * CHAN : (q + 1) * CHAN]:
            copy.wait()
        if q == 0:
            keep.start()
        evens, odds = [], []
        for b in range(BATCH):
            for h in range(2):
                block = full[q, b * 384 : (b + 1) * 384, h * 256 : (h + 1) * 256]
                e = dot(block, pick, (1, 0)).astype(BF)
                evens.append(e[:, :128])
                odds.append(e[:, 128:])
                place = q1 - (q * BATCH + b) * 5
                if h == 0:
                    sel = (((p1 < 2) & (place == 3)) | ((p1 == 0) & (place == 4))).astype(BF)
                    last = last + dot(block[:, :128], sel, (1, 0))
                    sel = (p1 == 127) & (place == 0)
                else:
                    sel = ((p1 == 127) & (place == 1)) | ((p1 >= 126) & (place == 2))
                last = last + dot(block[:, 128:], sel.astype(BF), (1, 0))
        g_even = g_even + dot(jnp.concatenate(evens, axis=1), tr_ref[q], (1, 0))
        g_odd = g_odd + dot(jnp.concatenate(odds, axis=1), tr_ref[q, :, :768], (1, 0))
    last = last.astype(BF)
    side = [dot(last, trx_ref[:, k * 384 : (k + 1) * 384], (1, 0)) for k in range(KERNEL)]
    pad = jnp.zeros((ROWS - 360, LANES), F32)
    taps = (g_even[:, :384], g_odd[:, :384], g_even[:, 384:768], g_odd[:, 384:], g_even[:, 768:])
    taps = [tap + term for tap, term in zip(taps, side)]
    stores = []
    for s in range(16):
        blocks = []
        for l in range(3):
            for tap in taps:
                blocks.append(tap[s * 24 : (s + 1) * 24, l * LANES : (l + 1) * LANES])
        out_ref[s] = jnp.concatenate(blocks + [pad], axis=0).astype(BF)
        if s % 4 == 3:
            part = pl.ds(s - 3, 4)
            stores.append(pltpu.make_async_copy(out_ref.at[part], out_hbm.at[part], out_sems.at[s // 4]))
            stores[-1].start()
    for store in stores:
        store.wait()
    keep.wait()


def weight_grad(ids, pieces, tr, trx):
    return pl.pallas_call(
        weight_kernel,
        out_shape=(jax.ShapeDtypeStruct((16, ROWS, LANES), BF),
                   jax.ShapeDtypeStruct((KEPT, HALF, 512), BF)),
        in_specs=[SM] + [ANY] * 8 + [VM] * 2,
        out_specs=(HBM, HBM),
        scratch_shapes=[pltpu.VMEM((PAIR, HALF, 512), BF), pltpu.VMEM((16, ROWS, LANES), BF),
                        pltpu.SemaphoreType.DMA((PAIR, CHAN)), pltpu.SemaphoreType.DMA,
                        pltpu.SemaphoreType.DMA((4,))],
        compiler_params=params(40 * MIB),
        cost_estimate=pl.CostEstimate(flops=4 * 10**9, bytes_accessed=10 * 2**20, transcendentals=0),
        name="weight_grad",
    )(ids, *pieces, tr, trx)


def trunk_kernel(ids_ref, *refs):
    mine, other = refs[0], refs[1:5]
    conv_hbm, out_ref, skip_ref, full, sums, rims, conv_ref, sems, mine_sems, other_sems, skip_sem, conv_sem = refs[5:]
    me = ids_ref[0]
    half = ids_ref[2]
    skip = pltpu.make_async_copy(full.at[:, me // 2, me % 2], skip_ref, skip_sem)
    copies = []
    for b in range(BATCH):
        for g in range(2):
            rows = pl.ds((b * 2 + g) * 192, 192)
            copies.append(pltpu.make_async_copy(mine.at[0, rows, :], full.at[b, g, half], mine_sems.at[b, g]))
            for r in range(CHAN):
                lanes = pl.ds(pl.multiple_of((me ^ r) * LANES, LANES), LANES)
                copies.append(
                    pltpu.make_async_copy(
                        other[r].at[rows, :], full.at[b, g, 1 - half, :, lanes], other_sems.at[r, b, g]
                    )
                )
    for r in range(CHAN):
        copies.append(pltpu.make_async_copy(other[r].at[pl.ds(HALF, 96), :], rims.at[r], sems.at[r]))
    load = pltpu.make_async_copy(conv_hbm, conv_ref, conv_sem)
    for copy in copies + [load]:
        copy.start()
    row = lax.broadcasted_iota(jnp.int32, (2 * EXT, 512), 0)
    p = lax.broadcasted_iota(jnp.int32, (2 * EXT, 512), 1)
    lo = jnp.where(row < EXT, 2 * (row - 8), 2 * (row - EXT - 8) - 1)
    pick = ((p == lo) | (p == lo + 1)).astype(BF)
    col = lax.broadcasted_iota(jnp.int32, (2 * EXT, 32), 1)
    lo = lo[:, :32]
    for copy in copies:
        copy.wait()
    skip.start()
    rim = jnp.concatenate(
        [jnp.concatenate([rims[x, l * 16 : (l + 1) * 16, :] for l in range(6)], axis=1) for x in (me, me ^ 3)],
        axis=0,
    )
    for b in range(BATCH):
        offset = col % 16 - 2 * b
        rim_ok = (offset >= 0) & (offset < 2)
        rim_pos = jnp.where(col < 16, offset - 2, 512 + offset)
        pick_r = (rim_ok & ((rim_pos == lo) | (rim_pos == lo + 1))).astype(BF)
        e = (dot(pick, full[b].reshape(C_OUT, 512), (1, 1)) + dot(pick_r, rim, (1, 0))).astype(BF)
        sums[pl.ds(b * EXT, EXT), :C_OUT] = e[:EXT]
        sums[pl.ds(b * EXT, EXT), C_OUT:] = e[EXT:]
    load.wait()
    even, odd = sums[:, :C_OUT], sums[:, C_OUT:]
    up = dot(even, conv_ref[0], (1, 1)) + dot(odd, conv_ref[1], (1, 1))
    here = dot(even, conv_ref[2], (1, 1)) + dot(odd, conv_ref[3], (1, 1))
    down = dot(even, conv_ref[4], (1, 1))
    for b in range(BATCH):
        o = b * EXT + 8
        total = up[o + 1 : o + 257] + here[o : o + 256] + down[o - 1 : o + 255]
        out_ref[b] = total.astype(BF)
    skip.wait()


EXT = 272


def trunk_grad(ids, mine, other, conv_w):
    return pl.pallas_call(
        trunk_kernel,
        out_shape=(jax.ShapeDtypeStruct((BATCH, 256, 384), BF), jax.ShapeDtypeStruct((BATCH, 192, 512), BF)),
        in_specs=[SM] + [HBM] * 6,
        out_specs=(VM, HBM),
        scratch_shapes=[pltpu.VMEM((BATCH, 2, 2, 192, 512), BF), pltpu.VMEM((BATCH * EXT, 2 * C_OUT), BF),
                        pltpu.VMEM((CHAN, 96, LANES), BF), pltpu.VMEM((KERNEL, 384, C_OUT), BF),
                        pltpu.SemaphoreType.DMA((CHAN,)), pltpu.SemaphoreType.DMA((BATCH, 2)),
                        pltpu.SemaphoreType.DMA((CHAN, BATCH, 2)), pltpu.SemaphoreType.DMA,
                        pltpu.SemaphoreType.DMA],
        compiler_params=params(),
        cost_estimate=pl.CostEstimate(flops=8 * 10**9, bytes_accessed=16 * 2**20, transcendentals=0),
        name="trunk_grad",
    )(ids, mine, *other, conv_w)


def sum_kernel(scale, in_ref, out_ref):
    total = in_ref[0].astype(F32)
    for s in range(1, in_ref.shape[0]):
        total = total + in_ref[s].astype(F32)
    total = total * scale
    for l in range(3):
        for k in range(KERNEL):
            start = l * 120 + k * 24
            out_ref[k, :, l * LANES : (l + 1) * LANES] = total[start : start + 24]


def sum_weights(terms, scale):
    return pl.pallas_call(
        functools.partial(sum_kernel, scale),
        out_shape=jax.ShapeDtypeStruct((KERNEL, 24, 384), F32),
        in_specs=[VM],
        out_specs=VM,
        compiler_params=params(30 * MIB),
        name="sum_weights",
    )(terms)


def flip(x, r):
    return lax.ppermute(x, "chan", [(i, i ^ r) for i in range(CHAN)])


def partner(x):
    return lax.ppermute(x, "seq", [(i, i ^ 8) for i in range(SEQ)])


def partner_far(x):
    pairs = [(s * CHAN + c, (s ^ 8) * CHAN + (c ^ 2)) for s in range(SEQ) for c in range(CHAN)]
    return lax.ppermute(x, ("seq", "chan"), pairs)


def rim(x):
    up = [(s * CHAN + 3, (s + 1) * CHAN) for s in range(SEQ - 1)]
    down = [(s * CHAN, (s - 1) * CHAN + 3) for s in range(1, SEQ)]
    return lax.ppermute(x, ("seq", "chan"), up + down)


def across(x):
    pairs = [(s * CHAN + c, (s ^ 16) * CHAN + (c ^ 2)) for s in range(SEQ) for c in range(CHAN)]
    return lax.ppermute(x, ("seq", "chan"), pairs)


def local(
    trunk, merged, conv_w, norm_gain, head_w, head_bias, head_scale, head_of_track, valid_len, cot
):
    me = lax.axis_index("chan").astype(jnp.int32)
    place = lax.axis_index("seq").astype(jnp.int32)
    half = (place // 8) % 2
    ids = jnp.stack([me, place * 512 + me * LANES, half, place])
    trunk_far = partner(trunk)
    p0, p1, p2, p3 = cut_pieces(ids, merged, norm_gain[None])
    p1, p2, p3, cot = lax.optimization_barrier((p1, p2, p3, cot))
    send = cut_cot(ids, cot, trunk)
    p1, p2, p3 = flip(p1, 1), flip(p2, 2), flip(p3, 3)
    send, trunk, head_w = lax.optimization_barrier((send, trunk, head_w))
    far_head = across(head_w)
    near_head = flip(head_w, 1)
    send, p1, p2 = lax.optimization_barrier((send, p1, p2))
    p3, trunk_far, far_head = lax.optimization_barrier((p3, trunk_far, far_head))
    got = lax.all_to_all(send, "seq", 0, 0, tiled=True).reshape(SEQ, COT_ROWS, LANES)
    pieces = (p0, p1, p2, p3)
    heads = (head_w, near_head, far_head, flip(far_head, 1))

    scored = scores(pieces, heads, head_bias[None], head_of_track[None], head_scale)
    mine, other, edge = head(ids, valid_len, scored, got)
    trunk, _ = lax.optimization_barrier((trunk, mine))
    tr, trx = trunk_rows(ids, trunk, trunk_far, got)

    mine_far, other_x, other_far_x = flip(mine, 2), partner(other), partner_far(other)
    other = jnp.concatenate([other, rim(edge)])
    mine_far, other_x, other_far_x, other, tr, trx = lax.optimization_barrier(
        (mine_far, other_x, other_far_x, other, tr, trx)
    )
    mine_all = (mine, flip(mine, 1), mine_far, flip(mine_far, 1))
    blocks = mine_all + (other_x, flip(other_x, 1), other_far_x, flip(other_far_x, 1))
    terms, mine_rows = weight_grad(ids, blocks, tr, trx)
    other_late, _ = lax.optimization_barrier((other, mine_far))
    other_far = flip(other_late, 2)
    other_all = (other, flip(other, 1), other_far, flip(other_far, 1))
    groups = [[s for s in range(SEQ) if (s // 8) % 2 == u] for u in range(2)]
    summed = lax.all_to_all(terms, "seq", 0, 0, tiled=True, axis_index_groups=groups)
    d_trunk, d_skip = trunk_grad(ids, mine_rows, other_all, conv_w)
    grad_scale = 1.0 / math.sqrt(BATCH * 512 * SEQ)
    d_conv_w = sum_weights(summed, grad_scale)
    return (d_trunk, d_skip, d_conv_w)


def solution(mesh):
    placed = (
        P(None, "seq", "chan"),
        P(None, "chan", "seq"),
        P(None, "chan", None),
        P("chan"),
        P("chan", None),
        P(),
        P(),
        P(),
        P(),
        P(None, "seq", None),
    )
    return jax.shard_map(
        local,
        mesh=mesh,
        in_specs=placed,
        out_specs=(P(None, "seq", "chan"), P(None, "chan", "seq"), P(None, "seq", "chan")),
        check_vma=False,
    )
```

```python
import functools
import math

import jax
import jax.numpy as jnp
from jax import lax
from jax.experimental import pallas as pl
from jax.experimental.pallas import tpu as pltpu
from jax.sharding import PartitionSpec as P

BATCH = 4
C_OUT = 768
TRACKS = 1024
KERNEL = 5
SEQ = 32
CHAN = 4
LANES = 128
epsilon = 1e-06

BF = jnp.bfloat16
F32 = jnp.float32
MIB = 1024 * 1024


def params(limit=62 * MIB):
    return pltpu.CompilerParams(vmem_limit_bytes=limit)


def dot(a, b, contract):
    return lax.dot_general(a, b, ((contract[:1], contract[1:]), ((), ())), preferred_element_type=F32)


ANY = pl.BlockSpec(memory_space=pl.ANY)
VM = pl.BlockSpec(memory_space=pltpu.VMEM)
HBM = pl.BlockSpec(memory_space=pltpu.HBM)
SM = pl.BlockSpec(memory_space=pltpu.SMEM)


PIECE = BATCH * 192 + 16


def pieces_kernel(ids_ref, merged_ref, gain_ref, p0, p1, p2, p3, line, sems, line_sem):
    me = ids_ref[0]
    load = pltpu.make_async_copy(gain_ref, line, line_sem)
    load.start()
    copies = []
    for r, piece in enumerate((p0, p1, p2, p3)):
        lanes = pl.ds(pl.multiple_of((me ^ r) * LANES, LANES), LANES)
        for b in range(BATCH):
            rows = pl.ds(b * 192, 192)
            copies.append(pltpu.make_async_copy(merged_ref.at[b, :, lanes], piece.at[rows, :], sems.at[r, b]))
    for copy in copies:
        copy.start()
    load.wait()
    tail = jnp.concatenate([line[:, LANES:], jnp.zeros((1, 2 * LANES - 192), F32)], axis=1)
    rest = jnp.concatenate([line[:, :LANES], tail], axis=0)
    rows = []
    for _ in range(3):
        part = rest.astype(BF).astype(F32)
        rows.append(part)
        rest = rest - part
    gains = jnp.concatenate(rows + [jnp.zeros((10, LANES), F32)], axis=0).astype(BF)
    for piece in (p0, p1, p2, p3):
        piece[BATCH * 192 :, :] = gains
    for copy in copies:
        copy.wait()


def cut_pieces(ids, merged, gain):
    return pl.pallas_call(
        pieces_kernel,
        out_shape=(jax.ShapeDtypeStruct((PIECE, LANES), BF),) * CHAN,
        in_specs=[SM, HBM, HBM],
        out_specs=(VM,) * CHAN,
        scratch_shapes=[pltpu.VMEM((1, 192), F32), pltpu.SemaphoreType.DMA((CHAN, BATCH)), pltpu.SemaphoreType.DMA],
        compiler_params=params(),
        name="cut_pieces",
    )(ids, merged, gain)


COT_ROWS = 9 * 16


def cot_kernel(ids_ref, cot_ref, trunk_ref, send_ref, edges, sems, edge_sems):
    me, place = ids_ref[0], ids_ref[3]
    copies = []
    for d in range(SEQ):
        start = pl.multiple_of(d * CHAN * LANES + me * LANES, LANES)
        copies.append(
            pltpu.make_async_copy(cot_ref.at[:, :, pl.ds(start, LANES)], send_ref.at[d, pl.ds(0, 8)], sems.at[d])
        )
    loads = [
        pltpu.make_async_copy(trunk_ref.at[:, pl.ds(row, 16), :], edges.at[i], edge_sems.at[i])
        for i, row in enumerate((0, 240))
    ]
    for copy in loads + copies:
        copy.start()
    for load in loads:
        load.wait()
    rows = []
    for i, row in enumerate((0, 15)):
        parts = []
        for b in range(BATCH):
            line = edges[i, b].astype(F32)[row : row + 1]
            parts += [line[:, l * LANES : (l + 1) * LANES] for l in range(3)]
        rows.append(jnp.concatenate(parts + [jnp.zeros((4, LANES), F32)], axis=0))
    for d in range(SEQ):
        up = ((place + 1 == d) | (place + 1 == (d ^ 8))).astype(F32)
        down = ((place - 1 == d) | (place - 1 == (d ^ 8))).astype(F32)
        send_ref[d, 8] = (rows[1] * up + rows[0] * down).astype(BF)
    for copy in copies:
        copy.wait()


def cut_cot(ids, cot, trunk):
    return pl.pallas_call(
        cot_kernel,
        out_shape=jax.ShapeDtypeStruct((SEQ, 9, 16, LANES), BF),
        in_specs=[SM, HBM, HBM],
        out_specs=VM,
        scratch_shapes=[pltpu.VMEM((2, BATCH, 16, 384), BF), pltpu.SemaphoreType.DMA((SEQ,)),
                        pltpu.SemaphoreType.DMA((2,))],
        compiler_params=params(),
        cost_estimate=pl.CostEstimate(flops=0, bytes_accessed=5 * 2**20, transcendentals=0),
        name="cut_cot",
    )(ids, cot.reshape(BATCH * 2, 16, -1), trunk)


WIDE, NARROW = 9, 12


def score_kernel(*refs):
    pieces, heads, (bias_ref, of_track_ref, scale_ref) = refs[:4], refs[4:8], refs[8:11]
    wide_hbm, narrow_hbm, raw_ref, cols_ref, inv_ref, gain_ref, weights_ref, merged_ref = refs[11:19]
    parts, sems, head_sems, part_sems, out_sems = refs[19:]
    copies = []
    for r in range(CHAN):
        rows = pl.ds(r * 192, 192)
        for b in range(BATCH):
            copies.append(
                pltpu.make_async_copy(
                    pieces[r].at[pl.ds(b * 192, 192), :],
                    merged_ref.at[rows, pl.ds(b * LANES, LANES)],
                    sems.at[r, b],
                )
            )
        copies.append(
            pltpu.make_async_copy(pieces[r].at[pl.ds(BATCH * 192, 16), :], parts.at[r], part_sems.at[r])
        )
    loads = [
        pltpu.make_async_copy(heads[r], weights_ref.at[pl.ds(r * 192, 192), :], head_sems.at[r])
        for r in range(CHAN)
    ]
    for copy in copies + loads:
        copy.start()
    track_scale = jnp.zeros((1, TRACKS), F32)
    for h in range(scale_ref.shape[0]):
        track_scale = jnp.where(of_track_ref[...] == h, scale_ref[h], track_scale)
    lines = []
    for rest in (bias_ref[...], track_scale):
        for _ in range(3):
            part = rest.astype(BF).astype(F32)
            lines.append(part)
            rest = rest - part
    lines = jnp.concatenate(lines + [jnp.zeros((10, TRACKS), F32)], axis=0).astype(BF)
    row = lax.broadcasted_iota(jnp.int32, (16, LANES), 0)
    lane = lax.broadcasted_iota(jnp.int32, (16, LANES), 1)
    cols_ref[...] = dot(lines, ((row < 6) & (row // 3 == lane)).astype(BF), (0, 0))
    for copy in copies:
        copy.wait()
    for r in range(CHAN):
        for side in range(2):
            pick = ((row < 6) & (row % 2 == side)).astype(BF)
            size = LANES - side * 64
            start = r * 192 + side * LANES
            gain_ref[start : start + size, :] = dot(parts[r], pick, (0, 0))[:size]
    m32 = merged_ref[...].astype(F32)
    total = jnp.sum(m32 * m32, axis=0, keepdims=True)
    inv = lax.rsqrt(total / C_OUT + epsilon)
    for b in range(BATCH):
        inv_ref[8 * b : 8 * b + 8, :] = jnp.broadcast_to(inv[:, b * LANES : (b + 1) * LANES], (8, LANES))
    lane = lax.broadcasted_iota(jnp.int32, (C_OUT, LANES), 1)
    cols_ref[0:C_OUT, :] = jnp.where(lane == 2, gain_ref[...], cols_ref[0:C_OUT, :])
    normed = (m32 * gain_ref[:, 0:1]).astype(BF)
    for load in loads:
        load.wait()
    stores = [
        pltpu.make_async_copy(cols_ref, wide_hbm.at[1, :, pl.ds(0, LANES)], out_sems.at[0]),
        pltpu.make_async_copy(inv_ref, wide_hbm.at[1, pl.ds(0, 32), pl.ds(LANES, LANES)], out_sems.at[4]),
        pltpu.make_async_copy(weights_ref, narrow_hbm.at[0], out_sems.at[1]),
        pltpu.make_async_copy(merged_ref, narrow_hbm.at[1, :, pl.ds(0, BATCH * LANES)], out_sems.at[2]),
    ]
    for store in stores:
        store.start()
    raw_ref[...] = dot(weights_ref[...], normed, (0, 0))
    stores.append(pltpu.make_async_copy(raw_ref, wide_hbm.at[0], out_sems.at[3]))
    stores[-1].start()
    for store in stores:
        store.wait()


def scores(pieces, heads, bias, of_track, scale):
    return pl.pallas_call(
        score_kernel,
        out_shape=(jax.ShapeDtypeStruct((WIDE, TRACKS, BATCH * LANES), F32),
                   jax.ShapeDtypeStruct((NARROW, C_OUT, TRACKS), BF)),
        in_specs=[HBM] * 8 + [VM, VM, SM],
        out_specs=(HBM, HBM),
        scratch_shapes=[
            pltpu.VMEM((TRACKS, BATCH * LANES), F32),
            pltpu.VMEM((TRACKS, LANES), F32),
            pltpu.VMEM((32, LANES), F32),
            pltpu.VMEM((C_OUT, LANES), F32),
            pltpu.VMEM((C_OUT, TRACKS), BF),
            pltpu.VMEM((C_OUT, BATCH * LANES), BF),
            pltpu.VMEM((CHAN, 16, LANES), BF),
            pltpu.SemaphoreType.DMA((CHAN, BATCH)),
            pltpu.SemaphoreType.DMA((CHAN,)),
            pltpu.SemaphoreType.DMA((CHAN,)),
            pltpu.SemaphoreType.DMA((5,)),
        ],
        compiler_params=params(),
        cost_estimate=pl.CostEstimate(flops=6500000000, bytes_accessed=8 * 2**20, transcendentals=0),
        name="scores",
    )(*pieces, *heads, bias, of_track, scale)


HALF = BATCH * 384


def head_kernel(
    ids_ref, valid_ref, wide_hbm, narrow_hbm, cot_ref,
    mine_ref, other_ref, edge_ref, full, raw_ref, cols_ref, inv_ref, weights_ref, merged_ref, sems
):
    load_cols = pltpu.make_async_copy(wide_hbm.at[1, :, pl.ds(0, LANES)], cols_ref, sems.at[1, 2])
    load_inv = pltpu.make_async_copy(wide_hbm.at[1, pl.ds(0, 32), pl.ds(LANES, LANES)], inv_ref, sems.at[1, 3])
    load_cols.start()
    load_inv.start()
    loads = []
    for b in range(BATCH):
        loads.append(
            pltpu.make_async_copy(wide_hbm.at[0, :, pl.ds(b * LANES, LANES)], raw_ref.at[b], sems.at[0, b])
        )
    load_weights = pltpu.make_async_copy(narrow_hbm.at[0], weights_ref, sems.at[1, 0])
    load_merged = pltpu.make_async_copy(narrow_hbm.at[1, :, pl.ds(0, BATCH * LANES)], merged_ref, sems.at[1, 1])
    for copy in loads:
        copy.start()
    load_weights.start()
    load_merged.start()
    load_cols.wait()
    load_inv.wait()
    me = ids_ref[0]
    first = ids_ref[1]
    half = ids_ref[2]
    scale = cols_ref[:, 1:2]
    bias = cols_ref[:, 0:1]
    lane = lax.broadcasted_iota(jnp.int32, (1, LANES), 1)
    scaled, coefs = [], []
    for b in range(BATCH):
        cols = slice(b * LANES, (b + 1) * LANES)
        loads[b].wait()
        raw = raw_ref[b]
        inv = inv_ref[8 * b : 8 * b + 1, :]
        live = (first + lane < valid_ref[b]).astype(F32)
        gate = 0.5 * jnp.tanh(0.5 * (inv * raw + bias)) + 0.5
        cot = cot_ref[:, b * 32 : (b + 1) * 32, :].reshape(TRACKS, LANES).astype(F32)
        d_logits = (cot * scale) * gate
        d_rms = live * jnp.sum(d_logits * raw, axis=0, keepdims=True)
        scaled.append(((inv * live) * d_logits).astype(BF))
        coefs.append(inv * inv * inv * d_rms * (1.0 / C_OUT))
    load_weights.wait()
    load_merged.wait()
    d = dot(weights_ref[...], jnp.concatenate(scaled, axis=1), (1, 0)) * cols_ref[0:C_OUT, 2:3]
    for r in range(CHAN):
        rows = slice(r * 192, (r + 1) * 192)
        for b in range(BATCH):
            cols = slice(b * LANES, (b + 1) * LANES)
            full[b, me ^ r] = d[rows, cols] - coefs[b] * merged_ref[rows, cols].astype(F32)
    for b in range(BATCH):
        for g in range(2):
            rows = slice((b * 2 + g) * 192, (b * 2 + g + 1) * 192)
            mine_ref[rows, :] = full[b, 2 * g + half].astype(BF)
            other_ref[rows, :] = full[b, 2 * g + 1 - half].astype(BF)
    start = jnp.where(me == CHAN - 1, LANES - 2, 0)
    row = lax.broadcasted_iota(jnp.int32, (16, LANES), 0)
    col = lax.broadcasted_iota(jnp.int32, (16, LANES), 1) - start
    edge = jnp.zeros((16, C_OUT), F32)
    for b in range(BATCH):
        sel = ((col >= 0) & (col < 2) & (row == b * 2 + col)).astype(BF)
        edge = edge + dot(sel, full[b].reshape(C_OUT, LANES).astype(BF), (1, 1))
    for l in range(6):
        edge_ref[l * 16 : (l + 1) * 16, :] = edge[:, l * LANES : (l + 1) * LANES].astype(BF)


def head(ids, valid, scored, cot):
    return pl.pallas_call(
        head_kernel,
        out_shape=(jax.ShapeDtypeStruct((HALF, LANES), BF),) * 2 + (jax.ShapeDtypeStruct((96, LANES), BF),),
        in_specs=[SM, SM, HBM, HBM, VM],
        out_specs=(VM,) * 3,
        scratch_shapes=[
            pltpu.VMEM((BATCH, CHAN, 192, LANES), F32),
            pltpu.VMEM((BATCH, TRACKS, LANES), F32),
            pltpu.VMEM((TRACKS, LANES), F32),
            pltpu.VMEM((32, LANES), F32),
            pltpu.VMEM((C_OUT, TRACKS), BF),
            pltpu.VMEM((C_OUT, BATCH * LANES), BF),
            pltpu.SemaphoreType.DMA((2, BATCH)),
        ],
        compiler_params=params(48 * MIB),
        name="head",
    )(ids, valid, *scored, cot)


PAIR = 2


def rows_kernel(ids_ref, own_ref, far_ref, got_ref, tr_ref, trx_ref, edges, trunks, sems, trunk_sems):
    place = ids_ref[3]
    copies = [
        pltpu.make_async_copy(ref, trunks.at[q], trunk_sems.at[q]) for q, ref in enumerate((own_ref, far_ref))
    ]
    for q in range(PAIR):
        for i, step in enumerate((-1, 1)):
            source = jnp.clip((place ^ (8 * q)) + step, 0, SEQ - 1)
            copies.append(
                pltpu.make_async_copy(got_ref.at[source, pl.ds(128, 16)], edges.at[q, i], sems.at[q, i])
            )
    for copy in copies:
        copy.start()
    for copy in copies:
        copy.wait()
    row = lax.broadcasted_iota(jnp.int32, (256, 384), 0)
    ends = [jnp.zeros((LANES, 384), F32) for _ in range(KERNEL)]
    at = lax.broadcasted_iota(jnp.int32, (LANES, 384), 0)
    for q in range(PAIR):
        before = edges[q, 0].astype(F32) * ((place ^ (8 * q)) > 0).astype(F32)
        after = edges[q, 1].astype(F32) * ((place ^ (8 * q)) < SEQ - 1).astype(F32)
        for b in range(BATCH):
            t = trunks[q, b].astype(F32)
            rows = slice(b * 256, (b + 1) * 256)
            tr_ref[q, rows, 0:384] = jnp.where(row == 0, 0.0, pltpu.roll(t, 1, 0)).astype(BF)
            tr_ref[q, rows, 384:768] = trunks[q, b]
            tr_ref[q, rows, 768:1152] = jnp.where(row == 255, 0.0, pltpu.roll(t, 255, 0)).astype(BF)
            base = (q * BATCH + b) * 5
            first, last = (
                jnp.concatenate([x[b * 3 + l : b * 3 + l + 1] for l in range(3)], axis=1)
                for x in (before, after)
            )
            for column, tap, x in (
                (0, 1, t[127:128]), (0, 3, t[128:129]), (1, 1, t[255:256]), (1, 3, last),
                (2, 4, last), (3, 0, first), (4, 1, first),
            ):
                ends[tap] = jnp.where(at == base + column, x, ends[tap])
    for k in range(KERNEL):
        trx_ref[:, k * 384 : (k + 1) * 384] = ends[k].astype(BF)


def trunk_rows(ids, own, far, got):
    return pl.pallas_call(
        rows_kernel,
        out_shape=(jax.ShapeDtypeStruct((PAIR, 1024, 1152), BF),
                   jax.ShapeDtypeStruct((LANES, KERNEL * 384), BF)),
        in_specs=[SM, HBM, HBM, ANY],
        out_specs=(VM, VM),
        scratch_shapes=[pltpu.VMEM((PAIR, 2, 16, LANES), BF), pltpu.VMEM((PAIR, BATCH, 256, 384), BF),
                        pltpu.SemaphoreType.DMA((PAIR, 2)), pltpu.SemaphoreType.DMA((PAIR,))],
        compiler_params=params(30 * MIB),
        cost_estimate=pl.CostEstimate(flops=10**7, bytes_accessed=8 * 2**20, transcendentals=0),
        name="trunk_rows",
    )(ids, own, far, got)


ROWS = 368
KEPT = 18


def weight_kernel(ids_ref, *refs):
    pieces, (tr_ref, trx_ref, out_hbm, own_ref, full, out_ref, sems, own_sem, out_sems) = refs[:8], refs[8:]
    me = ids_ref[0]
    copies = []
    for q in range(PAIR):
        for r in range(CHAN):
            lanes = pl.ds(pl.multiple_of((me ^ r) * LANES, LANES), LANES)
            copies.append(pltpu.make_async_copy(pieces[q * CHAN + r], full.at[q, :, lanes], sems.at[q, r]))
    for copy in copies:
        copy.start()
    keep = pltpu.make_async_copy(full.at[0], own_ref.at[0], own_sem)
    p = lax.broadcasted_iota(jnp.int32, (256, 256), 0)
    q_ = lax.broadcasted_iota(jnp.int32, (256, 256), 1)
    even = (q_ < 128) & (p // 2 == q_)
    odd = (q_ >= 128) & ((p + 1) // 2 == q_ - 128)
    pick = (even | odd).astype(BF)
    last = jnp.zeros((384, LANES), F32)
    p1 = lax.broadcasted_iota(jnp.int32, (LANES, LANES), 0)
    q1 = lax.broadcasted_iota(jnp.int32, (LANES, LANES), 1)
    g_even = jnp.zeros((384, 1152), F32)
    g_odd = jnp.zeros((384, 768), F32)
    for q in range(PAIR):
        for copy in copies[q * CHAN : (q + 1) * CHAN]:
            copy.wait()
        if q == 0:
            keep.start()
        evens, odds = [], []
        for b in range(BATCH):
            for h in range(2):
                block = full[q, b * 384 : (b + 1) * 384, h * 256 : (h + 1) * 256]
                e = dot(block, pick, (1, 0)).astype(BF)
                evens.append(e[:, :128])
                odds.append(e[:, 128:])
                place = q1 - (q * BATCH + b) * 5
                if h == 0:
                    sel = (((p1 < 2) & (place == 3)) | ((p1 == 0) & (place == 4))).astype(BF)
                    last = last + dot(block[:, :128], sel, (1, 0))
                    sel = (p1 == 127) & (place == 0)
                else:
                    sel = ((p1 == 127) & (place == 1)) | ((p1 >= 126) & (place == 2))
                last = last + dot(block[:, 128:], sel.astype(BF), (1, 0))
        g_even = g_even + dot(jnp.concatenate(evens, axis=1), tr_ref[q], (1, 0))
        g_odd = g_odd + dot(jnp.concatenate(odds, axis=1), tr_ref[q, :, :768], (1, 0))
    last = last.astype(BF)
    side = [dot(last, trx_ref[:, k * 384 : (k + 1) * 384], (1, 0)) for k in range(KERNEL)]
    pad = jnp.zeros((ROWS - 360, LANES), F32)
    taps = (g_even[:, :384], g_odd[:, :384], g_even[:, 384:768], g_odd[:, 384:], g_even[:, 768:])
    taps = [tap + term for tap, term in zip(taps, side)]
    stores = []
    for s in range(16):
        blocks = []
        for l in range(3):
            for tap in taps:
                blocks.append(tap[s * 24 : (s + 1) * 24, l * LANES : (l + 1) * LANES])
        out_ref[s] = jnp.concatenate(blocks + [pad], axis=0).astype(BF)
        if s % 4 == 3:
            part = pl.ds(s - 3, 4)
            stores.append(pltpu.make_async_copy(out_ref.at[part], out_hbm.at[part], out_sems.at[s // 4]))
            stores[-1].start()
    for store in stores:
        store.wait()
    keep.wait()


def weight_grad(ids, pieces, tr, trx):
    return pl.pallas_call(
        weight_kernel,
        out_shape=(jax.ShapeDtypeStruct((16, ROWS, LANES), BF),
                   jax.ShapeDtypeStruct((KEPT, HALF, 512), BF)),
        in_specs=[SM] + [ANY] * 8 + [VM] * 2,
        out_specs=(HBM, HBM),
        scratch_shapes=[pltpu.VMEM((PAIR, HALF, 512), BF), pltpu.VMEM((16, ROWS, LANES), BF),
                        pltpu.SemaphoreType.DMA((PAIR, CHAN)), pltpu.SemaphoreType.DMA,
                        pltpu.SemaphoreType.DMA((4,))],
        compiler_params=params(40 * MIB),
        cost_estimate=pl.CostEstimate(flops=4 * 10**9, bytes_accessed=10 * 2**20, transcendentals=0),
        name="weight_grad",
    )(ids, *pieces, tr, trx)


def trunk_kernel(ids_ref, *refs):
    mine, other = refs[0], refs[1:5]
    conv_hbm, out_ref, skip_ref, full, sums, rims, conv_ref, sems, mine_sems, other_sems, skip_sem, conv_sem = refs[5:]
    me = ids_ref[0]
    half = ids_ref[2]
    skip = pltpu.make_async_copy(full.at[:, me // 2, me % 2], skip_ref, skip_sem)
    copies = []
    for b in range(BATCH):
        for g in range(2):
            rows = pl.ds((b * 2 + g) * 192, 192)
            copies.append(pltpu.make_async_copy(mine.at[0, rows, :], full.at[b, g, half], mine_sems.at[b, g]))
            for r in range(CHAN):
                lanes = pl.ds(pl.multiple_of((me ^ r) * LANES, LANES), LANES)
                copies.append(
                    pltpu.make_async_copy(
                        other[r].at[rows, :], full.at[b, g, 1 - half, :, lanes], other_sems.at[r, b, g]
                    )
                )
    for r in range(CHAN):
        copies.append(pltpu.make_async_copy(other[r].at[pl.ds(HALF, 96), :], rims.at[r], sems.at[r]))
    load = pltpu.make_async_copy(conv_hbm, conv_ref, conv_sem)
    for copy in copies + [load]:
        copy.start()
    row = lax.broadcasted_iota(jnp.int32, (2 * EXT, 512), 0)
    p = lax.broadcasted_iota(jnp.int32, (2 * EXT, 512), 1)
    lo = jnp.where(row < EXT, 2 * (row - 8), 2 * (row - EXT - 8) - 1)
    pick = ((p == lo) | (p == lo + 1)).astype(BF)
    col = lax.broadcasted_iota(jnp.int32, (2 * EXT, 32), 1)
    lo = lo[:, :32]
    for copy in copies:
        copy.wait()
    skip.start()
    rim = jnp.concatenate(
        [jnp.concatenate([rims[x, l * 16 : (l + 1) * 16, :] for l in range(6)], axis=1) for x in (me, me ^ 3)],
        axis=0,
    )
    for b in range(BATCH):
        offset = col % 16 - 2 * b
        rim_ok = (offset >= 0) & (offset < 2)
        rim_pos = jnp.where(col < 16, offset - 2, 512 + offset)
        pick_r = (rim_ok & ((rim_pos == lo) | (rim_pos == lo + 1))).astype(BF)
        e = (dot(pick, full[b].reshape(C_OUT, 512), (1, 1)) + dot(pick_r, rim, (1, 0))).astype(BF)
        sums[pl.ds(b * EXT, EXT), :C_OUT] = e[:EXT]
        sums[pl.ds(b * EXT, EXT), C_OUT:] = e[EXT:]
    load.wait()
    even, odd = sums[:, :C_OUT], sums[:, C_OUT:]
    up = dot(even, conv_ref[0], (1, 1)) + dot(odd, conv_ref[1], (1, 1))
    here = dot(even, conv_ref[2], (1, 1)) + dot(odd, conv_ref[3], (1, 1))
    down = dot(even, conv_ref[4], (1, 1))
    for b in range(BATCH):
        o = b * EXT + 8
        total = up[o + 1 : o + 257] + here[o : o + 256] + down[o - 1 : o + 255]
        out_ref[b] = total.astype(BF)
    skip.wait()


EXT = 272


def trunk_grad(ids, mine, other, conv_w):
    return pl.pallas_call(
        trunk_kernel,
        out_shape=(jax.ShapeDtypeStruct((BATCH, 256, 384), BF), jax.ShapeDtypeStruct((BATCH, 192, 512), BF)),
        in_specs=[SM] + [HBM] * 6,
        out_specs=(VM, HBM),
        scratch_shapes=[pltpu.VMEM((BATCH, 2, 2, 192, 512), BF), pltpu.VMEM((BATCH * EXT, 2 * C_OUT), BF),
                        pltpu.VMEM((CHAN, 96, LANES), BF), pltpu.VMEM((KERNEL, 384, C_OUT), BF),
                        pltpu.SemaphoreType.DMA((CHAN,)), pltpu.SemaphoreType.DMA((BATCH, 2)),
                        pltpu.SemaphoreType.DMA((CHAN, BATCH, 2)), pltpu.SemaphoreType.DMA,
                        pltpu.SemaphoreType.DMA],
        compiler_params=params(),
        cost_estimate=pl.CostEstimate(flops=8 * 10**9, bytes_accessed=16 * 2**20, transcendentals=0),
        name="trunk_grad",
    )(ids, mine, *other, conv_w)


def sum_kernel(scale, in_ref, out_ref):
    total = in_ref[0].astype(F32)
    for s in range(1, in_ref.shape[0]):
        total = total + in_ref[s].astype(F32)
    total = total * scale
    for l in range(3):
        for k in range(KERNEL):
            start = l * 120 + k * 24
            out_ref[k, :, l * LANES : (l + 1) * LANES] = total[start : start + 24]


def sum_weights(terms, scale):
    return pl.pallas_call(
        functools.partial(sum_kernel, scale),
        out_shape=jax.ShapeDtypeStruct((KERNEL, 24, 384), F32),
        in_specs=[VM],
        out_specs=VM,
        compiler_params=params(30 * MIB),
        name="sum_weights",
    )(terms)


def flip(x, r):
    return lax.ppermute(x, "chan", [(i, i ^ r) for i in range(CHAN)])


def partner(x):
    return lax.ppermute(x, "seq", [(i, i ^ 8) for i in range(SEQ)])


def partner_far(x):
    pairs = [(s * CHAN + c, (s ^ 8) * CHAN + (c ^ 2)) for s in range(SEQ) for c in range(CHAN)]
    return lax.ppermute(x, ("seq", "chan"), pairs)


def rim(x):
    up = [(s * CHAN + 3, (s + 1) * CHAN) for s in range(SEQ - 1)]
    down = [(s * CHAN, (s - 1) * CHAN + 3) for s in range(1, SEQ)]
    return lax.ppermute(x, ("seq", "chan"), up + down)


def across(x):
    pairs = [(s * CHAN + c, (s ^ 16) * CHAN + (c ^ 2)) for s in range(SEQ) for c in range(CHAN)]
    return lax.ppermute(x, ("seq", "chan"), pairs)


def local(
    trunk, merged, conv_w, norm_gain, head_w, head_bias, head_scale, head_of_track, valid_len, cot
):
    me = lax.axis_index("chan").astype(jnp.int32)
    place = lax.axis_index("seq").astype(jnp.int32)
    half = (place // 8) % 2
    ids = jnp.stack([me, place * 512 + me * LANES, half, place])
    trunk_far = partner(trunk)
    p0, p1, p2, p3 = cut_pieces(ids, merged, norm_gain[None])
    p1, p2, p3, cot = lax.optimization_barrier((p1, p2, p3, cot))
    send = cut_cot(ids, cot, trunk)
    p1, p2, p3 = flip(p1, 1), flip(p2, 2), flip(p3, 3)
    send, trunk, head_w = lax.optimization_barrier((send, trunk, head_w))
    far_head = across(head_w)
    near_head = flip(head_w, 1)
    send, p1, p2 = lax.optimization_barrier((send, p1, p2))
    p3, trunk_far, far_head = lax.optimization_barrier((p3, trunk_far, far_head))
    got = lax.all_to_all(send, "seq", 0, 0, tiled=True).reshape(SEQ, COT_ROWS, LANES)
    pieces = (p0, p1, p2, p3)
    heads = (head_w, near_head, far_head, flip(far_head, 1))

    scored = scores(pieces, heads, head_bias[None], head_of_track[None], head_scale)
    mine, other, edge = head(ids, valid_len, scored, got)
    trunk, _ = lax.optimization_barrier((trunk, mine))
    tr, trx = trunk_rows(ids, trunk, trunk_far, got)

    mine_far, other_x, other_far_x = flip(mine, 2), partner(other), partner_far(other)
    other = jnp.concatenate([other, rim(edge)])
    mine_far, other_x, other_far_x, other, tr, trx = lax.optimization_barrier(
        (mine_far, other_x, other_far_x, other, tr, trx)
    )
    mine_all = (mine, flip(mine, 1), mine_far, flip(mine_far, 1))
    blocks = mine_all + (other_x, flip(other_x, 1), other_far_x, flip(other_far_x, 1))
    terms, mine_rows = weight_grad(ids, blocks, tr, trx)
    other_late, _ = lax.optimization_barrier((other, mine_far))
    other_far = flip(other_late, 2)
    other_all = (other, flip(other, 1), other_far, flip(other_far, 1))
    groups = [[s for s in range(SEQ) if (s // 8) % 2 == u] for u in range(2)]
    summed = lax.all_to_all(terms, "seq", 0, 0, tiled=True, axis_index_groups=groups)
    d_trunk, d_skip = trunk_grad(ids, mine_rows, other_all, conv_w)
    grad_scale = 1.0 / math.sqrt(BATCH * 512 * SEQ)
    d_conv_w = sum_weights(summed, grad_scale)
    return (d_trunk, d_skip, d_conv_w)


def solution(mesh):
    placed = (
        P(None, "seq", "chan"),
        P(None, "chan", "seq"),
        P(None, "chan", None),
        P("chan"),
        P("chan", None),
        P(),
        P(),
        P(),
        P(),
        P(None, "seq", None),
    )
    return jax.shard_map(
        local,
        mesh=mesh,
        in_specs=placed,
        out_specs=(P(None, "seq", "chan"), P(None, "chan", "seq"), P(None, "seq", "chan")),
        check_vma=False,
    )
```

```python
import functools
import math

import jax
import jax.numpy as jnp
from jax import lax
from jax.experimental import pallas as pl
from jax.experimental.pallas import tpu as pltpu
from jax.sharding import PartitionSpec as P

BATCH = 4
C_OUT = 768
TRACKS = 1024
KERNEL = 5
SEQ = 32
CHAN = 4
LANES = 128
epsilon = 1e-06

BF = jnp.bfloat16
F32 = jnp.float32
MIB = 1024 * 1024


def params(limit=62 * MIB):
    return pltpu.CompilerParams(vmem_limit_bytes=limit)


def dot(a, b, contract):
    return lax.dot_general(a, b, ((contract[:1], contract[1:]), ((), ())), preferred_element_type=F32)


ANY = pl.BlockSpec(memory_space=pl.ANY)
VM = pl.BlockSpec(memory_space=pltpu.VMEM)
HBM = pl.BlockSpec(memory_space=pltpu.HBM)
SM = pl.BlockSpec(memory_space=pltpu.SMEM)


PIECE = BATCH * 192 + 16


def pieces_kernel(ids_ref, merged_ref, gain_ref, p0, p1, p2, p3, line, sems, line_sem):
    me = ids_ref[0]
    load = pltpu.make_async_copy(gain_ref, line, line_sem)
    load.start()
    copies = []
    for r, piece in enumerate((p0, p1, p2, p3)):
        lanes = pl.ds(pl.multiple_of((me ^ r) * LANES, LANES), LANES)
        for b in range(BATCH):
            rows = pl.ds(b * 192, 192)
            copies.append(pltpu.make_async_copy(merged_ref.at[b, :, lanes], piece.at[rows, :], sems.at[r, b]))
    for copy in copies:
        copy.start()
    load.wait()
    tail = jnp.concatenate([line[:, LANES:], jnp.zeros((1, 2 * LANES - 192), F32)], axis=1)
    rest = jnp.concatenate([line[:, :LANES], tail], axis=0)
    rows = []
    for _ in range(3):
        part = rest.astype(BF).astype(F32)
        rows.append(part)
        rest = rest - part
    gains = jnp.concatenate(rows + [jnp.zeros((10, LANES), F32)], axis=0).astype(BF)
    for piece in (p0, p1, p2, p3):
        piece[BATCH * 192 :, :] = gains
    for copy in copies:
        copy.wait()


def cut_pieces(ids, merged, gain):
    return pl.pallas_call(
        pieces_kernel,
        out_shape=(jax.ShapeDtypeStruct((PIECE, LANES), BF),) * CHAN,
        in_specs=[SM, HBM, HBM],
        out_specs=(VM,) * CHAN,
        scratch_shapes=[pltpu.VMEM((1, 192), F32), pltpu.SemaphoreType.DMA((CHAN, BATCH)), pltpu.SemaphoreType.DMA],
        compiler_params=params(),
        name="cut_pieces",
    )(ids, merged, gain)


COT_ROWS = 9 * 16


def cot_kernel(ids_ref, cot_ref, trunk_ref, send_ref, edges, sems, edge_sems):
    me, place = ids_ref[0], ids_ref[3]
    copies = []
    for d in range(SEQ):
        start = pl.multiple_of(d * CHAN * LANES + me * LANES, LANES)
        copies.append(
            pltpu.make_async_copy(cot_ref.at[:, :, pl.ds(start, LANES)], send_ref.at[d, pl.ds(0, 8)], sems.at[d])
        )
    loads = [
        pltpu.make_async_copy(trunk_ref.at[:, pl.ds(row, 16), :], edges.at[i], edge_sems.at[i])
        for i, row in enumerate((0, 240))
    ]
    for copy in loads + copies:
        copy.start()
    for load in loads:
        load.wait()
    rows = []
    for i, row in enumerate((0, 15)):
        parts = []
        for b in range(BATCH):
            line = edges[i, b].astype(F32)[row : row + 1]
            parts += [line[:, l * LANES : (l + 1) * LANES] for l in range(3)]
        rows.append(jnp.concatenate(parts + [jnp.zeros((4, LANES), F32)], axis=0))
    for d in range(SEQ):
        up = ((place + 1 == d) | (place + 1 == (d ^ 8))).astype(F32)
        down = ((place - 1 == d) | (place - 1 == (d ^ 8))).astype(F32)
        send_ref[d, 8] = (rows[1] * up + rows[0] * down).astype(BF)
    for copy in copies:
        copy.wait()


def cut_cot(ids, cot, trunk):
    return pl.pallas_call(
        cot_kernel,
        out_shape=jax.ShapeDtypeStruct((SEQ, 9, 16, LANES), BF),
        in_specs=[SM, HBM, HBM],
        out_specs=VM,
        scratch_shapes=[pltpu.VMEM((2, BATCH, 16, 384), BF), pltpu.SemaphoreType.DMA((SEQ,)),
                        pltpu.SemaphoreType.DMA((2,))],
        compiler_params=params(),
        cost_estimate=pl.CostEstimate(flops=0, bytes_accessed=5 * 2**20, transcendentals=0),
        name="cut_cot",
    )(ids, cot.reshape(BATCH * 2, 16, -1), trunk)


WIDE, NARROW = 9, 12


def score_kernel(*refs):
    pieces, heads, (bias_ref, of_track_ref, scale_ref) = refs[:4], refs[4:8], refs[8:11]
    wide_hbm, narrow_hbm, raw_ref, cols_ref, inv_ref, gain_ref, weights_ref, merged_ref = refs[11:19]
    parts, sems, head_sems, part_sems, out_sems = refs[19:]
    copies = []
    for r in range(CHAN):
        rows = pl.ds(r * 192, 192)
        for b in range(BATCH):
            copies.append(
                pltpu.make_async_copy(
                    pieces[r].at[pl.ds(b * 192, 192), :],
                    merged_ref.at[rows, pl.ds(b * LANES, LANES)],
                    sems.at[r, b],
                )
            )
        copies.append(
            pltpu.make_async_copy(pieces[r].at[pl.ds(BATCH * 192, 16), :], parts.at[r], part_sems.at[r])
        )
    loads = [
        pltpu.make_async_copy(heads[r], weights_ref.at[pl.ds(r * 192, 192), :], head_sems.at[r])
        for r in range(CHAN)
    ]
    for copy in copies + loads:
        copy.start()
    track_scale = jnp.zeros((1, TRACKS), F32)
    for h in range(scale_ref.shape[0]):
        track_scale = jnp.where(of_track_ref[...] == h, scale_ref[h], track_scale)
    lines = []
    for rest in (bias_ref[...], track_scale):
        for _ in range(3):
            part = rest.astype(BF).astype(F32)
            lines.append(part)
            rest = rest - part
    lines = jnp.concatenate(lines + [jnp.zeros((10, TRACKS), F32)], axis=0).astype(BF)
    row = lax.broadcasted_iota(jnp.int32, (16, LANES), 0)
    lane = lax.broadcasted_iota(jnp.int32, (16, LANES), 1)
    cols_ref[...] = dot(lines, ((row < 6) & (row // 3 == lane)).astype(BF), (0, 0))
    for copy in copies:
        copy.wait()
    for r in range(CHAN):
        for side in range(2):
            pick = ((row < 6) & (row % 2 == side)).astype(BF)
            size = LANES - side * 64
            start = r * 192 + side * LANES
            gain_ref[start : start + size, :] = dot(parts[r], pick, (0, 0))[:size]
    m32 = merged_ref[...].astype(F32)
    total = jnp.sum(m32 * m32, axis=0, keepdims=True)
    inv = lax.rsqrt(total / C_OUT + epsilon)
    for b in range(BATCH):
        inv_ref[8 * b : 8 * b + 8, :] = jnp.broadcast_to(inv[:, b * LANES : (b + 1) * LANES], (8, LANES))
    lane = lax.broadcasted_iota(jnp.int32, (C_OUT, LANES), 1)
    cols_ref[0:C_OUT, :] = jnp.where(lane == 2, gain_ref[...], cols_ref[0:C_OUT, :])
    normed = (m32 * gain_ref[:, 0:1]).astype(BF)
    for load in loads:
        load.wait()
    stores = [
        pltpu.make_async_copy(cols_ref, wide_hbm.at[1, :, pl.ds(0, LANES)], out_sems.at[0]),
        pltpu.make_async_copy(inv_ref, wide_hbm.at[1, pl.ds(0, 32), pl.ds(LANES, LANES)], out_sems.at[4]),
        pltpu.make_async_copy(weights_ref, narrow_hbm.at[0], out_sems.at[1]),
        pltpu.make_async_copy(merged_ref, narrow_hbm.at[1, :, pl.ds(0, BATCH * LANES)], out_sems.at[2]),
    ]
    for store in stores:
        store.start()
    raw_ref[...] = dot(weights_ref[...], normed, (0, 0))
    stores.append(pltpu.make_async_copy(raw_ref, wide_hbm.at[0], out_sems.at[3]))
    stores[-1].start()
    for store in stores:
        store.wait()


def scores(pieces, heads, bias, of_track, scale):
    return pl.pallas_call(
        score_kernel,
        out_shape=(jax.ShapeDtypeStruct((WIDE, TRACKS, BATCH * LANES), F32),
                   jax.ShapeDtypeStruct((NARROW, C_OUT, TRACKS), BF)),
        in_specs=[HBM] * 8 + [VM, VM, SM],
        out_specs=(HBM, HBM),
        scratch_shapes=[
            pltpu.VMEM((TRACKS, BATCH * LANES), F32),
            pltpu.VMEM((TRACKS, LANES), F32),
            pltpu.VMEM((32, LANES), F32),
            pltpu.VMEM((C_OUT, LANES), F32),
            pltpu.VMEM((C_OUT, TRACKS), BF),
            pltpu.VMEM((C_OUT, BATCH * LANES), BF),
            pltpu.VMEM((CHAN, 16, LANES), BF),
            pltpu.SemaphoreType.DMA((CHAN, BATCH)),
            pltpu.SemaphoreType.DMA((CHAN,)),
            pltpu.SemaphoreType.DMA((CHAN,)),
            pltpu.SemaphoreType.DMA((5,)),
        ],
        compiler_params=params(),
        cost_estimate=pl.CostEstimate(flops=6500000000, bytes_accessed=8 * 2**20, transcendentals=0),
        name="scores",
    )(*pieces, *heads, bias, of_track, scale)


HALF = BATCH * 384


def head_kernel(
    ids_ref, valid_ref, wide_hbm, narrow_hbm, cot_ref,
    mine_ref, other_ref, edge_ref, full, raw_ref, cols_ref, inv_ref, weights_ref, merged_ref, sems
):
    load_cols = pltpu.make_async_copy(wide_hbm.at[1, :, pl.ds(0, LANES)], cols_ref, sems.at[1, 2])
    load_inv = pltpu.make_async_copy(wide_hbm.at[1, pl.ds(0, 32), pl.ds(LANES, LANES)], inv_ref, sems.at[1, 3])
    load_cols.start()
    load_inv.start()
    loads = []
    for b in range(BATCH):
        loads.append(
            pltpu.make_async_copy(wide_hbm.at[0, :, pl.ds(b * LANES, LANES)], raw_ref.at[b], sems.at[0, b])
        )
    load_weights = pltpu.make_async_copy(narrow_hbm.at[0], weights_ref, sems.at[1, 0])
    load_merged = pltpu.make_async_copy(narrow_hbm.at[1, :, pl.ds(0, BATCH * LANES)], merged_ref, sems.at[1, 1])
    for copy in loads:
        copy.start()
    load_weights.start()
    load_merged.start()
    load_cols.wait()
    load_inv.wait()
    me = ids_ref[0]
    first = ids_ref[1]
    half = ids_ref[2]
    scale = cols_ref[:, 1:2]
    bias = cols_ref[:, 0:1]
    lane = lax.broadcasted_iota(jnp.int32, (1, LANES), 1)
    scaled, coefs = [], []
    for b in range(BATCH):
        cols = slice(b * LANES, (b + 1) * LANES)
        loads[b].wait()
        raw = raw_ref[b]
        inv = inv_ref[8 * b : 8 * b + 1, :]
        live = (first + lane < valid_ref[b]).astype(F32)
        gate = 0.5 * jnp.tanh(0.5 * (inv * raw + bias)) + 0.5
        cot = cot_ref[:, b * 32 : (b + 1) * 32, :].reshape(TRACKS, LANES).astype(F32)
        d_logits = (cot * scale) * gate
        d_rms = live * jnp.sum(d_logits * raw, axis=0, keepdims=True)
        scaled.append(((inv * live) * d_logits).astype(BF))
        coefs.append(inv * inv * inv * d_rms * (1.0 / C_OUT))
    load_weights.wait()
    load_merged.wait()
    d = dot(weights_ref[...], jnp.concatenate(scaled, axis=1), (1, 0)) * cols_ref[0:C_OUT, 2:3]
    for r in range(CHAN):
        rows = slice(r * 192, (r + 1) * 192)
        for b in range(BATCH):
            cols = slice(b * LANES, (b + 1) * LANES)
            full[b, me ^ r] = d[rows, cols] - coefs[b] * merged_ref[rows, cols].astype(F32)
    for b in range(BATCH):
        for g in range(2):
            rows = slice((b * 2 + g) * 192, (b * 2 + g + 1) * 192)
            mine_ref[rows, :] = full[b, 2 * g + half].astype(BF)
            other_ref[rows, :] = full[b, 2 * g + 1 - half].astype(BF)
    start = jnp.where(me == CHAN - 1, LANES - 2, 0)
    row = lax.broadcasted_iota(jnp.int32, (16, LANES), 0)
    col = lax.broadcasted_iota(jnp.int32, (16, LANES), 1) - start
    edge = jnp.zeros((16, C_OUT), F32)
    for b in range(BATCH):
        sel = ((col >= 0) & (col < 2) & (row == b * 2 + col)).astype(BF)
        edge = edge + dot(sel, full[b].reshape(C_OUT, LANES).astype(BF), (1, 1))
    for l in range(6):
        edge_ref[l * 16 : (l + 1) * 16, :] = edge[:, l * LANES : (l + 1) * LANES].astype(BF)


def head(ids, valid, scored, cot):
    return pl.pallas_call(
        head_kernel,
        out_shape=(jax.ShapeDtypeStruct((HALF, LANES), BF),) * 2 + (jax.ShapeDtypeStruct((96, LANES), BF),),
        in_specs=[SM, SM, HBM, HBM, VM],
        out_specs=(VM,) * 3,
        scratch_shapes=[
            pltpu.VMEM((BATCH, CHAN, 192, LANES), F32),
            pltpu.VMEM((BATCH, TRACKS, LANES), F32),
            pltpu.VMEM((TRACKS, LANES), F32),
            pltpu.VMEM((32, LANES), F32),
            pltpu.VMEM((C_OUT, TRACKS), BF),
            pltpu.VMEM((C_OUT, BATCH * LANES), BF),
            pltpu.SemaphoreType.DMA((2, BATCH)),
        ],
        compiler_params=params(48 * MIB),
        name="head",
    )(ids, valid, *scored, cot)


PAIR = 2


def rows_kernel(ids_ref, own_ref, far_ref, got_ref, tr_ref, trx_ref, edges, trunks, sems, trunk_sems):
    place = ids_ref[3]
    copies = [
        pltpu.make_async_copy(ref, trunks.at[q], trunk_sems.at[q]) for q, ref in enumerate((own_ref, far_ref))
    ]
    for q in range(PAIR):
        for i, step in enumerate((-1, 1)):
            source = jnp.clip((place ^ (8 * q)) + step, 0, SEQ - 1)
            copies.append(
                pltpu.make_async_copy(got_ref.at[source, pl.ds(128, 16)], edges.at[q, i], sems.at[q, i])
            )
    for copy in copies:
        copy.start()
    for copy in copies:
        copy.wait()
    row = lax.broadcasted_iota(jnp.int32, (256, 384), 0)
    ends = [jnp.zeros((LANES, 384), F32) for _ in range(KERNEL)]
    at = lax.broadcasted_iota(jnp.int32, (LANES, 384), 0)
    for q in range(PAIR):
        before = edges[q, 0].astype(F32) * ((place ^ (8 * q)) > 0).astype(F32)
        after = edges[q, 1].astype(F32) * ((place ^ (8 * q)) < SEQ - 1).astype(F32)
        for b in range(BATCH):
            t = trunks[q, b].astype(F32)
            rows = slice(b * 256, (b + 1) * 256)
            tr_ref[q, rows, 0:384] = jnp.where(row == 0, 0.0, pltpu.roll(t, 1, 0)).astype(BF)
            tr_ref[q, rows, 384:768] = trunks[q, b]
            tr_ref[q, rows, 768:1152] = jnp.where(row == 255, 0.0, pltpu.roll(t, 255, 0)).astype(BF)
            base = (q * BATCH + b) * 5
            first, last = (
                jnp.concatenate([x[b * 3 + l : b * 3 + l + 1] for l in range(3)], axis=1)
                for x in (before, after)
            )
            for column, tap, x in (
                (0, 1, t[127:128]), (0, 3, t[128:129]), (1, 1, t[255:256]), (1, 3, last),
                (2, 4, last), (3, 0, first), (4, 1, first),
            ):
                ends[tap] = jnp.where(at == base + column, x, ends[tap])
    for k in range(KERNEL):
        trx_ref[:, k * 384 : (k + 1) * 384] = ends[k].astype(BF)


def trunk_rows(ids, own, far, got):
    return pl.pallas_call(
        rows_kernel,
        out_shape=(jax.ShapeDtypeStruct((PAIR, 1024, 1152), BF),
                   jax.ShapeDtypeStruct((LANES, KERNEL * 384), BF)),
        in_specs=[SM, HBM, HBM, ANY],
        out_specs=(VM, VM),
        scratch_shapes=[pltpu.VMEM((PAIR, 2, 16, LANES), BF), pltpu.VMEM((PAIR, BATCH, 256, 384), BF),
                        pltpu.SemaphoreType.DMA((PAIR, 2)), pltpu.SemaphoreType.DMA((PAIR,))],
        compiler_params=params(30 * MIB),
        cost_estimate=pl.CostEstimate(flops=10**7, bytes_accessed=8 * 2**20, transcendentals=0),
        name="trunk_rows",
    )(ids, own, far, got)


ROWS = 368
KEPT = 18


def weight_kernel(ids_ref, *refs):
    pieces, (tr_ref, trx_ref, out_hbm, own_ref, full, out_ref, sems, own_sem, out_sems) = refs[:8], refs[8:]
    me = ids_ref[0]
    copies = []
    for q in range(PAIR):
        for r in range(CHAN):
            lanes = pl.ds(pl.multiple_of((me ^ r) * LANES, LANES), LANES)
            copies.append(pltpu.make_async_copy(pieces[q * CHAN + r], full.at[q, :, lanes], sems.at[q, r]))
    for copy in copies:
        copy.start()
    keep = pltpu.make_async_copy(full.at[0], own_ref.at[0], own_sem)
    p = lax.broadcasted_iota(jnp.int32, (256, 256), 0)
    q_ = lax.broadcasted_iota(jnp.int32, (256, 256), 1)
    even = (q_ < 128) & (p // 2 == q_)
    odd = (q_ >= 128) & ((p + 1) // 2 == q_ - 128)
    pick = (even | odd).astype(BF)
    last = jnp.zeros((384, LANES), F32)
    p1 = lax.broadcasted_iota(jnp.int32, (256, LANES), 0)
    q1 = lax.broadcasted_iota(jnp.int32, (256, LANES), 1)
    g_even = jnp.zeros((384, 1152), F32)
    g_odd = jnp.zeros((384, 768), F32)
    for q in range(PAIR):
        for copy in copies[q * CHAN : (q + 1) * CHAN]:
            copy.wait()
        if q == 0:
            keep.start()
        evens, odds = [], []
        for b in range(BATCH):
            for h in range(2):
                block = full[q, b * 384 : (b + 1) * 384, h * 256 : (h + 1) * 256]
                place = q1 - (q * BATCH + b) * 5
                if h == 0:
                    sel = ((p1 == 255) & (place == 0)) | ((p1 < 2) & (place == 3)) | ((p1 == 0) & (place == 4))
                else:
                    sel = ((p1 == 255) & (place == 1)) | ((p1 >= 254) & (place == 2))
                e = dot(block, jnp.concatenate([pick, sel.astype(BF)], axis=1), (1, 0))
                evens.append(e[:, :128].astype(BF))
                odds.append(e[:, 128:256].astype(BF))
                last = last + e[:, 256:]
        g_even = g_even + dot(jnp.concatenate(evens, axis=1), tr_ref[q], (1, 0))
        g_odd = g_odd + dot(jnp.concatenate(odds, axis=1), tr_ref[q, :, :768], (1, 0))
    last = last.astype(BF)
    side = [dot(last, trx_ref[:, k * 384 : (k + 1) * 384], (1, 0)) for k in range(KERNEL)]
    pad = jnp.zeros((ROWS - 360, LANES), F32)
    taps = (g_even[:, :384], g_odd[:, :384], g_even[:, 384:768], g_odd[:, 384:], g_even[:, 768:])
    taps = [tap + term for tap, term in zip(taps, side)]
    stores = []
    for s in range(16):
        blocks = []
        for l in range(3):
            for tap in taps:
                blocks.append(tap[s * 24 : (s + 1) * 24, l * LANES : (l + 1) * LANES])
        out_ref[s] = jnp.concatenate(blocks + [pad], axis=0).astype(BF)
        if s % 4 == 3:
            part = pl.ds(s - 3, 4)
            stores.append(pltpu.make_async_copy(out_ref.at[part], out_hbm.at[part], out_sems.at[s // 4]))
            stores[-1].start()
    for store in stores:
        store.wait()
    keep.wait()


def weight_grad(ids, pieces, tr, trx):
    return pl.pallas_call(
        weight_kernel,
        out_shape=(jax.ShapeDtypeStruct((16, ROWS, LANES), BF),
                   jax.ShapeDtypeStruct((KEPT, HALF, 512), BF)),
        in_specs=[SM] + [ANY] * 8 + [VM] * 2,
        out_specs=(HBM, HBM),
        scratch_shapes=[pltpu.VMEM((PAIR, HALF, 512), BF), pltpu.VMEM((16, ROWS, LANES), BF),
                        pltpu.SemaphoreType.DMA((PAIR, CHAN)), pltpu.SemaphoreType.DMA,
                        pltpu.SemaphoreType.DMA((4,))],
        compiler_params=params(40 * MIB),
        cost_estimate=pl.CostEstimate(flops=4 * 10**9, bytes_accessed=10 * 2**20, transcendentals=0),
        name="weight_grad",
    )(ids, *pieces, tr, trx)


def trunk_kernel(ids_ref, *refs):
    mine, other = refs[0], refs[1:5]
    conv_hbm, out_ref, skip_ref, full, sums, rims, conv_ref, sems, mine_sems, other_sems, skip_sem, conv_sem = refs[5:]
    me = ids_ref[0]
    half = ids_ref[2]
    skip = pltpu.make_async_copy(full.at[:, me // 2, me % 2], skip_ref, skip_sem)
    copies = []
    for b in range(BATCH):
        for g in range(2):
            rows = pl.ds((b * 2 + g) * 192, 192)
            copies.append(pltpu.make_async_copy(mine.at[0, rows, :], full.at[b, g, half], mine_sems.at[b, g]))
            for r in range(CHAN):
                lanes = pl.ds(pl.multiple_of((me ^ r) * LANES, LANES), LANES)
                copies.append(
                    pltpu.make_async_copy(
                        other[r].at[rows, :], full.at[b, g, 1 - half, :, lanes], other_sems.at[r, b, g]
                    )
                )
    for r in range(CHAN):
        copies.append(pltpu.make_async_copy(other[r].at[pl.ds(HALF, 96), :], rims.at[r], sems.at[r]))
    load = pltpu.make_async_copy(conv_hbm, conv_ref, conv_sem)
    for copy in copies + [load]:
        copy.start()
    row = lax.broadcasted_iota(jnp.int32, (2 * EXT, 512), 0)
    p = lax.broadcasted_iota(jnp.int32, (2 * EXT, 512), 1)
    lo = jnp.where(row < EXT, 2 * (row - 8), 2 * (row - EXT - 8) - 1)
    pick = ((p == lo) | (p == lo + 1)).astype(BF)
    col = lax.broadcasted_iota(jnp.int32, (2 * EXT, 32), 1)
    lo = lo[:, :32]
    for copy in copies:
        copy.wait()
    skip.start()
    rim = jnp.concatenate(
        [jnp.concatenate([rims[x, l * 16 : (l + 1) * 16, :] for l in range(6)], axis=1) for x in (me, me ^ 3)],
        axis=0,
    )
    for b in range(BATCH):
        offset = col % 16 - 2 * b
        rim_ok = (offset >= 0) & (offset < 2)
        rim_pos = jnp.where(col < 16, offset - 2, 512 + offset)
        pick_r = (rim_ok & ((rim_pos == lo) | (rim_pos == lo + 1))).astype(BF)
        e = (dot(pick, full[b].reshape(C_OUT, 512), (1, 1)) + dot(pick_r, rim, (1, 0))).astype(BF)
        sums[pl.ds(b * EXT, EXT), :C_OUT] = e[:EXT]
        sums[pl.ds(b * EXT, EXT), C_OUT:] = e[EXT:]
    load.wait()
    even, odd = sums[:, :C_OUT], sums[:, C_OUT:]
    up = dot(even, conv_ref[0], (1, 1)) + dot(odd, conv_ref[1], (1, 1))
    here = dot(even, conv_ref[2], (1, 1)) + dot(odd, conv_ref[3], (1, 1))
    down = dot(even, conv_ref[4], (1, 1))
    for b in range(BATCH):
        o = b * EXT + 8
        total = up[o + 1 : o + 257] + here[o : o + 256] + down[o - 1 : o + 255]
        out_ref[b] = total.astype(BF)
    skip.wait()


EXT = 272


def trunk_grad(ids, mine, other, conv_w):
    return pl.pallas_call(
        trunk_kernel,
        out_shape=(jax.ShapeDtypeStruct((BATCH, 256, 384), BF), jax.ShapeDtypeStruct((BATCH, 192, 512), BF)),
        in_specs=[SM] + [HBM] * 6,
        out_specs=(VM, HBM),
        scratch_shapes=[pltpu.VMEM((BATCH, 2, 2, 192, 512), BF), pltpu.VMEM((BATCH * EXT, 2 * C_OUT), BF),
                        pltpu.VMEM((CHAN, 96, LANES), BF), pltpu.VMEM((KERNEL, 384, C_OUT), BF),
                        pltpu.SemaphoreType.DMA((CHAN,)), pltpu.SemaphoreType.DMA((BATCH, 2)),
                        pltpu.SemaphoreType.DMA((CHAN, BATCH, 2)), pltpu.SemaphoreType.DMA,
                        pltpu.SemaphoreType.DMA],
        compiler_params=params(),
        cost_estimate=pl.CostEstimate(flops=8 * 10**9, bytes_accessed=16 * 2**20, transcendentals=0),
        name="trunk_grad",
    )(ids, mine, *other, conv_w)


def sum_kernel(scale, in_ref, out_ref):
    total = in_ref[0].astype(F32)
    for s in range(1, in_ref.shape[0]):
        total = total + in_ref[s].astype(F32)
    total = total * scale
    for l in range(3):
        for k in range(KERNEL):
            start = l * 120 + k * 24
            out_ref[k, :, l * LANES : (l + 1) * LANES] = total[start : start + 24]


def sum_weights(terms, scale):
    return pl.pallas_call(
        functools.partial(sum_kernel, scale),
        out_shape=jax.ShapeDtypeStruct((KERNEL, 24, 384), F32),
        in_specs=[VM],
        out_specs=VM,
        compiler_params=params(30 * MIB),
        name="sum_weights",
    )(terms)


def flip(x, r):
    return lax.ppermute(x, "chan", [(i, i ^ r) for i in range(CHAN)])


def partner(x):
    return lax.ppermute(x, "seq", [(i, i ^ 8) for i in range(SEQ)])


def partner_far(x):
    pairs = [(s * CHAN + c, (s ^ 8) * CHAN + (c ^ 2)) for s in range(SEQ) for c in range(CHAN)]
    return lax.ppermute(x, ("seq", "chan"), pairs)


def rim(x):
    up = [(s * CHAN + 3, (s + 1) * CHAN) for s in range(SEQ - 1)]
    down = [(s * CHAN, (s - 1) * CHAN + 3) for s in range(1, SEQ)]
    return lax.ppermute(x, ("seq", "chan"), up + down)


def across(x):
    pairs = [(s * CHAN + c, (s ^ 16) * CHAN + (c ^ 2)) for s in range(SEQ) for c in range(CHAN)]
    return lax.ppermute(x, ("seq", "chan"), pairs)


def local(
    trunk, merged, conv_w, norm_gain, head_w, head_bias, head_scale, head_of_track, valid_len, cot
):
    me = lax.axis_index("chan").astype(jnp.int32)
    place = lax.axis_index("seq").astype(jnp.int32)
    half = (place // 8) % 2
    ids = jnp.stack([me, place * 512 + me * LANES, half, place])
    trunk_far = partner(trunk)
    p0, p1, p2, p3 = cut_pieces(ids, merged, norm_gain[None])
    p1, p2, p3, cot = lax.optimization_barrier((p1, p2, p3, cot))
    send = cut_cot(ids, cot, trunk)
    p1, p2, p3 = flip(p1, 1), flip(p2, 2), flip(p3, 3)
    send, trunk, head_w = lax.optimization_barrier((send, trunk, head_w))
    far_head = across(head_w)
    near_head = flip(head_w, 1)
    send, p1, p2 = lax.optimization_barrier((send, p1, p2))
    p3, trunk_far, far_head = lax.optimization_barrier((p3, trunk_far, far_head))
    got = lax.all_to_all(send, "seq", 0, 0, tiled=True).reshape(SEQ, COT_ROWS, LANES)
    pieces = (p0, p1, p2, p3)
    heads = (head_w, near_head, far_head, flip(far_head, 1))

    scored = scores(pieces, heads, head_bias[None], head_of_track[None], head_scale)
    mine, other, edge = head(ids, valid_len, scored, got)
    trunk, _ = lax.optimization_barrier((trunk, mine))
    tr, trx = trunk_rows(ids, trunk, trunk_far, got)

    mine_far, other_x, other_far_x = flip(mine, 2), partner(other), partner_far(other)
    other = jnp.concatenate([other, rim(edge)])
    mine_far, other_x, other_far_x, other, tr, trx = lax.optimization_barrier(
        (mine_far, other_x, other_far_x, other, tr, trx)
    )
    mine_all = (mine, flip(mine, 1), mine_far, flip(mine_far, 1))
    blocks = mine_all + (other_x, flip(other_x, 1), other_far_x, flip(other_far_x, 1))
    terms, mine_rows = weight_grad(ids, blocks, tr, trx)
    other_late, _ = lax.optimization_barrier((other, mine_far))
    other_far = flip(other_late, 2)
    other_all = (other, flip(other, 1), other_far, flip(other_far, 1))
    groups = [[s for s in range(SEQ) if (s // 8) % 2 == u] for u in range(2)]
    summed = lax.all_to_all(terms, "seq", 0, 0, tiled=True, axis_index_groups=groups)
    d_trunk, d_skip = trunk_grad(ids, mine_rows, other_all, conv_w)
    grad_scale = 1.0 / math.sqrt(BATCH * 512 * SEQ)
    d_conv_w = sum_weights(summed, grad_scale)
    return (d_trunk, d_skip, d_conv_w)


def solution(mesh):
    placed = (
        P(None, "seq", "chan"),
        P(None, "chan", "seq"),
        P(None, "chan", None),
        P("chan"),
        P("chan", None),
        P(),
        P(),
        P(),
        P(),
        P(None, "seq", None),
    )
    return jax.shard_map(
        local,
        mesh=mesh,
        in_specs=placed,
        out_specs=(P(None, "seq", "chan"), P(None, "chan", "seq"), P(None, "seq", "chan")),
        check_vma=False,
    )
```
